256 devices in a mesh: lat: 8 (over x, y_lo), lon: 32 (over z, y_hi, core).
Axes of the slice: x: 4, y: 4 (y_hi: 2, y_lo: 2; y = y_hi * 2 + y_lo), z: 8, core: 2. Of those that a mesh axis runs over, the one named last changes fastest.
Arguments:
- inputs: bfloat16 [128, 4096, 64], P('lat', 'lon'), may hold values from -6 to 6
- pre_first: bfloat16 [128, 4096, 128], P('lat', 'lon'), may hold values from -6 to 6
- grad_out: bfloat16 [64, 2048, 128], P('lat', 'lon'), may hold values from -6 to 6
- w_first: bfloat16 [3, 3, 64, 128], replicated, may hold values from -0.25 to 0.25
- w_second: bfloat16 [3, 3, 128, 128], replicated, may hold values from -0.1875 to 0.1875
Outputs:
- grad_inputs: bfloat16 [128, 4096, 64], P('lat', 'lon')
- grad_w_first: float32 [3, 3, 64, 128], replicated
- grad_w_second: float32 [3, 3, 128, 128], replicated
The draws below stay inside these ranges and needn't reach their ends.
All inputs are finite; a program needn't handle non-finite values.
Results may differ from the reference program's by a relative error of at most 0.0049.
Values may be sent and summed in bfloat16 or wider, within the bound.
A program may use at most 64 MiB of HBM per device.

```python
import jax
import jax.numpy as jnp
from jax import lax

C0 = 64
C1 = 128
NLAT = 128
NLON = 4096


def levels(own_key, shape, shards, smallest, high):
    factor_of, own = 1.0, jax.random.fold_in(own_key, 6)
    for dim, shards_of in shards:
        steps = jnp.exp(jax.random.uniform(jax.random.fold_in(own, dim), (shards_of,), jnp.float32, smallest / len(shards), high / len(shards)))
        factor_of = factor_of * jnp.repeat(steps, shape[dim] // shards_of).reshape([-1 if axis == dim else 1 for axis in range(len(shape))])
    return factor_of


def scatter_about(own_key, extent, scale, limit, shards=(), kind=jnp.bfloat16):
    drawn = jax.random.normal(own_key, extent, jnp.float32) * scale
    if len(shards) > 0:
        drawn = levels(own_key, extent, shards, -0.22, 0.18) * drawn
    return jnp.clip(drawn, min=-limit, max=limit).astype(kind)


def setup_inputs(seed: int = 0) -> dict:
    key_list = jax.random.split(jax.random.key(seed), 6)
    inputs = scatter_about(key_list[0], (NLAT, NLON, C0), 1.0, 6.0, ((0, 8), (1, 32)))
    pre_first = scatter_about(key_list[1], (NLAT, NLON, C1), 1.0, 6.0, ((0, 8), (1, 32)))
    grad_out = scatter_about(key_list[2], (NLAT // 2, NLON // 2, C1), 1.0, 6.0, ((0, 8), (1, 32)))
    w_first = scatter_about(key_list[3], (3, 3, C0, C1), (9 * C0) ** -0.5, 0.25)
    w_second = scatter_about(key_list[4], (3, 3, C1, C1), (9 * C1) ** -0.5, 0.1875)
    return dict(inputs=inputs, pre_first=pre_first, grad_out=grad_out, w_first=w_first, w_second=w_second)


inv_root = 0.7071067811865476
density = 0.3989422804014327

def pad_fold(field):
    width = field.shape[1]
    cycle = jnp.concatenate([field[:, -1:], field, field[:, :1]], 1)
    turned = jnp.roll(field[0], -(width // 2), axis=0)
    top = jnp.concatenate([turned[-1:], turned, turned[:1]], 0)
    bottom = jnp.zeros_like(top)
    return jnp.concatenate([top[None], cycle, bottom[None]], 0)

def adjoint(grid, shape):
    _, pull = jax.vjp(pad_fold, jnp.zeros(shape, jnp.float32))
    return pull(grid)[0]

def taps_product(padded, grads):
    rows, cols = (grads.shape[0], grads.shape[1])
    flat = grads.reshape(rows * cols, grads.shape[2])
    result = []
    for a in range(3):
        line = []
        for b in range(3):
            piece = padded[a:a + rows, b:b + cols].reshape(rows * cols, padded.shape[2])
            line.append(jnp.dot(piece.T, flat, preferred_element_type=jnp.float32))
        result.append(jnp.stack(line, 0))
    return jnp.stack(result, 0)

def spread(grads, weight):
    rows, cols, cout = grads.shape
    cin = weight.shape[2]
    every = jnp.transpose(weight, (3, 0, 1, 2)).reshape(cout, 9 * cin)
    terms = jnp.dot(grads.reshape(rows * cols, cout), every, preferred_element_type=jnp.float32)
    terms = terms.reshape(rows, cols, 3, 3, cin)
    grid = jnp.zeros((rows + 2, cols + 2, cin), jnp.float32)
    for a in range(3):
        for b in range(3):
            grid = grid.at[a:a + rows, b:b + cols].add(terms[:, :, a, b])
    return grid

def reference(inputs, pre_first, grad_out, w_first, w_second):
    value = pre_first.astype(jnp.float32)
    cdf = 0.5 * (1.0 + lax.erf(value * inv_root))
    activated = (value * cdf).astype(jnp.bfloat16)
    slope = cdf + value * jnp.exp(-0.5 * value * value) * density
    grad_pool = jnp.repeat(jnp.repeat(grad_out, 2, 0), 2, 1) * jnp.asarray(0.25, grad_out.dtype)
    grad_w_second = taps_product(pad_fold(activated), grad_pool)
    grad_act = adjoint(spread(grad_pool, w_second), activated.shape)
    grad_pre = (grad_act * slope).astype(jnp.bfloat16)
    grad_w_first = taps_product(pad_fold(inputs), grad_pre)
    grad_inputs = adjoint(spread(grad_pre, w_first), inputs.shape).astype(jnp.bfloat16)
    return (grad_inputs, grad_w_first, grad_w_second)
```

```python
import functools

import jax
import jax.numpy as jnp
from jax import lax
from jax.experimental import pallas as pl
from jax.experimental.pallas import tpu as pltpu
from jax.sharding import PartitionSpec as P

INV_ROOT = 0.7071067811865476
DENSITY = 0.3989422804014327
BF16 = jnp.bfloat16
F32 = jnp.float32
MESH = pl.DeviceIdType.MESH

ROWS, COLS, C0, C1 = 16, 128, 64, 128
WIDE = COLS + 32
PWIDE = COLS // 2 + 16
GROUPS = 4


def gelu_parts(value):
    cdf = 0.5 * (1.0 + lax.erf(value * INV_ROOT))
    act = value * cdf
    slope = cdf + value * jnp.exp(-0.5 * value * value) * DENSITY
    return act, slope


def dot(a, b):
    return lax.dot_general(a, b, (((1,), (0,)), ((), ())), preferred_element_type=F32)


def kernel(
    nlat, nlon,
    pre_h, in_h, go_h, w1_h, w2_h,
    gi_o, gw_o,
    pre_v, in_v, go_v, w1_v, w2_v, wa, wb,
    e_s, row_s, e_r, row_r, hc, hs, hg,
    act_f, slope_f, act3, pext, gpt, in3, g_v, ga_f, gi_v,
    acc, p1s, p1r, p2s, p2r, zb, res,
    load_sem, halo_send, halo_recv, p1_send, p1_recv, p2_send, p2_recv,
    z_send, z_recv, p4_send, p4_recv, p5_send, p5_recv, out_sem,
):
    lat, lon = lax.axis_index("lat"), lax.axis_index("lon")
    nq, nz = nlat * 2, nlon // 4
    chunk = 1024 // nq
    per = nq // GROUPS
    z, yhi, core = lon // 4, (lon % 4) // 2, lon % 2
    q = lat * 2 + yhi
    is_pole = lat == 0
    is_last = lat == nlat - 1
    half = nlon // 2

    def chip(p, k):
        return (p // 2, z * 4 + (p % 2) * 2 + k)

    def at(dlat, dlon):
        return (dlat, lax.rem(dlon + 2 * nlon, nlon))

    loads = [
        pltpu.make_async_copy(src, dst, load_sem.at[i])
        for i, (src, dst) in enumerate(
            ((pre_h, pre_v), (in_h, in_v), (go_h, go_v), (w2_h, w2_v), (w1_h, w1_v))
        )
    ]
    for load in loads:
        load.start()

    barrier = pltpu.get_barrier_semaphore()

    def greet(device):
        pl.semaphore_signal(barrier, inc=1, device_id=device, device_id_type=MESH)

    top_lat = jnp.where(is_pole, 0, lat - 1)
    top_lon = jnp.where(is_pole, lon + half, lon)
    for d in (-1, 1):
        greet(at(lat, lon + d))
    for d in (-1, 0, 1):
        greet(at(top_lat, top_lon + d))

    @pl.when(jnp.logical_not(is_last))
    def _():
        for d in (-1, 0, 1):
            greet(at(lat + 1, lon + d))

    greet(chip(q, 1 - core))
    for k in range(1, nq):
        greet(chip(lax.rem(q + k, nq), core))
    for k in range(1, nz):
        greet((lat, lax.rem(lon + 4 * k, nlon)))

    loads[0].wait()
    loads[1].wait()
    loads[2].wait()
    lane = lax.broadcasted_iota(jnp.int32, (C0, 128), 1)
    sub = lax.broadcasted_iota(jnp.int32, (16, 128), 0)
    zero16 = jnp.zeros((16, 128), F32)
    for side, (col, first) in enumerate(((0, 0), (15, 112))):
        edge = zero16
        for r in range(ROWS):
            tile = pre_v[r, first : first + 16, :].astype(F32)
            edge = jnp.where(sub == r, jnp.broadcast_to(tile[col : col + 1], (16, 128)), edge)
        e_s[side, 0:16, :] = edge.astype(BF16)
        edge = zero16
        for r in range(ROWS // 2):
            tile = go_v[r, first // 112 * 48 : first // 112 * 48 + 16, :].astype(F32)
            edge = jnp.where(sub == r, jnp.broadcast_to(tile[col : col + 1], (16, 128)), edge)
        e_s[side, 16:32, :] = edge.astype(BF16)
        edge = jnp.zeros((C0, 128), F32)
        for r in range(ROWS):
            shift = r if side == 0 else r + 1
            edge = jnp.where(lane == r, pltpu.roll(in_v[r].astype(F32), shift, 1), edge)
        e_s[side, 32:96, :] = edge.astype(BF16)
    for end, r in enumerate((0, ROWS - 1)):
        row_s[end, 0:128, :] = pre_v[r]
        row_s[end, 128:192, :] = in_v[r]
        row_s[end, 192:256, :] = go_v[r // 2]

    pl.semaphore_wait(barrier, jnp.where(is_last, 0, 3) + 2 + 3 + 1 + (nq - 1) + (nz - 1))

    up = jnp.where(is_pole, 0, 2)
    up_row = jnp.where(is_pole, 0, 1)

    def edge_copy(number, side, slot, device):
        return pltpu.make_async_remote_copy(
            src_ref=e_s.at[side], dst_ref=e_r.at[slot], send_sem=halo_send.at[number],
            recv_sem=halo_recv.at[slot], device_id=device, device_id_type=MESH,
        )

    def row_copy(number, end, slot, device):
        return pltpu.make_async_remote_copy(
            src_ref=row_s.at[end], dst_ref=row_r.at[slot], send_sem=halo_send.at[number],
            recv_sem=halo_recv.at[6 + slot], device_id=device, device_id_type=MESH,
        )

    always = [
        row_copy(0, 0, up_row, at(top_lat, top_lon)),
        edge_copy(1, 1, 1, at(lat, lon + 1)),
        edge_copy(2, 0, 4, at(lat, lon - 1)),
        edge_copy(3, 1, up, at(top_lat, top_lon + 1)),
        edge_copy(4, 0, up + 3, at(top_lat, top_lon - 1)),
    ]
    down = [
        row_copy(5, 1, 0, at(lat + 1, lon)),
        edge_copy(6, 1, 0, at(lat + 1, lon + 1)),
        edge_copy(7, 0, 3, at(lat + 1, lon - 1)),
    ]
    for copy in always:
        copy.start()

    @pl.when(jnp.logical_not(is_last))
    def _():
        for copy in down:
            copy.start()

    @pl.when(is_last)
    def _():
        e_r[2] = jnp.zeros((96, 128), BF16)
        e_r[5] = jnp.zeros((96, 128), BF16)
        row_r[1] = jnp.zeros((256, 128), BF16)

    loads[3].wait()
    loads[4].wait()
    for a in range(3):
        for b in range(3):
            t = w2_v[3 * a + b].astype(F32).T.astype(BF16)
            wa[0, 128 * a : 128 * a + 128, 128 * b : 128 * b + 128] = t
            u = w1_v[3 * a + b].astype(F32).T.astype(BF16)
            wb[0, 128 * a : 128 * a + 128, 64 * b : 64 * b + 64] = u
    wa[1] = wa[0]
    wb[1] = wb[0]

    @pl.when(is_pole)
    def _():
        wa[1, 256:384, :] = wa[0, 0:128, :]
        wb[1, 256:384, :] = wb[0, 0:128, :]

    @pl.loop(0, ROWS)
    def _(r):
        act, slope = gelu_parts(pre_v[r].astype(F32))
        act_f[r + 1, 0:128, :] = act
        slope_f[r + 1, 0:128, :] = slope

    copies = lax.broadcasted_iota(jnp.int32, (64, 128), 1) // 2
    copies = jnp.where(copies == lax.broadcasted_iota(jnp.int32, (64, 128), 0), 0.25, 0.0).astype(BF16)
    gpt[:, 0:256] = jnp.zeros((128, 256), BF16)
    gpt[:, 18 * 128 : 20 * 128] = jnp.zeros((128, 256), BF16)
    for i in range(ROWS // 2):
        t = lax.dot_general(
            go_v[i], copies, (((0,), (0,)), ((), ())), preferred_element_type=F32
        ).astype(BF16)
        gpt[:, (2 * i + 2) * 128 : (2 * i + 3) * 128] = t
        gpt[:, (2 * i + 3) * 128 : (2 * i + 4) * 128] = t

    for number in range(5):
        always[number].wait_send()

    @pl.when(jnp.logical_not(is_last))
    def _():
        for copy in down:
            copy.wait_send()

    def arrived(slot):
        dst = e_r.at[slot] if slot < 6 else row_r.at[slot - 6]
        pltpu.make_async_copy(dst, dst, halo_recv.at[slot]).wait()

    for slot in (1, 4, 0, 3, 6):
        arrived(slot)

    @pl.when(jnp.logical_not(is_last))
    def _():
        for slot in (2, 5, 7):
            arrived(slot)

    keep = jnp.where(is_last, 0.0, 1.0).astype(F32)
    for side in range(2):
        top = e_r[3 * side, 0:32, :].astype(F32)
        mid = e_r[3 * side + 1, 0:32, :].astype(F32)
        low = e_r[3 * side + 2, 0:32, :].astype(F32)
        hc[side, 0:8, :] = jnp.broadcast_to(jnp.where(is_pole, top[0:1], top[15:16]), (8, 128))
        hc[side, 8:24, :] = mid[0:16]
        hc[side, 24:32, :] = jnp.broadcast_to(low[0:1], (8, 128))
        act, slope = gelu_parts(hc[side])
        hc[side] = act
        hs[side] = slope
        hg[side, 0:8, :] = 0.25 * jnp.broadcast_to(jnp.where(is_pole, top[16:17], top[23:24]), (8, 128))
        hg[side, 8:16, :] = 0.25 * mid[16:24]
        hg[side, 16:24, :] = 0.25 * jnp.broadcast_to(low[16:17], (8, 128))
    for end, t in enumerate((0, 17)):
        act, slope = gelu_parts(row_r[end, 0:128, :].astype(F32))
        act_f[t, 0:128, :] = act
        slope_f[t, 0:128, :] = slope if end == 0 else slope * keep
    for t in range(18):
        scale = keep if t == 17 else 1.0
        for side, place in enumerate((152, 128)):
            act_f[t, place : place + 8, :] = jnp.broadcast_to(hc[side, t + 7 : t + 8, :], (8, 128))
            slope_f[t, place : place + 8, :] = scale * jnp.broadcast_to(hs[side, t + 7 : t + 8, :], (8, 128))

    for i in range(10):
        part = go_v[i - 1] if 0 < i < 9 else row_r[0 if i == 0 else 1, 192:256, :]
        pext[i, 0:64, :] = (0.25 * part.astype(F32)).astype(BF16)
        left = jnp.broadcast_to(hg[0, i + 7 : i + 8, :], (16, 128))
        right = jnp.broadcast_to(hg[1, i + 7 : i + 8, :], (16, 128))
        tile = jnp.where(sub == 0, right, jnp.where(sub == 15, left, 0.0))
        pext[i, 64:80, :] = tile.astype(BF16)

    @pl.loop(0, 18)
    def _(t):
        x = act_f[t]
        rows = pl.ds(pl.multiple_of(t * 128, 128), 128)
        act3[rows, 0:128] = pltpu.roll(x, 1, 0)[0:128].astype(BF16)
        act3[rows, 128:256] = x[0:128].astype(BF16)
        act3[rows, 256:384] = pltpu.roll(x, WIDE - 1, 0)[0:128].astype(BF16)

    lhs = jnp.concatenate([gpt[:, (2 - a) * 128 : (2 - a) * 128 + 18 * 128] for a in range(3)], 0)
    both = dot(lhs, act3[...])
    for a in range(3):
        for b in range(3):
            block = both[128 * a : 128 * a + 128, 128 * b : 128 * b + 128]
            acc[(3 * a + b) * 128 : (3 * a + b + 1) * 128, :] = block.T

    @pl.loop(0, 9)
    def _(i):
        here, after = pext[i], pext[i + 1]
        lhs = jnp.concatenate(
            [jnp.concatenate([after, here, here], 1), jnp.concatenate([after, after, here], 1)], 0
        )
        taps = wa[jnp.where(i == 0, 1, 0)]
        terms = dot(lhs, taps)
        for s in range(2):
            part = terms[PWIDE * s : PWIDE * (s + 1)]
            t0, t1, t2 = part[:, 0:128], part[:, 128:256], part[:, 256:384]
            ga_f[s, pl.ds(0, PWIDE, stride=2), :] = t0 + t1 + pltpu.roll(t2, 1, 0)
            ga_f[s, pl.ds(1, PWIDE, stride=2), :] = pltpu.roll(t0, PWIDE - 1, 0) + t1 + t2
            g_v[2 * i + s] = (ga_f[s] * slope_f[2 * i + s]).astype(BF16)

    for t in range(18):
        if 0 < t < 17:
            x = in_v[t - 1].astype(F32)
            left = pltpu.roll(e_r[1, 32:96, :].astype(F32), (129 - t) % 128, 1)
            right = pltpu.roll(e_r[4, 32:96, :].astype(F32), 128 - t, 1)
        elif t == 0:
            x = row_r[0, 128:192, :].astype(F32)
            left = e_r[0, 32:96, :].astype(F32)
            left = jnp.where(is_pole, left, pltpu.roll(left, 128 - 15, 1))
            right = e_r[3, 32:96, :].astype(F32)
            right = jnp.where(is_pole, pltpu.roll(right, 127, 1), pltpu.roll(right, 112, 1))
        else:
            x = row_r[1, 128:192, :].astype(F32)
            left = e_r[2, 32:96, :].astype(F32)
            right = pltpu.roll(e_r[5, 32:96, :].astype(F32), 127, 1)
        cells = slice(128 * t, 128 * t + 128)
        in3[0:64, cells] = jnp.where(lane == 0, left, pltpu.roll(x, 1, 1)).astype(BF16)
        in3[64:128, cells] = x.astype(BF16)
        in3[128:192, cells] = jnp.where(lane == 127, right, pltpu.roll(x, 127, 1)).astype(BF16)

    lhs = jnp.concatenate([in3[:, a * 128 : a * 128 + 2048] for a in range(3)], 0)
    acc[1152:1728, :] = dot(lhs, g_v[1:17, 0:128, :].reshape(2048, 128))
    acc[1728:2048, :] = jnp.zeros((320, 128), F32)

    p1s[...] = acc[pl.ds(pl.multiple_of((1 - core) * 1024, 1024), 1024), :].astype(BF16)

    def group(i):
        return lax.rem(q // per + i, GROUPS)

    def group_rows(g):
        return pl.ds(pl.multiple_of(g * (per * chunk), 64), per * chunk)

    def p1_copy(i):
        rows = group_rows(group(i))
        return pltpu.make_async_remote_copy(
            src_ref=p1s.at[rows], dst_ref=p1r.at[rows], send_sem=p1_send.at[i], recv_sem=p1_recv.at[i],
            device_id=chip(q, 1 - core), device_id_type=MESH,
        )

    order = (1, 2, 3, 0)
    for i in order:
        p1_copy(i).start()

    def p2_copy(p):
        rows = pl.ds(pl.multiple_of(p * chunk, 64), chunk)
        return pltpu.make_async_remote_copy(
            src_ref=p2s.at[rows], dst_ref=p2r.at[q], send_sem=p2_send.at[p], recv_sem=p2_recv.at[q],
            device_id=chip(p, core), device_id_type=MESH,
        )

    for i in order:
        p1_copy(i).wait()
        rows = group_rows(group(i))
        own = pl.ds(pl.multiple_of(core * 1024 + group(i) * (per * chunk), 64), per * chunk)
        total = acc[own, :] + p1r[rows, :].astype(F32)
        acc[own, :] = total
        p2s[rows, :] = total.astype(BF16)
        for j in range(per):
            p = group(i) * per + lax.rem(q + j, per)
            if i == 0 and j == 0:
                continue
            p2_copy(p).start()

    @pl.loop(0, ROWS)
    def _(r):
        lhs = jnp.concatenate([g_v[r + 2], g_v[r + 1], g_v[r]], 1)
        terms = dot(lhs, wb[jnp.where(r == 0, 1, 0)])
        t01, t2 = terms[:, 0:128], terms[:, 128:192]
        first = lax.broadcasted_iota(jnp.int32, (128, 128), 1) < 64
        t01 = jnp.where(first, pltpu.roll(t01, WIDE - 1, 0)[0:128], t01[0:128]).T
        t2 = pltpu.roll(t2, 1, 0)[0:128].T
        gi_v[r] = (t01[0:64] + t01[64:128] + t2).astype(BF16)

    gi_copy = pltpu.make_async_copy(gi_v, gi_o, out_sem.at[0])
    gi_copy.start()

    total = acc[pl.ds(pl.multiple_of(core * 1024 + q * chunk, 64), chunk), :]
    for k in range(1, nq):
        p = lax.rem(q + nq - k, nq)
        pltpu.make_async_copy(p2r.at[p], p2r.at[p], p2_recv.at[p]).wait()
        total = total + p2r[p].astype(F32)
    zb[z] = total.astype(BF16)

    def z_copy(k):
        return pltpu.make_async_remote_copy(
            src_ref=zb.at[z], dst_ref=zb.at[z], send_sem=z_send.at[k], recv_sem=z_recv.at[z],
            device_id=(lat, lax.rem(lon + 4 * k, nlon)), device_id_type=MESH,
        )

    for k in range(1, nz):
        z_copy(k).start()
    for k in range(1, nz):
        p = lax.rem(z + nz - k, nz)
        pltpu.make_async_copy(zb.at[p], zb.at[p], z_recv.at[p]).wait()
    total = zb[0].astype(F32)
    for k in range(1, nz):
        total = total + zb[k].astype(F32)
    mine = pl.ds(pl.multiple_of(q * chunk, 64), chunk)
    res[core, mine, :] = total.astype(BF16)

    def p4_copy(p):
        return pltpu.make_async_remote_copy(
            src_ref=res.at[core, mine], dst_ref=res.at[core, mine], send_sem=p4_send.at[p],
            recv_sem=p4_recv.at[q], device_id=chip(p, core), device_id_type=MESH,
        )

    for k in range(1, nq):
        p4_copy(lax.rem(q + k, nq)).start()

    def p5_copy(i):
        rows = group_rows(group(i))
        return pltpu.make_async_remote_copy(
            src_ref=res.at[core, rows], dst_ref=res.at[core, rows], send_sem=p5_send.at[i],
            recv_sem=p5_recv.at[i], device_id=chip(q, 1 - core), device_id_type=MESH,
        )

    for i in (0, 3, 2, 1):
        for j in range(per):
            p = group(i) * per + lax.rem(q + per - j, per)
            if i == 0 and j == 0:
                continue
            there = pl.ds(pl.multiple_of(p * chunk, 64), chunk)
            pltpu.make_async_copy(res.at[core, there], res.at[core, there], p4_recv.at[p]).wait()
        p5_copy(i).start()
    for i in (0, 3, 2, 1):
        rows = group_rows(group(i))
        other = res.at[1 - core, rows]
        pltpu.make_async_copy(other, other, p5_recv.at[i]).wait()
    outs = [pltpu.make_async_copy(res.at[k], gw_o.at[pl.ds(1024 * k, 1024)], out_sem.at[1 + k]) for k in range(2)]
    for copy in outs:
        copy.start()

    for k in range(1, nq):
        p2_copy(lax.rem(q + k, nq)).wait_send()
        p4_copy(lax.rem(q + k, nq)).wait_send()
    for k in range(1, nz):
        z_copy(k).wait_send()
    for i in range(GROUPS):
        p5_copy(i).wait_send()
    gi_copy.wait()
    for copy in outs:
        copy.wait()


def section(nlat, nlon, inputs, pre_first, grad_out, w_first, w_second):
    nq, nz = nlat * 2, nlon // 4
    chunk = 1024 // nq
    hbm = pl.BlockSpec(memory_space=pl.ANY)
    vmem = pltpu.VMEM
    dma = pltpu.SemaphoreType.DMA
    gi, gw = pl.pallas_call(
        functools.partial(kernel, nlat, nlon),
        out_shape=(
            jax.ShapeDtypeStruct((ROWS, C0, COLS), BF16),
            jax.ShapeDtypeStruct((2048, 128), BF16),
        ),
        in_specs=[hbm] * 5,
        out_specs=(hbm, hbm),
        scratch_shapes=[
            vmem((ROWS, COLS, C1), BF16),
            vmem((ROWS, C0, COLS), BF16),
            vmem((ROWS // 2, COLS // 2, C1), BF16),
            vmem((9, C0, C1), BF16),
            vmem((9, C1, C1), BF16),
            vmem((2, 384, 384), BF16),
            vmem((2, 384, 192), BF16),
            vmem((2, 96, 128), BF16),
            vmem((2, 256, 128), BF16),
            vmem((6, 96, 128), BF16),
            vmem((2, 256, 128), BF16),
            vmem((2, 32, 128), F32),
            vmem((2, 32, 128), F32),
            vmem((2, 24, 128), F32),
            vmem((18, WIDE, 128), F32),
            vmem((18, WIDE, 128), F32),
            vmem((18 * 128, 384), BF16),
            vmem((10, PWIDE, 128), BF16),
            vmem((128, 20 * 128), BF16),
            vmem((192, 18 * 128), BF16),
            vmem((18, WIDE, 128), BF16),
            vmem((2, WIDE, 128), F32),
            vmem((ROWS, C0, COLS), BF16),
            vmem((2048, 128), F32),
            vmem((1024, 128), BF16),
            vmem((1024, 128), BF16),
            vmem((1024, 128), BF16),
            vmem((nq, chunk, 128), BF16),
            vmem((nz, chunk, 128), BF16),
            vmem((2, 1024, 128), BF16),
            dma((5,)),
            dma((8,)), dma((8,)),
            dma((GROUPS,)), dma((GROUPS,)),
            dma((nq,)), dma((nq,)),
            dma((nz,)), dma((nz,)),
            dma((nq,)), dma((nq,)),
            dma((GROUPS,)), dma((GROUPS,)),
            dma((3,)),
        ],
        compiler_params=pltpu.CompilerParams(
            collective_id=0, has_side_effects=True, vmem_limit_bytes=40 * 1024 * 1024
        ),
        cost_estimate=pl.CostEstimate(flops=1_800_000_000, bytes_accessed=3_000_000, transcendentals=600_000),
    )(
        pre_first,
        jnp.transpose(inputs, (0, 2, 1)),
        grad_out,
        w_first.reshape(9, C0, C1),
        w_second.reshape(9, C1, C1),
    )
    grad_w_second = gw[0:1152].astype(F32).reshape(3, 3, C1, C1)
    grad_w_first = gw[1152:1728].astype(F32).reshape(3, 3, C0, C1)
    return jnp.transpose(gi, (0, 2, 1)), grad_w_first, grad_w_second


def solution(mesh):
    nlat, nlon = mesh.shape["lat"], mesh.shape["lon"]
    in_specs = (P("lat", "lon", None), P("lat", "lon", None), P("lat", "lon", None), P(), P())
    out_specs = (P("lat", "lon", None), P(), P())
    return jax.shard_map(
        functools.partial(section, nlat, nlon), mesh=mesh, in_specs=in_specs, out_specs=out_specs, check_vma=False
    )
```

```python
import functools

import jax
import jax.numpy as jnp
from jax import lax
from jax.experimental import pallas as pl
from jax.experimental.pallas import tpu as pltpu
from jax.sharding import PartitionSpec as P

INV_ROOT = 0.7071067811865476
DENSITY = 0.3989422804014327
BF16 = jnp.bfloat16
F32 = jnp.float32
MESH = pl.DeviceIdType.MESH

ROWS, COLS, C0, C1 = 16, 128, 64, 128
WIDE = COLS + 32
PWIDE = COLS // 2 + 16
GROUPS = 4


def gelu_parts(value):
    cdf = 0.5 * (1.0 + lax.erf(value * INV_ROOT))
    act = value * cdf
    slope = cdf + value * jnp.exp(-0.5 * value * value) * DENSITY
    return act, slope


def dot(a, b):
    return lax.dot_general(a, b, (((1,), (0,)), ((), ())), preferred_element_type=F32)


def kernel(
    nlat, nlon,
    pre_h, in_h, go_h, w1_h, w2_h,
    gi_o, gw_o,
    pre_v, in_v, go_v, w1_v, w2_v, wa, wb,
    e_s, row_s, e_r, row_r, hc, hs, hg, hi,
    act_f, slope_f, act3, pext, gpt, gpt_top, in3, g_v, ga_f, both,
    acc, p1s, p1r, p2s, p2r, zb, res,
    load_sem, halo_send, halo_recv, p1_send, p1_recv, p2_send, p2_recv,
    z_send, z_recv, p4_send, p4_recv, p5_send, p5_recv,
):
    lat, lon = lax.axis_index("lat"), lax.axis_index("lon")
    nq, nz = nlat * 2, nlon // 4
    chunk = 1024 // nq
    per = nq // GROUPS
    z, yhi, core = lon // 4, (lon % 4) // 2, lon % 2
    q = lat * 2 + yhi
    is_pole = lat == 0
    is_last = lat == nlat - 1
    half = nlon // 2

    def chip(p, k):
        return (p // 2, z * 4 + (p % 2) * 2 + k)

    def at(dlat, dlon):
        return (dlat, lax.rem(dlon + 2 * nlon, nlon))

    loads = [
        pltpu.make_async_copy(src, dst, load_sem.at[i])
        for i, (src, dst) in enumerate(
            ((pre_h, pre_v), (in_h, in_v), (go_h, go_v), (w2_h, w2_v), (w1_h, w1_v))
        )
    ]
    for load in loads:
        load.start()

    barrier = pltpu.get_barrier_semaphore()

    def greet(device):
        pl.semaphore_signal(barrier, inc=1, device_id=device, device_id_type=MESH)

    top_lat = jnp.where(is_pole, 0, lat - 1)
    top_lon = jnp.where(is_pole, lon + half, lon)
    for d in (-1, 1):
        greet(at(lat, lon + d))
    for d in (-1, 0, 1):
        greet(at(top_lat, top_lon + d))

    @pl.when(jnp.logical_not(is_last))
    def _():
        for d in (-1, 0, 1):
            greet(at(lat + 1, lon + d))

    greet(chip(q, 1 - core))
    for k in range(1, nq):
        greet(chip(lax.rem(q + k, nq), core))
    for k in range(1, nz):
        greet((lat, lax.rem(lon + 4 * k, nlon)))

    loads[0].wait()
    loads[1].wait()
    loads[2].wait()
    lane = lax.broadcasted_iota(jnp.int32, (C0, 128), 1)
    sub = lax.broadcasted_iota(jnp.int32, (16, 128), 0)
    zero16 = jnp.zeros((16, 128), F32)
    for side, (col, first) in enumerate(((0, 0), (15, 112))):
        edge = zero16
        for r in range(ROWS):
            tile = pre_v[r, first : first + 16, :].astype(F32)
            edge = jnp.where(sub == r, jnp.broadcast_to(tile[col : col + 1], (16, 128)), edge)
        e_s[side, 0:16, :] = edge.astype(BF16)
        edge = zero16
        for r in range(ROWS // 2):
            tile = go_v[r, first // 112 * 48 : first // 112 * 48 + 16, :].astype(F32)
            edge = jnp.where(sub == r, jnp.broadcast_to(tile[col : col + 1], (16, 128)), edge)
        e_s[side, 16:32, :] = edge.astype(BF16)
        edge = jnp.zeros((C0, 128), F32)
        for r in range(ROWS):
            shift = r if side == 0 else r + 1
            edge = jnp.where(lane == r, pltpu.roll(in_v[r].astype(F32), shift, 1), edge)
        e_s[side, 32:48, 0:64] = edge.T[0:16].astype(BF16)
        e_s[side, 32:48, 64:128] = jnp.zeros((16, 64), BF16)
    for end, r in enumerate((0, ROWS - 1)):
        row_s[end, 0:128, :] = pre_v[r]
        row_s[end, 128:192, :] = go_v[r // 2]
        row_s[end, 192:256, :] = in_v[r]

    pl.semaphore_wait(barrier, jnp.where(is_last, 0, 3) + 2 + 3 + 1 + (nq - 1) + (nz - 1))

    up = jnp.where(is_pole, 0, 2)

    def edge_copy(number, side, slot, device):
        return pltpu.make_async_remote_copy(
            src_ref=e_s.at[side], dst_ref=e_r.at[slot], send_sem=halo_send.at[number],
            recv_sem=halo_recv.at[slot], device_id=device, device_id_type=MESH,
        )

    def row_copy(number, end, slot, device, size=256):
        return pltpu.make_async_remote_copy(
            src_ref=row_s.at[end, pl.ds(0, size)], dst_ref=row_r.at[slot, pl.ds(0, size)], send_sem=halo_send.at[number],
            recv_sem=halo_recv.at[6 + slot], device_id=device, device_id_type=MESH,
        )

    turned = row_copy(0, 0, 0, at(0, lon + half), 192)
    above = row_copy(0, 0, 1, at(lat - 1, lon))
    always = [
        edge_copy(1, 1, 1, at(lat, lon + 1)),
        edge_copy(2, 0, 4, at(lat, lon - 1)),
        edge_copy(3, 1, up, at(top_lat, top_lon + 1)),
        edge_copy(4, 0, up + 3, at(top_lat, top_lon - 1)),
    ]
    down = [
        row_copy(5, 1, 0, at(lat + 1, lon)),
        edge_copy(6, 1, 0, at(lat + 1, lon + 1)),
        edge_copy(7, 0, 3, at(lat + 1, lon - 1)),
    ]
    @pl.when(is_pole)
    def _():
        turned.start()

    @pl.when(jnp.logical_not(is_pole))
    def _():
        above.start()

    for copy in always:
        copy.start()

    @pl.when(jnp.logical_not(is_last))
    def _():
        for copy in down:
            copy.start()

    @pl.when(is_last)
    def _():
        e_r[2] = jnp.zeros((48, 128), BF16)
        e_r[5] = jnp.zeros((48, 128), BF16)
        row_r[1] = jnp.zeros((256, 128), BF16)

    loads[3].wait()
    loads[4].wait()
    for a in range(3):
        for b in range(3):
            t = w2_v[3 * a + b].astype(F32).T.astype(BF16)
            wa[0, 128 * a : 128 * a + 128, 128 * b : 128 * b + 128] = t
            u = w1_v[3 * a + b].astype(F32).T.astype(BF16)
            wb[0, 128 * a : 128 * a + 128, 64 * b : 64 * b + 64] = u
    wa[1] = wa[0]
    wb[1] = wb[0]

    @pl.when(is_pole)
    def _():
        wa[1, 256:384, :] = wa[0, 0:128, :]
        wb[1, 256:384, :] = wb[0, 0:128, :]

    @pl.loop(0, ROWS)
    def _(r):
        act, slope = gelu_parts(pre_v[r].astype(F32))
        act_f[r + 1, 0:128, :] = act
        slope_f[r + 1, 0:128, :] = slope

    copies = lax.broadcasted_iota(jnp.int32, (64, 128), 1) // 2
    copies = jnp.where(copies == lax.broadcasted_iota(jnp.int32, (64, 128), 0), 0.25, 0.0).astype(BF16)
    gpt[:, 0:256] = jnp.zeros((128, 256), BF16)
    gpt[:, 18 * 128 : 20 * 128] = jnp.zeros((128, 256), BF16)
    for i in range(ROWS // 2):
        t = lax.dot_general(
            go_v[i], copies, (((0,), (0,)), ((), ())), preferred_element_type=F32
        ).astype(BF16)
        gpt[:, (2 * i + 2) * 128 : (2 * i + 3) * 128] = t
        gpt[:, (2 * i + 3) * 128 : (2 * i + 4) * 128] = t

    def arrived(slot):
        dst = e_r.at[slot] if slot < 6 else row_r.at[slot - 6]
        pltpu.make_async_copy(dst, dst, halo_recv.at[slot]).wait()

    for slot in (1, 4):
        arrived(slot)

    @pl.when(jnp.logical_not(is_last))
    def _():
        for slot in (2, 5, 7):
            arrived(slot)

    keep = jnp.where(is_last, 0.0, 1.0).astype(F32)
    zero8 = jnp.zeros((8, 128), F32)
    for side in range(2):
        mid = e_r[3 * side + 1].astype(F32)
        low = e_r[3 * side + 2].astype(F32)
        hc[side, 8:24, :] = mid[0:16]
        hc[side, 24:32, :] = jnp.broadcast_to(low[0:1], (8, 128))
        act, slope = gelu_parts(hc[side, 8:32, :])
        hc[side, 8:32, :] = act
        hs[side, 8:32, :] = slope
        hg[side, 8:16, :] = 0.25 * mid[16:24]
        hg[side, 16:24, :] = 0.25 * jnp.broadcast_to(low[16:17], (8, 128))
        hi[side, 0:8, :] = zero8
        hi[side, 8:24, :] = mid[32:48]
        hi[side, 24:32, :] = jnp.broadcast_to(low[32:33], (8, 128))
    act, slope = gelu_parts(row_r[1, 0:128, :].astype(F32))
    act_f[17, 0:128, :] = act
    slope_f[17, 0:128, :] = slope * keep

    def sides(t):
        scale = keep if t == 17 else 1.0
        for side, place in enumerate((152, 128)):
            act_f[t, place : place + 8, :] = jnp.broadcast_to(hc[side, t + 7 : t + 8, :], (8, 128))
            slope_f[t, place : place + 8, :] = scale * jnp.broadcast_to(hs[side, t + 7 : t + 8, :], (8, 128))

    def pooled(i, part):
        pext[i, 0:64, :] = (0.25 * part.astype(F32)).astype(BF16)
        left = jnp.broadcast_to(hg[0, i + 7 : i + 8, :], (16, 128))
        right = jnp.broadcast_to(hg[1, i + 7 : i + 8, :], (16, 128))
        tile = jnp.where(sub == 0, right, jnp.where(sub == 15, left, 0.0))
        pext[i, 64:80, :] = tile.astype(BF16)

    def act_row(t):
        x = act_f[t]
        rows = pl.ds(pl.multiple_of(t * 128, 128), 128)
        act3[rows, 0:128] = pltpu.roll(x, 1, 0)[0:128].astype(BF16)
        act3[rows, 128:256] = x[0:128].astype(BF16)
        act3[rows, 256:384] = pltpu.roll(x, WIDE - 1, 0)[0:128].astype(BF16)

    for t in range(1, 18):
        sides(t)
    for i in range(1, 10):
        pooled(i, go_v[i - 1] if i < 9 else row_r[1, 128:192, :])

    @pl.loop(1, 18)
    def _(t):
        act_row(t)

    lhs = jnp.concatenate([gpt[:, (3 - a) * 128 : (3 - a) * 128 + 17 * 128] for a in range(3)], 0)
    terms = dot(lhs, act3[128:2304, :])
    both[...] = terms[0:128]
    for a in range(1, 3):
        for b in range(3):
            block = terms[128 * a : 128 * a + 128, 128 * b : 128 * b + 128]
            acc[(3 * a + b) * 128 : (3 * a + b + 1) * 128, :] = block.T

    def grad_rows(i, taps):
        here, after = pext[i], pext[i + 1]
        lhs = jnp.concatenate(
            [jnp.concatenate([after, here, here], 1), jnp.concatenate([after, after, here], 1)], 0
        )
        terms = dot(lhs, taps)
        for s in range(2):
            part = terms[PWIDE * s : PWIDE * (s + 1)]
            t0, t1, t2 = part[:, 0:128], part[:, 128:256], part[:, 256:384]
            ga_f[s, pl.ds(0, PWIDE, stride=2), :] = t0 + t1 + pltpu.roll(t2, 1, 0)
            ga_f[s, pl.ds(1, PWIDE, stride=2), :] = pltpu.roll(t0, PWIDE - 1, 0) + t1 + t2
            g_v[2 * i + s] = (ga_f[s] * slope_f[2 * i + s]).astype(BF16)

    @pl.loop(1, 9)
    def _(i):
        grad_rows(i, wa[0])

    edges = [jnp.concatenate([hi[side], jnp.zeros((96, 128), F32)], 0).T[0:64] for side in range(2)]

    def in_row(t, x, left, right):
        cells = slice(128 * t, 128 * t + 128)
        in3[0:64, cells] = jnp.where(lane == 0, left, pltpu.roll(x, 1, 1)).astype(BF16)
        in3[64:128, cells] = x.astype(BF16)
        in3[128:192, cells] = jnp.where(lane == 127, right, pltpu.roll(x, 127, 1)).astype(BF16)

    for t in range(1, 18):
        x = (in_v[t - 1] if t < 17 else row_r[1, 192:256, :]).astype(F32)
        in_row(t, x, pltpu.roll(edges[0], 121 - t, 1), pltpu.roll(edges[1], 120 - t, 1))

    lhs = jnp.concatenate([in3[:, (a + 1) * 128 : (a + 16) * 128] for a in range(3)], 0)
    acc[1152:1728, :] = dot(lhs, g_v[2:17, 0:128, :].reshape(1920, 128))
    acc[1728:2048, :] = jnp.zeros((320, 128), F32)

    @pl.when(is_pole)
    def _():
        dst = row_r.at[0, pl.ds(0, 192)]
        pltpu.make_async_copy(dst, dst, halo_recv.at[6]).wait()
        row_r[0, 192:256, :] = jnp.zeros((64, 128), BF16)

    @pl.when(jnp.logical_not(is_pole))
    def _():
        arrived(6)

    arrived(0)
    arrived(3)
    for side in range(2):
        top = e_r[3 * side].astype(F32)

        def pick(first, last):
            return jnp.broadcast_to(jnp.where(is_pole, top[first : first + 1], top[last : last + 1]), (8, 128))

        act, slope = gelu_parts(pick(0, 15))
        hc[side, 0:8, :] = act
        hs[side, 0:8, :] = slope
        hg[side, 0:8, :] = 0.25 * pick(16, 23)
        hi[side, 0:8, :] = jnp.where(is_pole, 0.0, pick(32, 47))
    act, slope = gelu_parts(row_r[0, 0:128, :].astype(F32))
    act_f[0, 0:128, :] = act
    slope_f[0, 0:128, :] = slope
    sides(0)
    pooled(0, row_r[0, 128:192, :])
    grad_rows(0, wa[1])

    act_row(0)
    top_go = lax.dot_general(
        row_r[0, 128:192, :], copies, (((0,), (0,)), ((), ())), preferred_element_type=F32
    ).astype(BF16)
    gpt_top[...] = jnp.where(is_pole, top_go.astype(F32), gpt[:, 256:384].astype(F32)).astype(BF16)

    @pl.when(is_pole)
    def _():
        act3[0:128, :] = act3[128:256, :]

    first_row = both[...] + dot(gpt_top[...], act3[0:128, :])
    for b in range(3):
        acc[b * 128 : (b + 1) * 128, :] = first_row[:, 128 * b : 128 * b + 128].T

    x = row_r[0, 192:256, :].astype(F32)
    edges = [jnp.concatenate([hi[side], jnp.zeros((96, 128), F32)], 0).T[0:64] for side in range(2)]
    in_row(0, x, pltpu.roll(edges[0], 121, 1), pltpu.roll(edges[1], 120, 1))
    here = jnp.concatenate([in3[:, 0:128], in3[:, 128:256], in3[:, 256:384]], 0)
    fold = jnp.where(is_pole, in3[:, 128:256].astype(F32), 0.0).astype(BF16)
    there = jnp.concatenate([fold, jnp.zeros((384, 128), BF16)], 0)
    acc[1152:1728, :] += dot(jnp.concatenate([here, there], 1), jnp.concatenate([g_v[1, 0:128, :], g_v[0, 0:128, :]], 0))

    p1s[...] = acc[pl.ds(pl.multiple_of((1 - core) * 1024, 1024), 1024), :].astype(BF16)

    def group(i):
        return lax.rem(q // per + i, GROUPS)

    def group_rows(g):
        return pl.ds(pl.multiple_of(g * (per * chunk), 64), per * chunk)

    def p1_copy(i):
        rows = group_rows(group(i))
        return pltpu.make_async_remote_copy(
            src_ref=p1s.at[rows], dst_ref=p1r.at[rows], send_sem=p1_send.at[i], recv_sem=p1_recv.at[i],
            device_id=chip(q, 1 - core), device_id_type=MESH,
        )

    order = (1, 2, 3, 0)
    for i in order:
        p1_copy(i).start()

    def p2_copy(p):
        rows = pl.ds(pl.multiple_of(p * chunk, 64), chunk)
        return pltpu.make_async_remote_copy(
            src_ref=p2s.at[rows], dst_ref=p2r.at[q], send_sem=p2_send.at[p], recv_sem=p2_recv.at[q],
            device_id=chip(p, core), device_id_type=MESH,
        )

    for i in order:
        p1_copy(i).wait()
        rows = group_rows(group(i))
        own = pl.ds(pl.multiple_of(core * 1024 + group(i) * (per * chunk), 64), per * chunk)
        total = acc[own, :] + p1r[rows, :].astype(F32)
        acc[own, :] = total
        p2s[rows, :] = total.astype(BF16)
        for j in range(per):
            p = group(i) * per + lax.rem(q + j, per)
            if i == 0 and j == 0:
                continue
            p2_copy(p).start()

    @pl.loop(0, ROWS)
    def _(r):
        lhs = jnp.concatenate([g_v[r + 2], g_v[r + 1], g_v[r]], 1)
        terms = dot(lhs, wb[jnp.where(r == 0, 1, 0)])
        t01, t2 = terms[:, 0:128], terms[:, 128:192]
        first = lax.broadcasted_iota(jnp.int32, (128, 128), 1) < 64
        t01 = jnp.where(first, pltpu.roll(t01, WIDE - 1, 0)[0:128], t01[0:128]).T
        t2 = pltpu.roll(t2, 1, 0)[0:128].T
        gi_o[r] = (t01[0:64] + t01[64:128] + t2).astype(BF16)

    total = acc[pl.ds(pl.multiple_of(core * 1024 + q * chunk, 64), chunk), :]
    for k in range(1, nq):
        p = lax.rem(q + nq - k, nq)
        pltpu.make_async_copy(p2r.at[p], p2r.at[p], p2_recv.at[p]).wait()
        total = total + p2r[p].astype(F32)
    zb[z] = total.astype(BF16)

    def z_copy(k):
        return pltpu.make_async_remote_copy(
            src_ref=zb.at[z], dst_ref=zb.at[z], send_sem=z_send.at[k], recv_sem=z_recv.at[z],
            device_id=(lat, lax.rem(lon + 4 * k, nlon)), device_id_type=MESH,
        )

    for k in range(1, nz):
        z_copy(k).start()
    for k in range(1, nz):
        p = lax.rem(z + nz - k, nz)
        pltpu.make_async_copy(zb.at[p], zb.at[p], z_recv.at[p]).wait()
    total = zb[0].astype(F32)
    for k in range(1, nz):
        total = total + zb[k].astype(F32)
    mine = pl.ds(pl.multiple_of(q * chunk, 64), chunk)
    res[core, mine, :] = total.astype(BF16)

    def p4_copy(p):
        return pltpu.make_async_remote_copy(
            src_ref=res.at[core, mine], dst_ref=res.at[core, mine], send_sem=p4_send.at[p],
            recv_sem=p4_recv.at[q], device_id=chip(p, core), device_id_type=MESH,
        )

    for k in range(1, nq):
        p4_copy(lax.rem(q + k, nq)).start()

    def p5_copy(p):
        rows = pl.ds(pl.multiple_of(p * chunk, 64), chunk)
        return pltpu.make_async_remote_copy(
            src_ref=res.at[core, rows], dst_ref=res.at[core, rows], send_sem=p5_send.at[p],
            recv_sem=p5_recv.at[p], device_id=chip(q, 1 - core), device_id_type=MESH,
        )

    def deliver(k, p):
        rows = pl.ds(pl.multiple_of(p * chunk, 64), chunk)
        gw_o[pl.ds(pl.multiple_of(k * 1024 + p * chunk, 64), chunk), :] = res[k, rows, :].astype(F32)

    p5_copy(q).start()
    deliver(core, q)
    for k in range(1, nq):
        p = lax.rem(q + nq - k, nq)
        there = pl.ds(pl.multiple_of(p * chunk, 64), chunk)
        pltpu.make_async_copy(res.at[core, there], res.at[core, there], p4_recv.at[p]).wait()
        p5_copy(p).start()
        deliver(core, p)
    for k in range(nq):
        p = lax.rem(q + nq - k, nq)
        there = pl.ds(pl.multiple_of(p * chunk, 64), chunk)
        other = res.at[1 - core, there]
        pltpu.make_async_copy(other, other, p5_recv.at[p]).wait()
        deliver(1 - core, p)

    @pl.when(is_pole)
    def _():
        turned.wait_send()

    @pl.when(jnp.logical_not(is_pole))
    def _():
        above.wait_send()

    for copy in always:
        copy.wait_send()

    @pl.when(jnp.logical_not(is_last))
    def _():
        for copy in down:
            copy.wait_send()

    for k in range(1, nq):
        p2_copy(lax.rem(q + k, nq)).wait_send()
        p4_copy(lax.rem(q + k, nq)).wait_send()
    for k in range(1, nz):
        z_copy(k).wait_send()
    for p in range(nq):
        p5_copy(p).wait_send()


def write_out(gi_v, gw_v, gi_o, gw1_o, gw2_o, sem):
    copies = [
        pltpu.make_async_copy(gw_v.at[pl.ds(0, 1152)], gw2_o, sem.at[0]),
        pltpu.make_async_copy(gw_v.at[pl.ds(1152, 576)], gw1_o, sem.at[1]),
        pltpu.make_async_copy(gi_v, gi_o, sem.at[2]),
    ]
    for copy in copies:
        copy.start()
    for copy in copies:
        copy.wait()


def section(nlat, nlon, inputs, pre_first, grad_out, w_first, w_second):
    nq, nz = nlat * 2, nlon // 4
    chunk = 1024 // nq
    hbm = pl.BlockSpec(memory_space=pltpu.HBM)
    vmem = pltpu.VMEM
    dma = pltpu.SemaphoreType.DMA
    gi, gw = pl.pallas_call(
        functools.partial(kernel, nlat, nlon),
        out_shape=(vmem((ROWS, C0, COLS), BF16), vmem((2048, 128), F32)),
        in_specs=[hbm] * 5,
        out_specs=(pl.BlockSpec(memory_space=vmem), pl.BlockSpec(memory_space=vmem)),
        scratch_shapes=[
            vmem((ROWS, COLS, C1), BF16),
            vmem((ROWS, C0, COLS), BF16),
            vmem((ROWS // 2, COLS // 2, C1), BF16),
            vmem((9, C0, C1), BF16),
            vmem((9, C1, C1), BF16),
            vmem((2, 384, 384), BF16),
            vmem((2, 384, 192), BF16),
            vmem((2, 48, 128), BF16),
            vmem((2, 256, 128), BF16),
            vmem((6, 48, 128), BF16),
            vmem((2, 256, 128), BF16),
            vmem((2, 32, 128), F32),
            vmem((2, 32, 128), F32),
            vmem((2, 24, 128), F32),
            vmem((2, 32, 128), F32),
            vmem((18, WIDE, 128), F32),
            vmem((18, WIDE, 128), F32),
            vmem((18 * 128, 384), BF16),
            vmem((10, PWIDE, 128), BF16),
            vmem((128, 20 * 128), BF16),
            vmem((128, 128), BF16),
            vmem((192, 18 * 128), BF16),
            vmem((18, WIDE, 128), BF16),
            vmem((2, WIDE, 128), F32),
            vmem((128, 384), F32),
            vmem((2048, 128), F32),
            vmem((1024, 128), BF16),
            vmem((1024, 128), BF16),
            vmem((1024, 128), BF16),
            vmem((nq, chunk, 128), BF16),
            vmem((nz, chunk, 128), BF16),
            vmem((2, 1024, 128), BF16),
            dma((5,)),
            dma((8,)), dma((8,)),
            dma((GROUPS,)), dma((GROUPS,)),
            dma((nq,)), dma((nq,)),
            dma((nz,)), dma((nz,)),
            dma((nq,)), dma((nq,)),
            dma((nq,)), dma((nq,)),
        ],
        compiler_params=pltpu.CompilerParams(
            collective_id=0, has_side_effects=True, vmem_limit_bytes=40 * 1024 * 1024
        ),
        cost_estimate=pl.CostEstimate(flops=1_800_000_000, bytes_accessed=3_000_000, transcendentals=600_000),
    )(
        *(
            pltpu.with_memory_space_constraint(x, pltpu.HBM)
            for x in (
                pre_first,
                jnp.transpose(inputs, (0, 2, 1)),
                grad_out,
                w_first.reshape(9, C0, C1),
                w_second.reshape(9, C1, C1),
            )
        )
    )
    gi, grad_w_first, grad_w_second = pl.pallas_call(
        write_out,
        out_shape=(
            jax.ShapeDtypeStruct((ROWS, C0, COLS), BF16),
            jax.ShapeDtypeStruct((9 * C0, C1), F32),
            jax.ShapeDtypeStruct((9 * C1, C1), F32),
        ),
        in_specs=[pl.BlockSpec(memory_space=vmem)] * 2,
        out_specs=(pl.BlockSpec(memory_space=pl.ANY),) * 3,
        scratch_shapes=[dma((3,))],
        compiler_params=pltpu.CompilerParams(vmem_limit_bytes=16 * 1024 * 1024),
    )(gi, gw)
    return (
        jnp.transpose(gi, (0, 2, 1)),
        grad_w_first.reshape(3, 3, C0, C1),
        grad_w_second.reshape(3, 3, C1, C1),
    )


def solution(mesh):
    nlat, nlon = mesh.shape["lat"], mesh.shape["lon"]
    in_specs = (P("lat", "lon", None), P("lat", "lon", None), P("lat", "lon", None), P(), P())
    out_specs = (P("lat", "lon", None), P(), P())
    return jax.shard_map(
        functools.partial(section, nlat, nlon), mesh=mesh, in_specs=in_specs, out_specs=out_specs, check_vma=False
    )
```

```python
import functools

import jax
import jax.numpy as jnp
from jax import lax
from jax.experimental import pallas as pl
from jax.experimental.pallas import tpu as pltpu
from jax.sharding import PartitionSpec as P

INV_ROOT = 0.7071067811865476
DENSITY = 0.3989422804014327
BF16 = jnp.bfloat16
F32 = jnp.float32
MESH = pl.DeviceIdType.MESH

ROWS, COLS, C0, C1 = 16, 128, 64, 128
WIDE = COLS + 32
PWIDE = COLS // 2 + 16
HALF = 512


def far_first(n):
    return sorted(range(1, n), key=lambda k: (-min(k, n - k), k))


def gelu_parts(value):
    cdf = 0.5 * (1.0 + lax.erf(value * INV_ROOT))
    act = value * cdf
    slope = cdf + value * jnp.exp(-0.5 * value * value) * DENSITY
    return act, slope


def dot(a, b):
    return lax.dot_general(a, b, (((1,), (0,)), ((), ())), preferred_element_type=F32)


def kernel(
    nlat, nlon,
    pre_h, in_h, go_h, w1_h, w2_h,
    gi_o, gw_o,
    pre_v, in_v, go_v, w1_v, w2_v, wa, wb,
    e_s, row_s, e_r, row_r, hc, hs, hg, hi,
    act_f, slope_f, act3, pext, gpt, gpt_top, in3, g_v, ga_f, both,
    acc, p1s, p1r, p2s, p2r, zb, res,
    load_sem, halo_send, halo_recv, p1_send, p1_recv, p2_send, p2_recv,
    z_send, z_recv, p4_send, p4_recv, p5_send, p5_recv,
):
    lat, lon = lax.axis_index("lat"), lax.axis_index("lon")
    nq, nz = nlat * 2, nlon // 4
    chunk = HALF // nq
    z, yhi, core = lon // 4, (lon % 4) // 2, lon % 2
    q = lat * 2 + yhi
    is_pole = lat == 0
    is_last = lat == nlat - 1
    half = nlon // 2

    def chip(p, k):
        return (p // 2, z * 4 + (p % 2) * 2 + k)

    def at(dlat, dlon):
        return (dlat, lax.rem(dlon + 2 * nlon, nlon))

    loads = [
        pltpu.make_async_copy(src, dst, load_sem.at[i])
        for i, (src, dst) in enumerate(
            ((pre_h, pre_v), (in_h, in_v), (go_h, go_v), (w2_h, w2_v), (w1_h, w1_v))
        )
    ]
    for load in loads:
        load.start()

    barrier = pltpu.get_barrier_semaphore()

    def greet(device):
        pl.semaphore_signal(barrier, inc=1, device_id=device, device_id_type=MESH)

    top_lat = jnp.where(is_pole, 0, lat - 1)
    top_lon = jnp.where(is_pole, lon + half, lon)
    for d in (-1, 0, 1):
        greet(at(top_lat, top_lon + d))
    for k in far_first(nz):
        greet((lat, lax.rem(lon + 4 * k, nlon)))
    for k in far_first(nq):
        greet(chip(lax.rem(q + k, nq), core))
    for d in (-1, 1):
        greet(at(lat, lon + d))

    @pl.when(jnp.logical_not(is_last))
    def _():
        for d in (-1, 0, 1):
            greet(at(lat + 1, lon + d))

    greet(chip(q, 1 - core))

    loads[0].wait()
    loads[1].wait()
    loads[2].wait()
    lane = lax.broadcasted_iota(jnp.int32, (C0, 128), 1)
    sub = lax.broadcasted_iota(jnp.int32, (16, 128), 0)
    zero16 = jnp.zeros((16, 128), F32)
    for side, (col, first) in enumerate(((0, 0), (15, 112))):
        edge = zero16
        for r in range(ROWS):
            tile = pre_v[r, first : first + 16, :].astype(F32)
            edge = jnp.where(sub == r, jnp.broadcast_to(tile[col : col + 1], (16, 128)), edge)
        e_s[side, 0:16, :] = edge.astype(BF16)
        edge = zero16
        for r in range(ROWS // 2):
            tile = go_v[r, first // 112 * 48 : first // 112 * 48 + 16, :].astype(F32)
            edge = jnp.where(sub == r, jnp.broadcast_to(tile[col : col + 1], (16, 128)), edge)
        e_s[side, 16:32, :] = edge.astype(BF16)
        edge = jnp.zeros((C0, 128), F32)
        for r in range(ROWS):
            shift = r if side == 0 else r + 1
            edge = jnp.where(lane == r, pltpu.roll(in_v[r].astype(F32), shift, 1), edge)
        e_s[side, 32:48, 0:64] = edge.T[0:16].astype(BF16)
        e_s[side, 32:48, 64:128] = jnp.zeros((16, 64), BF16)
    for end, r in enumerate((0, ROWS - 1)):
        row_s[end, 0:128, :] = pre_v[r]
        row_s[end, 128:192, :] = go_v[r // 2]
        row_s[end, 192:256, :] = in_v[r]

    pl.semaphore_wait(barrier, jnp.where(is_last, 0, 3) + 2 + 3 + 1 + (nq - 1) + (nz - 1))

    up = jnp.where(is_pole, 0, 2)

    def edge_copy(number, side, slot, device):
        return pltpu.make_async_remote_copy(
            src_ref=e_s.at[side], dst_ref=e_r.at[slot], send_sem=halo_send.at[number],
            recv_sem=halo_recv.at[slot], device_id=device, device_id_type=MESH,
        )

    def row_copy(number, end, slot, device, size=256):
        return pltpu.make_async_remote_copy(
            src_ref=row_s.at[end, pl.ds(0, size)], dst_ref=row_r.at[slot, pl.ds(0, size)], send_sem=halo_send.at[number],
            recv_sem=halo_recv.at[6 + slot], device_id=device, device_id_type=MESH,
        )

    turned = row_copy(0, 0, 0, at(0, lon + half), 192)
    above = row_copy(0, 0, 1, at(lat - 1, lon))
    always = [
        edge_copy(3, 1, up, at(top_lat, top_lon + 1)),
        edge_copy(4, 0, up + 3, at(top_lat, top_lon - 1)),
        edge_copy(1, 1, 1, at(lat, lon + 1)),
        edge_copy(2, 0, 4, at(lat, lon - 1)),
    ]
    down = [
        row_copy(5, 1, 0, at(lat + 1, lon)),
        edge_copy(6, 1, 0, at(lat + 1, lon + 1)),
        edge_copy(7, 0, 3, at(lat + 1, lon - 1)),
    ]
    for copy in always[:2]:
        copy.start()

    @pl.when(is_pole)
    def _():
        turned.start()

    @pl.when(jnp.logical_not(is_pole))
    def _():
        above.start()

    for copy in always[2:]:
        copy.start()

    @pl.when(jnp.logical_not(is_last))
    def _():
        for copy in down:
            copy.start()

    @pl.when(is_last)
    def _():
        e_r[2] = jnp.zeros((48, 128), BF16)
        e_r[5] = jnp.zeros((48, 128), BF16)
        row_r[1] = jnp.zeros((256, 128), BF16)

    loads[3].wait()
    loads[4].wait()
    for a in range(3):
        for b in range(3):
            t = w2_v[3 * a + b].astype(F32).T.astype(BF16)
            wa[0, 128 * a : 128 * a + 128, 128 * b : 128 * b + 128] = t
            u = w1_v[3 * a + b].astype(F32).T.astype(BF16)
            wb[0, 128 * a : 128 * a + 128, 64 * b : 64 * b + 64] = u
    wa[1] = wa[0]
    wb[1] = wb[0]

    @pl.when(is_pole)
    def _():
        wa[1, 256:384, :] = wa[0, 0:128, :]
        wb[1, 256:384, :] = wb[0, 0:128, :]

    def p1_copy(s):
        return pltpu.make_async_remote_copy(
            src_ref=p1s.at[s], dst_ref=p1r.at[s], send_sem=p1_send.at[s], recv_sem=p1_recv.at[s],
            device_id=chip(q, 1 - core), device_id_type=MESH,
        )

    def p1_start(s):
        p1s[s] = acc[s, pl.ds(pl.multiple_of((1 - core) * HALF, HALF), HALF), :].astype(BF16)
        p1_copy(s).start()

    def chunk_rows(p):
        return pl.ds(pl.multiple_of(p * chunk, 32), chunk)

    def p2_copy(s, p):
        return pltpu.make_async_remote_copy(
            src_ref=p2s.at[s, chunk_rows(p)], dst_ref=p2r.at[s, q], send_sem=p2_send.at[s],
            recv_sem=p2_recv.at[s], device_id=chip(p, core), device_id_type=MESH,
        )

    def p2_start(s):
        p1_copy(s).wait()
        own = pl.ds(pl.multiple_of(core * HALF, HALF), HALF)
        total = acc[s, own, :] + p1r[s].astype(F32)
        acc[s, own, :] = total
        p2s[s] = total.astype(BF16)
        for k in far_first(nq):
            p2_copy(s, lax.rem(q + k, nq)).start()

    def z_copy(s, k):
        return pltpu.make_async_remote_copy(
            src_ref=zb.at[s, z], dst_ref=zb.at[s, z], send_sem=z_send.at[s], recv_sem=z_recv.at[s],
            device_id=(lat, lax.rem(lon + 4 * k, nlon)), device_id_type=MESH,
        )

    def all_of(ref, sem):
        pltpu.make_async_copy(ref, ref, sem).wait()

    def z_start(s):
        total = acc[s, pl.ds(pl.multiple_of(core * HALF + q * chunk, 32), chunk), :]
        all_of(p2r.at[s, pl.ds(0, nq - 1)], p2_recv.at[s])
        for k in range(1, nq):
            total = total + p2r[s, lax.rem(q + nq - k, nq)].astype(F32)
        zb[s, z] = total.astype(BF16)
        for k in far_first(nz):
            z_copy(s, k).start()

    def p4_copy(s, p):
        mine = res.at[s, core, chunk_rows(q)]
        return pltpu.make_async_remote_copy(
            src_ref=mine, dst_ref=mine, send_sem=p4_send.at[s], recv_sem=p4_recv.at[s],
            device_id=chip(p, core), device_id_type=MESH,
        )

    def p4_start(s):
        all_of(zb.at[s, pl.ds(0, nz - 1)], z_recv.at[s])
        total = zb[s, 0].astype(F32)
        for k in range(1, nz):
            total = total + zb[s, k].astype(F32)
        res[s, core, chunk_rows(q), :] = total.astype(BF16)
        for k in far_first(nq):
            p4_copy(s, lax.rem(q + k, nq)).start()

    def p5_copy(s):
        rows = res.at[s, core]
        return pltpu.make_async_remote_copy(
            src_ref=rows, dst_ref=rows, send_sem=p5_send.at[s], recv_sem=p5_recv.at[s],
            device_id=chip(q, 1 - core), device_id_type=MESH,
        )

    def deliver(s, k):
        rows = pl.ds(pl.multiple_of(s * 2 * HALF + k * HALF, HALF), HALF)
        gw_o[rows, :] = res[s, k].astype(F32)

    def p5_start(s):
        all_of(res.at[s, core, pl.ds(0, HALF - chunk)], p4_recv.at[s])
        p5_copy(s).start()
        deliver(s, core)

    def p5_finish(s):
        p5_copy(s).wait_recv()
        deliver(s, 1 - core)

    def drain(s):
        all_of(p2s.at[s, pl.ds(0, HALF - chunk)], p2_send.at[s])
        all_of(zb.at[s, pl.ds(0, nz - 1)], z_send.at[s])
        all_of(res.at[s, core, pl.ds(0, HALF - chunk)], p4_send.at[s])

    @pl.loop(0, ROWS)
    def _(r):
        act, slope = gelu_parts(pre_v[r].astype(F32))
        act_f[r + 1, 0:128, :] = act
        slope_f[r + 1, 0:128, :] = slope

    copies = lax.broadcasted_iota(jnp.int32, (64, 128), 1) // 2
    copies = jnp.where(copies == lax.broadcasted_iota(jnp.int32, (64, 128), 0), 0.25, 0.0).astype(BF16)
    gpt[:, 0:256] = jnp.zeros((128, 256), BF16)
    gpt[:, 18 * 128 : 20 * 128] = jnp.zeros((128, 256), BF16)
    for i in range(ROWS // 2):
        t = lax.dot_general(
            go_v[i], copies, (((0,), (0,)), ((), ())), preferred_element_type=F32
        ).astype(BF16)
        gpt[:, (2 * i + 2) * 128 : (2 * i + 3) * 128] = t
        gpt[:, (2 * i + 3) * 128 : (2 * i + 4) * 128] = t

    def arrived(slot):
        dst = e_r.at[slot] if slot < 6 else row_r.at[slot - 6]
        pltpu.make_async_copy(dst, dst, halo_recv.at[slot]).wait()

    for slot in (1, 4):
        arrived(slot)

    @pl.when(jnp.logical_not(is_last))
    def _():
        for slot in (2, 5, 7):
            arrived(slot)

    keep = jnp.where(is_last, 0.0, 1.0).astype(F32)
    zero8 = jnp.zeros((8, 128), F32)
    for side in range(2):
        mid = e_r[3 * side + 1].astype(F32)
        low = e_r[3 * side + 2].astype(F32)
        hc[side, 8:24, :] = mid[0:16]
        hc[side, 24:32, :] = jnp.broadcast_to(low[0:1], (8, 128))
        act, slope = gelu_parts(hc[side, 8:32, :])
        hc[side, 8:32, :] = act
        hs[side, 8:32, :] = slope
        hg[side, 8:16, :] = 0.25 * mid[16:24]
        hg[side, 16:24, :] = 0.25 * jnp.broadcast_to(low[16:17], (8, 128))
        hi[side, 0:8, :] = zero8
        hi[side, 8:24, :] = mid[32:48]
        hi[side, 24:32, :] = jnp.broadcast_to(low[32:33], (8, 128))
    act, slope = gelu_parts(row_r[1, 0:128, :].astype(F32))
    act_f[17, 0:128, :] = act
    slope_f[17, 0:128, :] = slope * keep

    def sides(t):
        scale = keep if t == 17 else 1.0
        for side, place in enumerate((152, 128)):
            act_f[t, place : place + 8, :] = jnp.broadcast_to(hc[side, t + 7 : t + 8, :], (8, 128))
            slope_f[t, place : place + 8, :] = scale * jnp.broadcast_to(hs[side, t + 7 : t + 8, :], (8, 128))

    def pooled(i, part):
        pext[i, 0:64, :] = (0.25 * part.astype(F32)).astype(BF16)
        left = jnp.broadcast_to(hg[0, i + 7 : i + 8, :], (16, 128))
        right = jnp.broadcast_to(hg[1, i + 7 : i + 8, :], (16, 128))
        tile = jnp.where(sub == 0, right, jnp.where(sub == 15, left, 0.0))
        pext[i, 64:80, :] = tile.astype(BF16)

    def act_row(t):
        x = act_f[t]
        rows = pl.ds(pl.multiple_of(t * 128, 128), 128)
        act3[rows, 0:128] = pltpu.roll(x, 1, 0)[0:128].astype(BF16)
        act3[rows, 128:256] = x[0:128].astype(BF16)
        act3[rows, 256:384] = pltpu.roll(x, WIDE - 1, 0)[0:128].astype(BF16)

    for t in range(1, 18):
        sides(t)
    for i in range(1, 10):
        pooled(i, go_v[i - 1] if i < 9 else row_r[1, 128:192, :])

    @pl.loop(1, 18)
    def _(t):
        act_row(t)

    lhs = jnp.concatenate([gpt[:, (3 - a) * 128 : (3 - a) * 128 + 17 * 128] for a in range(3)], 0)
    terms = dot(lhs, act3[128:2304, :])
    both[...] = terms[0:128]
    for a in range(1, 3):
        for b in range(3):
            block = terms[128 * a : 128 * a + 128, 128 * b : 128 * b + 128]
            acc[0, (3 * a + b - 3) * 128 : (3 * a + b - 2) * 128, :] = block.T

    acc[0, 768:1024, :] = jnp.zeros((256, 128), F32)
    p1_start(0)

    def grad_rows(i, taps):
        here, after = pext[i], pext[i + 1]
        lhs = jnp.concatenate(
            [jnp.concatenate([after, here, here], 1), jnp.concatenate([after, after, here], 1)], 0
        )
        terms = dot(lhs, taps)
        for s in range(2):
            part = terms[PWIDE * s : PWIDE * (s + 1)]
            t0, t1, t2 = part[:, 0:128], part[:, 128:256], part[:, 256:384]
            ga_f[s, pl.ds(0, PWIDE, stride=2), :] = t0 + t1 + pltpu.roll(t2, 1, 0)
            ga_f[s, pl.ds(1, PWIDE, stride=2), :] = pltpu.roll(t0, PWIDE - 1, 0) + t1 + t2
            g_v[2 * i + s] = (ga_f[s] * slope_f[2 * i + s]).astype(BF16)

    @pl.loop(1, 9)
    def _(i):
        grad_rows(i, wa[0])

    p2_start(0)

    edges = [jnp.concatenate([hi[side], jnp.zeros((96, 128), F32)], 0).T[0:64] for side in range(2)]

    def in_row(t, x, left, right):
        cells = slice(128 * t, 128 * t + 128)
        in3[0:64, cells] = jnp.where(lane == 0, left, pltpu.roll(x, 1, 1)).astype(BF16)
        in3[64:128, cells] = x.astype(BF16)
        in3[128:192, cells] = jnp.where(lane == 127, right, pltpu.roll(x, 127, 1)).astype(BF16)

    for t in range(1, 18):
        x = (in_v[t - 1] if t < 17 else row_r[1, 192:256, :]).astype(F32)
        in_row(t, x, pltpu.roll(edges[0], 121 - t, 1), pltpu.roll(edges[1], 120 - t, 1))

    lhs = jnp.concatenate([in3[:, (a + 1) * 128 : (a + 16) * 128] for a in range(3)], 0)
    acc[1, 384:960, :] = dot(lhs, g_v[2:17, 0:128, :].reshape(1920, 128))
    acc[1, 960:1024, :] = jnp.zeros((64, 128), F32)

    @pl.when(is_pole)
    def _():
        dst = row_r.at[0, pl.ds(0, 192)]
        pltpu.make_async_copy(dst, dst, halo_recv.at[6]).wait()
        row_r[0, 192:256, :] = jnp.zeros((64, 128), BF16)

    @pl.when(jnp.logical_not(is_pole))
    def _():
        arrived(6)

    arrived(0)
    arrived(3)
    for side in range(2):
        top = e_r[3 * side].astype(F32)

        def pick(first, last):
            return jnp.broadcast_to(jnp.where(is_pole, top[first : first + 1], top[last : last + 1]), (8, 128))

        act, slope = gelu_parts(pick(0, 15))
        hc[side, 0:8, :] = act
        hs[side, 0:8, :] = slope
        hg[side, 0:8, :] = 0.25 * pick(16, 23)
        hi[side, 0:8, :] = jnp.where(is_pole, 0.0, pick(32, 47))
    act, slope = gelu_parts(row_r[0, 0:128, :].astype(F32))
    act_f[0, 0:128, :] = act
    slope_f[0, 0:128, :] = slope
    sides(0)
    pooled(0, row_r[0, 128:192, :])
    grad_rows(0, wa[1])

    act_row(0)
    top_go = lax.dot_general(
        row_r[0, 128:192, :], copies, (((0,), (0,)), ((), ())), preferred_element_type=F32
    ).astype(BF16)
    gpt_top[...] = jnp.where(is_pole, top_go.astype(F32), gpt[:, 256:384].astype(F32)).astype(BF16)

    @pl.when(is_pole)
    def _():
        act3[0:128, :] = act3[128:256, :]

    first_row = both[...] + dot(gpt_top[...], act3[0:128, :])
    for b in range(3):
        acc[1, b * 128 : (b + 1) * 128, :] = first_row[:, 128 * b : 128 * b + 128].T

    x = row_r[0, 192:256, :].astype(F32)
    edges = [jnp.concatenate([hi[side], jnp.zeros((96, 128), F32)], 0).T[0:64] for side in range(2)]
    in_row(0, x, pltpu.roll(edges[0], 121, 1), pltpu.roll(edges[1], 120, 1))
    here = jnp.concatenate([in3[:, 0:128], in3[:, 128:256], in3[:, 256:384]], 0)
    fold = jnp.where(is_pole, in3[:, 128:256].astype(F32), 0.0).astype(BF16)
    there = jnp.concatenate([fold, jnp.zeros((384, 128), BF16)], 0)
    acc[1, 384:960, :] += dot(jnp.concatenate([here, there], 1), jnp.concatenate([g_v[1, 0:128, :], g_v[0, 0:128, :]], 0))

    p1_start(1)

    def input_row(r):
        lhs = jnp.concatenate([g_v[r + 2], g_v[r + 1], g_v[r]], 1)
        terms = dot(lhs, wb[jnp.where(r == 0, 1, 0)])
        t01, t2 = terms[:, 0:128], terms[:, 128:192]
        first = lax.broadcasted_iota(jnp.int32, (128, 128), 1) < 64
        t01 = jnp.where(first, pltpu.roll(t01, WIDE - 1, 0)[0:128], t01[0:128]).T
        t2 = pltpu.roll(t2, 1, 0)[0:128].T
        gi_o[r] = (t01[0:64] + t01[64:128] + t2).astype(BF16)

    @pl.loop(0, ROWS // 2)
    def _(r):
        input_row(r)

    p2_start(1)

    @pl.loop(ROWS // 2, ROWS)
    def _(r):
        input_row(r)

    z_start(0)
    z_start(1)
    p4_start(0)
    p4_start(1)
    p5_start(0)

    @pl.when(is_pole)
    def _():
        turned.wait_send()

    @pl.when(jnp.logical_not(is_pole))
    def _():
        above.wait_send()

    for copy in always:
        copy.wait_send()

    @pl.when(jnp.logical_not(is_last))
    def _():
        for copy in down:
            copy.wait_send()

    drain(0)
    p5_finish(0)
    p5_start(1)
    drain(1)
    p5_finish(1)
    p5_copy(0).wait_send()
    p5_copy(1).wait_send()


def write_out(gi_v, gw_v, gi_o, gw1_o, gw2_o, sem):
    copies = [
        pltpu.make_async_copy(gw_v.at[pl.ds(0, 768)], gw2_o.at[pl.ds(384, 768)], sem.at[0]),
        pltpu.make_async_copy(gw_v.at[pl.ds(1024, 384)], gw2_o.at[pl.ds(0, 384)], sem.at[1]),
        pltpu.make_async_copy(gw_v.at[pl.ds(1408, 576)], gw1_o, sem.at[2]),
        pltpu.make_async_copy(gi_v, gi_o, sem.at[3]),
    ]
    for copy in copies:
        copy.start()
    for copy in copies:
        copy.wait()


def section(nlat, nlon, inputs, pre_first, grad_out, w_first, w_second):
    nq, nz = nlat * 2, nlon // 4
    chunk = HALF // nq
    hbm = pl.BlockSpec(memory_space=pltpu.HBM)
    vmem = pltpu.VMEM
    dma = pltpu.SemaphoreType.DMA
    gi, gw = pl.pallas_call(
        functools.partial(kernel, nlat, nlon),
        out_shape=(vmem((ROWS, C0, COLS), BF16), vmem((2048, 128), F32)),
        in_specs=[hbm] * 5,
        out_specs=(pl.BlockSpec(memory_space=vmem), pl.BlockSpec(memory_space=vmem)),
        scratch_shapes=[
            vmem((ROWS, COLS, C1), BF16),
            vmem((ROWS, C0, COLS), BF16),
            vmem((ROWS // 2, COLS // 2, C1), BF16),
            vmem((9, C0, C1), BF16),
            vmem((9, C1, C1), BF16),
            vmem((2, 384, 384), BF16),
            vmem((2, 384, 192), BF16),
            vmem((2, 48, 128), BF16),
            vmem((2, 256, 128), BF16),
            vmem((6, 48, 128), BF16),
            vmem((2, 256, 128), BF16),
            vmem((2, 32, 128), F32),
            vmem((2, 32, 128), F32),
            vmem((2, 24, 128), F32),
            vmem((2, 32, 128), F32),
            vmem((18, WIDE, 128), F32),
            vmem((18, WIDE, 128), F32),
            vmem((18 * 128, 384), BF16),
            vmem((10, PWIDE, 128), BF16),
            vmem((128, 20 * 128), BF16),
            vmem((128, 128), BF16),
            vmem((192, 18 * 128), BF16),
            vmem((18, WIDE, 128), BF16),
            vmem((2, WIDE, 128), F32),
            vmem((128, 384), F32),
            vmem((2, 2 * HALF, 128), F32),
            vmem((2, HALF, 128), BF16),
            vmem((2, HALF, 128), BF16),
            vmem((2, HALF, 128), BF16),
            vmem((2, nq, chunk, 128), BF16),
            vmem((2, nz, chunk, 128), BF16),
            vmem((2, 2, HALF, 128), BF16),
            dma((5,)),
            dma((8,)), dma((8,)),
            dma((2,)), dma((2,)),
            dma((2,)), dma((2,)),
            dma((2,)), dma((2,)),
            dma((2,)), dma((2,)),
            dma((2,)), dma((2,)),
        ],
        compiler_params=pltpu.CompilerParams(
            collective_id=0, has_side_effects=True, vmem_limit_bytes=40 * 1024 * 1024
        ),
        cost_estimate=pl.CostEstimate(flops=1_800_000_000, bytes_accessed=3_000_000, transcendentals=600_000),
    )(
        *(
            pltpu.with_memory_space_constraint(x, pltpu.HBM)
            for x in (
                pre_first,
                jnp.transpose(inputs, (0, 2, 1)),
                grad_out,
                w_first.reshape(9, C0, C1),
                w_second.reshape(9, C1, C1),
            )
        )
    )
    gi, grad_w_first, grad_w_second = pl.pallas_call(
        write_out,
        out_shape=(
            jax.ShapeDtypeStruct((ROWS, C0, COLS), BF16),
            jax.ShapeDtypeStruct((9 * C0, C1), F32),
            jax.ShapeDtypeStruct((9 * C1, C1), F32),
        ),
        in_specs=[pl.BlockSpec(memory_space=vmem)] * 2,
        out_specs=(pl.BlockSpec(memory_space=pl.ANY),) * 3,
        scratch_shapes=[dma((4,))],
        compiler_params=pltpu.CompilerParams(vmem_limit_bytes=16 * 1024 * 1024),
    )(gi, gw)
    return (
        jnp.transpose(gi, (0, 2, 1)),
        grad_w_first.reshape(3, 3, C0, C1),
        grad_w_second.reshape(3, 3, C1, C1),
    )


def solution(mesh):
    nlat, nlon = mesh.shape["lat"], mesh.shape["lon"]
    in_specs = (P("lat", "lon", None), P("lat", "lon", None), P("lat", "lon", None), P(), P())
    out_specs = (P("lat", "lon", None), P(), P())
    return jax.shard_map(
        functools.partial(section, nlat, nlon), mesh=mesh, in_specs=in_specs, out_specs=out_specs, check_vma=False
    )
```

```python
import functools

import jax
import jax.numpy as jnp
from jax import lax
from jax.experimental import pallas as pl
from jax.experimental.pallas import tpu as pltpu
from jax.sharding import PartitionSpec as P

INV_ROOT = 0.7071067811865476
DENSITY = 0.3989422804014327
BF16 = jnp.bfloat16
F32 = jnp.float32
MESH = pl.DeviceIdType.MESH

ROWS, COLS, C0, C1 = 16, 128, 64, 128
WIDE = COLS + 32
PWIDE = COLS // 2 + 16
HALF = 512


def far_first(n):
    return sorted(range(1, n), key=lambda k: (-min(k, n - k), k))


def gelu_parts(value):
    cdf = 0.5 * (1.0 + lax.erf(value * INV_ROOT))
    act = value * cdf
    slope = cdf + value * jnp.exp(-0.5 * value * value) * DENSITY
    return act, slope


def dot(a, b):
    return lax.dot_general(a, b, (((1,), (0,)), ((), ())), preferred_element_type=F32)


def kernel(
    nlat, nlon,
    pre_h, in_h, go_h, w1_h, w2_h,
    gi_o, gw_o,
    pre_v, in_v, go_v, w1_v, w2_v, wa, wb,
    e_s, row_s, e_r, row_r, hc, hs, hg, hi,
    slope_f, act3, pext, gpt, gpt_top, gpt_side, in3, g_v, ga_f, both,
    acc, p1s, p1r, p2s, p2r, zb, res,
    load_sem, halo_send, halo_recv, p1_send, p1_recv, p2_send, p2_recv,
    z_send, z_recv, p4_send, p4_recv, p5_send, p5_recv,
):
    lat, lon = lax.axis_index("lat"), lax.axis_index("lon")
    nq, nz = nlat * 2, nlon // 4
    chunk = HALF // nq
    z, yhi, core = lon // 4, (lon % 4) // 2, lon % 2
    q = lat * 2 + yhi
    is_pole = lat == 0
    is_last = lat == nlat - 1
    half = nlon // 2

    def chip(p, k):
        return (p // 2, z * 4 + (p % 2) * 2 + k)

    def at(dlat, dlon):
        return (dlat, lax.rem(dlon + 2 * nlon, nlon))

    loads = [
        pltpu.make_async_copy(src, dst, load_sem.at[i])
        for i, (src, dst) in enumerate(
            ((pre_h, pre_v), (in_h, in_v), (go_h, go_v), (w2_h, w2_v), (w1_h, w1_v))
        )
    ]
    for load in loads:
        load.start()

    barrier = pltpu.get_barrier_semaphore()

    def greet(device):
        pl.semaphore_signal(barrier, inc=1, device_id=device, device_id_type=MESH)

    top_lat = jnp.where(is_pole, 0, lat - 1)
    top_lon = jnp.where(is_pole, lon + half, lon)
    for d in (-1, 0, 1):
        greet(at(top_lat, top_lon + d))
    for k in far_first(nz):
        greet((lat, lax.rem(lon + 4 * k, nlon)))
    for k in far_first(nq):
        greet(chip(lax.rem(q + k, nq), core))
    for d in (-1, 1):
        greet(at(lat, lon + d))

    @pl.when(jnp.logical_not(is_last))
    def _():
        for d in (-1, 0, 1):
            greet(at(lat + 1, lon + d))

    greet(chip(q, 1 - core))

    loads[0].wait()
    loads[1].wait()
    loads[2].wait()
    lane = lax.broadcasted_iota(jnp.int32, (C0, 128), 1)
    sub = lax.broadcasted_iota(jnp.int32, (16, 128), 0)
    zero16 = jnp.zeros((16, 128), F32)
    for side, (col, first) in enumerate(((0, 0), (15, 112))):
        edge = zero16
        for r in range(ROWS):
            tile = pre_v[r, first : first + 16, :].astype(F32)
            edge = jnp.where(sub == r, jnp.broadcast_to(tile[col : col + 1], (16, 128)), edge)
        e_s[side, 0:16, :] = edge.astype(BF16)
        edge = zero16
        for r in range(ROWS // 2):
            tile = go_v[r, first // 112 * 48 : first // 112 * 48 + 16, :].astype(F32)
            edge = jnp.where(sub == r, jnp.broadcast_to(tile[col : col + 1], (16, 128)), edge)
        e_s[side, 16:32, :] = edge.astype(BF16)
        edge = jnp.zeros((C0, 128), F32)
        for r in range(ROWS):
            shift = r if side == 0 else r + 1
            edge = jnp.where(lane == r, pltpu.roll(in_v[r].astype(F32), shift, 1), edge)
        e_s[side, 32:48, 0:64] = edge.T[0:16].astype(BF16)
        e_s[side, 32:48, 64:128] = jnp.zeros((16, 64), BF16)
    for end, r in enumerate((0, ROWS - 1)):
        row_s[end, 0:128, :] = pre_v[r]
        row_s[end, 128:192, :] = go_v[r // 2]
        row_s[end, 192:256, :] = in_v[r]

    pl.semaphore_wait(barrier, jnp.where(is_last, 0, 3) + 2 + 3 + 1 + (nq - 1) + (nz - 1))

    up = jnp.where(is_pole, 0, 2)

    def edge_copy(number, side, slot, device):
        return pltpu.make_async_remote_copy(
            src_ref=e_s.at[side], dst_ref=e_r.at[slot], send_sem=halo_send.at[number],
            recv_sem=halo_recv.at[slot], device_id=device, device_id_type=MESH,
        )

    def row_copy(number, end, slot, device, size=256):
        return pltpu.make_async_remote_copy(
            src_ref=row_s.at[end, pl.ds(0, size)], dst_ref=row_r.at[slot, pl.ds(0, size)], send_sem=halo_send.at[number],
            recv_sem=halo_recv.at[6 + slot], device_id=device, device_id_type=MESH,
        )

    turned = row_copy(0, 0, 0, at(0, lon + half), 192)
    above = row_copy(0, 0, 1, at(lat - 1, lon))
    always = [
        edge_copy(3, 1, up, at(top_lat, top_lon + 1)),
        edge_copy(4, 0, up + 3, at(top_lat, top_lon - 1)),
        edge_copy(1, 1, 1, at(lat, lon + 1)),
        edge_copy(2, 0, 4, at(lat, lon - 1)),
    ]
    down = [
        row_copy(5, 1, 0, at(lat + 1, lon)),
        edge_copy(6, 1, 0, at(lat + 1, lon + 1)),
        edge_copy(7, 0, 3, at(lat + 1, lon - 1)),
    ]
    for copy in always[:2]:
        copy.start()

    @pl.when(is_pole)
    def _():
        turned.start()

    @pl.when(jnp.logical_not(is_pole))
    def _():
        above.start()

    for copy in always[2:]:
        copy.start()

    @pl.when(jnp.logical_not(is_last))
    def _():
        for copy in down:
            copy.start()

    @pl.when(is_last)
    def _():
        e_r[2] = jnp.zeros((48, 128), BF16)
        e_r[5] = jnp.zeros((48, 128), BF16)
        row_r[1] = jnp.zeros((256, 128), BF16)

    loads[3].wait()
    loads[4].wait()
    for a in range(3):
        for b in range(3):
            t = w2_v[3 * a + b].astype(F32).T.astype(BF16)
            wa[0, 128 * a : 128 * a + 128, 128 * b : 128 * b + 128] = t
            u = w1_v[3 * a + b].astype(F32).T.astype(BF16)
            wb[0, 128 * a : 128 * a + 128, 64 * b : 64 * b + 64] = u
    wa[1] = wa[0]
    wb[1] = wb[0]

    @pl.when(is_pole)
    def _():
        wa[1, 256:384, :] = wa[0, 0:128, :]
        wb[1, 256:384, :] = wb[0, 0:128, :]

    def p1_copy(s):
        return pltpu.make_async_remote_copy(
            src_ref=p1s.at[s], dst_ref=p1r.at[s], send_sem=p1_send.at[s], recv_sem=p1_recv.at[s],
            device_id=chip(q, 1 - core), device_id_type=MESH,
        )

    def p1_start(s):
        p1s[s] = acc[s, pl.ds(pl.multiple_of((1 - core) * HALF, HALF), HALF), :].astype(BF16)
        p1_copy(s).start()

    def chunk_rows(p):
        return pl.ds(pl.multiple_of(p * chunk, 32), chunk)

    def p2_copy(s, p):
        return pltpu.make_async_remote_copy(
            src_ref=p2s.at[s, chunk_rows(p)], dst_ref=p2r.at[s, q], send_sem=p2_send.at[s],
            recv_sem=p2_recv.at[s], device_id=chip(p, core), device_id_type=MESH,
        )

    def p2_start(s):
        p1_copy(s).wait()
        own = pl.ds(pl.multiple_of(core * HALF, HALF), HALF)
        total = acc[s, own, :] + p1r[s].astype(F32)
        acc[s, own, :] = total
        p2s[s] = total.astype(BF16)
        for k in far_first(nq):
            p2_copy(s, lax.rem(q + k, nq)).start()

    def z_copy(s, k):
        return pltpu.make_async_remote_copy(
            src_ref=zb.at[s, z], dst_ref=zb.at[s, z], send_sem=z_send.at[s], recv_sem=z_recv.at[s],
            device_id=(lat, lax.rem(lon + 4 * k, nlon)), device_id_type=MESH,
        )

    def all_of(ref, sem):
        pltpu.make_async_copy(ref, ref, sem).wait()

    def z_start(s):
        total = acc[s, pl.ds(pl.multiple_of(core * HALF + q * chunk, 32), chunk), :]
        all_of(p2r.at[s, pl.ds(0, nq - 1)], p2_recv.at[s])
        for k in range(1, nq):
            total = total + p2r[s, lax.rem(q + nq - k, nq)].astype(F32)
        zb[s, z] = total.astype(BF16)
        for k in far_first(nz):
            z_copy(s, k).start()

    def p4_copy(s, p):
        mine = res.at[s, core, chunk_rows(q)]
        return pltpu.make_async_remote_copy(
            src_ref=mine, dst_ref=mine, send_sem=p4_send.at[s], recv_sem=p4_recv.at[s],
            device_id=chip(p, core), device_id_type=MESH,
        )

    def p4_start(s):
        all_of(zb.at[s, pl.ds(0, nz - 1)], z_recv.at[s])
        total = zb[s, 0].astype(F32)
        for k in range(1, nz):
            total = total + zb[s, k].astype(F32)
        res[s, core, chunk_rows(q), :] = total.astype(BF16)
        for k in far_first(nq):
            p4_copy(s, lax.rem(q + k, nq)).start()

    def p5_copy(s):
        rows = res.at[s, core]
        return pltpu.make_async_remote_copy(
            src_ref=rows, dst_ref=rows, send_sem=p5_send.at[s], recv_sem=p5_recv.at[s],
            device_id=chip(q, 1 - core), device_id_type=MESH,
        )

    def deliver(s, k):
        rows = pl.ds(pl.multiple_of(s * 2 * HALF + k * HALF, HALF), HALF)
        gw_o[rows, :] = res[s, k].astype(F32)

    def p5_start(s):
        all_of(res.at[s, core, pl.ds(0, HALF - chunk)], p4_recv.at[s])
        p5_copy(s).start()
        deliver(s, core)

    def p5_finish(s):
        p5_copy(s).wait_recv()
        deliver(s, 1 - core)

    def drain(s):
        all_of(p2s.at[s, pl.ds(0, HALF - chunk)], p2_send.at[s])
        all_of(zb.at[s, pl.ds(0, nz - 1)], z_send.at[s])
        all_of(res.at[s, core, pl.ds(0, HALF - chunk)], p4_send.at[s])

    column = lax.broadcasted_iota(jnp.int32, (128, 128), 0)

    def act_row(t, x, left, right):
        rows = pl.ds(pl.multiple_of(t * 128, 128), 128)
        act3[rows, 0:128] = jnp.where(column == 0, left, pltpu.roll(x, 1, 0)).astype(BF16)
        act3[rows, 128:256] = x.astype(BF16)
        act3[rows, 256:384] = jnp.where(column == 127, right, pltpu.roll(x, 127, 0)).astype(BF16)

    @pl.loop(0, ROWS, unroll=2)
    def _(r):
        act, slope = gelu_parts(pre_v[r].astype(F32))
        act_row(r + 1, act, 0.0, 0.0)
        slope_f[r + 1, 0:128, :] = slope

    copies = lax.broadcasted_iota(jnp.int32, (64, 128), 1) // 2
    copies = jnp.where(copies == lax.broadcasted_iota(jnp.int32, (64, 128), 0), 0.25, 0.0).astype(BF16)
    gpt[:, 0:256] = jnp.zeros((128, 256), BF16)
    gpt[:, 18 * 128 : 20 * 128] = jnp.zeros((128, 256), BF16)
    for i in range(ROWS // 2):
        t = lax.dot_general(
            go_v[i], copies, (((0,), (0,)), ((), ())), preferred_element_type=F32
        ).astype(BF16)
        gpt[:, (2 * i + 2) * 128 : (2 * i + 3) * 128] = t
        gpt[:, (2 * i + 3) * 128 : (2 * i + 4) * 128] = t

    corner = jnp.concatenate([e_s[0, 16:32, :], e_s[1, 16:32, :]], 0)
    place = lax.broadcasted_iota(jnp.int32, (32, 128), 1)
    source = lax.broadcasted_iota(jnp.int32, (32, 128), 0)
    for a in range(3):
        row = place % 32 - 7 - a
        chosen = jnp.logical_and(
            jnp.logical_and(row >= 0, row < ROWS), place // 32 * 16 + (row + 16) // 2 - 8 == source
        )
        chosen = jnp.where(chosen, 0.25, 0.0).astype(BF16)
        gpt_side[128 * a : 128 * a + 128, :] = lax.dot_general(
            corner, chosen, (((0,), (0,)), ((), ())), preferred_element_type=F32
        ).astype(BF16)

    lhs = jnp.concatenate([gpt[:, (3 - a) * 128 : (3 - a) * 128 + 2048] for a in range(3)], 0)
    both[...] = dot(lhs, act3[128 : 17 * 128, :])

    def grad_rows(i, taps):
        here, after = pext[i], pext[i + 1]
        lhs = jnp.concatenate(
            [jnp.concatenate([after, here, here], 1), jnp.concatenate([after, after, here], 1)], 0
        )
        terms = dot(lhs, taps)
        for s in range(2):
            part = terms[PWIDE * s : PWIDE * (s + 1)]
            t0, t1, t2 = part[:, 0:128], part[:, 128:256], part[:, 256:384]
            ga_f[2 * i + s, pl.ds(0, PWIDE, stride=2), :] = t0 + t1 + pltpu.roll(t2, 1, 0)
            ga_f[2 * i + s, pl.ds(1, PWIDE, stride=2), :] = pltpu.roll(t0, PWIDE - 1, 0) + t1 + t2
            g_v[2 * i + s] = (ga_f[2 * i + s] * slope_f[2 * i + s]).astype(BF16)

    for i in range(1, 9):
        pext[i, 0:64, :] = (0.25 * go_v[i - 1].astype(F32)).astype(BF16)
        pext[i, 64:80, :] = jnp.zeros((16, 128), BF16)

    @pl.loop(1, 8, unroll=7)
    def _(i):
        grad_rows(i, wa[0])

    def arrived(slot):
        dst = e_r.at[slot] if slot < 6 else row_r.at[slot - 6]
        pltpu.make_async_copy(dst, dst, halo_recv.at[slot]).wait()

    for slot in (1, 4):
        arrived(slot)

    @pl.when(jnp.logical_not(is_last))
    def _():
        for slot in (2, 5, 7):
            arrived(slot)

    keep = jnp.where(is_last, 0.0, 1.0).astype(F32)
    zero8 = jnp.zeros((8, 128), F32)
    for side in range(2):
        mid = e_r[3 * side + 1].astype(F32)
        low = e_r[3 * side + 2].astype(F32)
        hc[side, 8:24, :] = mid[0:16]
        hc[side, 24:32, :] = jnp.broadcast_to(low[0:1], (8, 128))
        act, slope = gelu_parts(hc[side, 8:32, :])
        hc[side, 8:32, :] = act
        hs[side, 8:32, :] = slope
        hg[side, 8:16, :] = 0.25 * mid[16:24]
        hg[side, 16:24, :] = 0.25 * jnp.broadcast_to(low[16:17], (8, 128))
        hi[side, 0:8, :] = zero8
        hi[side, 8:24, :] = mid[32:48]
        hi[side, 24:32, :] = jnp.broadcast_to(low[32:33], (8, 128))
    act, slope = gelu_parts(row_r[1, 0:128, :].astype(F32))
    act_row(17, act, 0.0, 0.0)
    slope_f[17, 0:128, :] = slope * keep

    def sides(t):
        scale = keep if t == 17 else 1.0
        for side, place in enumerate((152, 128)):
            slope_f[t, place : place + 8, :] = scale * jnp.broadcast_to(hs[side, t + 7 : t + 8, :], (8, 128))

    def pooled(i):
        left = jnp.broadcast_to(hg[0, i + 7 : i + 8, :], (16, 128))
        right = jnp.broadcast_to(hg[1, i + 7 : i + 8, :], (16, 128))
        tile = jnp.where(sub == 0, right, jnp.where(sub == 15, left, 0.0))
        pext[i, 64:80, :] = tile.astype(BF16)

    below = jnp.logical_and(
        lax.broadcasted_iota(jnp.int32, (32, 128), 0) >= 8, lax.broadcasted_iota(jnp.int32, (32, 128), 0) < 25
    )
    act3[2304:2432, :] = jnp.zeros((128, 384), BF16)
    act3[2304:2336, 0:128] = jnp.where(below, hc[0], 0.0).astype(BF16)
    act3[2336:2368, 256:384] = jnp.where(below, hc[1], 0.0).astype(BF16)
    lhs = jnp.concatenate(
        [jnp.concatenate([gpt[:, (19 - a) * 128 : (20 - a) * 128] for a in range(3)], 0), gpt_side[...]], 1
    )
    terms = both[...] + dot(lhs, act3[2176:2432, :])
    for a in range(1, 3):
        for b in range(3):
            block = terms[128 * a : 128 * a + 128, 128 * b : 128 * b + 128]
            acc[0, (3 * a + b - 3) * 128 : (3 * a + b - 2) * 128, :] = block.T
    both[0:128, :] = terms[0:128]
    acc[0, 768:1024, :] = jnp.zeros((256, 128), F32)
    p1_start(0)

    for t in range(1, 18):
        sides(t)
    pext[9, 0:64, :] = (0.25 * row_r[1, 128:192, :].astype(F32)).astype(BF16)
    for i in range(1, 10):
        pooled(i)
    tiles = [pext[i, 64:80, :] for i in range(1, 9)]
    lhs = jnp.concatenate(
        [
            jnp.concatenate([tiles[(t + 2) // 2 - 1], tiles[(t + 1) // 2 - 1], tiles[t // 2 - 1]], 1)
            for t in range(2, 16)
        ],
        0,
    )
    terms = dot(lhs, wa[0])
    for t in range(2, 16):
        part = terms[16 * (t - 2) : 16 * (t - 1)]
        t0, t1, t2 = part[:, 0:128], part[:, 128:256], part[:, 256:384]
        for first, at_row, more in ((0, 0, t2[15:16]), (112, 15, t0[0:1]), (128, 0, (t0 + t1)[0:1]), (144, 15, (t1 + t2)[15:16])):
            more = jnp.where(sub == at_row, jnp.broadcast_to(more, (16, 128)), 0.0)
            cells = slice(first, first + 16)
            g_v[t, cells, :] = ((ga_f[t, cells, :] + more) * slope_f[t, cells, :]).astype(BF16)
    grad_rows(8, wa[0])

    p2_start(0)

    edges = [jnp.concatenate([hi[side], jnp.zeros((96, 128), F32)], 0).T[0:64] for side in range(2)]

    def in_row(t, x, left, right):
        cells = slice(128 * t, 128 * t + 128)
        in3[0:64, cells] = jnp.where(lane == 0, left, pltpu.roll(x, 1, 1)).astype(BF16)
        in3[64:128, cells] = x.astype(BF16)
        in3[128:192, cells] = jnp.where(lane == 127, right, pltpu.roll(x, 127, 1)).astype(BF16)

    for t in range(1, 18):
        x = (in_v[t - 1] if t < 17 else row_r[1, 192:256, :]).astype(F32)
        in_row(t, x, pltpu.roll(edges[0], 121 - t, 1), pltpu.roll(edges[1], 120 - t, 1))

    lhs = jnp.concatenate([in3[:, (a + 1) * 128 : (a + 16) * 128] for a in range(3)], 0)
    acc[1, 384:960, :] = dot(lhs, g_v[2:17, 0:128, :].reshape(1920, 128))
    acc[1, 960:1024, :] = jnp.zeros((64, 128), F32)

    @pl.when(is_pole)
    def _():
        dst = row_r.at[0, pl.ds(0, 192)]
        pltpu.make_async_copy(dst, dst, halo_recv.at[6]).wait()
        row_r[0, 192:256, :] = jnp.zeros((64, 128), BF16)

    @pl.when(jnp.logical_not(is_pole))
    def _():
        arrived(6)

    arrived(0)
    arrived(3)
    for side in range(2):
        top = e_r[3 * side].astype(F32)

        def pick(first, last):
            return jnp.broadcast_to(jnp.where(is_pole, top[first : first + 1], top[last : last + 1]), (8, 128))

        act, slope = gelu_parts(pick(0, 15))
        hc[side, 0:8, :] = act
        hs[side, 0:8, :] = slope
        hg[side, 0:8, :] = 0.25 * pick(16, 23)
        hi[side, 0:8, :] = jnp.where(is_pole, 0.0, pick(32, 47))
    act, slope = gelu_parts(row_r[0, 0:128, :].astype(F32))
    slope_f[0, 0:128, :] = slope
    sides(0)
    pext[0, 0:64, :] = (0.25 * row_r[0, 128:192, :].astype(F32)).astype(BF16)
    pooled(0)
    grad_rows(0, wa[1])

    act_row(0, act, jnp.broadcast_to(hc[0, 7:8, :], (128, 128)), jnp.broadcast_to(hc[1, 7:8, :], (128, 128)))
    top_go = lax.dot_general(
        row_r[0, 128:192, :], copies, (((0,), (0,)), ((), ())), preferred_element_type=F32
    ).astype(BF16)
    gpt_top[...] = jnp.where(is_pole, top_go.astype(F32), gpt[:, 256:384].astype(F32)).astype(BF16)

    @pl.when(is_pole)
    def _():
        act_row(
            0,
            act3[128:256, 128:256].astype(F32),
            jnp.broadcast_to(hc[0, 8:9, :], (128, 128)),
            jnp.broadcast_to(hc[1, 8:9, :], (128, 128)),
        )

    first_row = both[0:128, :] + dot(gpt_top[...], act3[0:128, :])
    for b in range(3):
        acc[1, b * 128 : (b + 1) * 128, :] = first_row[:, 128 * b : 128 * b + 128].T

    x = row_r[0, 192:256, :].astype(F32)
    edges = [jnp.concatenate([hi[side], jnp.zeros((96, 128), F32)], 0).T[0:64] for side in range(2)]
    in_row(0, x, pltpu.roll(edges[0], 121, 1), pltpu.roll(edges[1], 120, 1))
    here = jnp.concatenate([in3[:, 0:128], in3[:, 128:256], in3[:, 256:384]], 0)
    fold = jnp.where(is_pole, in3[:, 128:256].astype(F32), 0.0).astype(BF16)
    there = jnp.concatenate([fold, jnp.zeros((384, 128), BF16)], 0)
    acc[1, 384:960, :] += dot(jnp.concatenate([here, there], 1), jnp.concatenate([g_v[1, 0:128, :], g_v[0, 0:128, :]], 0))

    p1_start(1)

    def input_row(r):
        lhs = jnp.concatenate([g_v[r + 2], g_v[r + 1], g_v[r]], 1)
        terms = dot(lhs, wb[jnp.where(r == 0, 1, 0)])
        t01, t2 = terms[:, 0:128], terms[:, 128:192]
        first = lax.broadcasted_iota(jnp.int32, (128, 128), 1) < 64
        t01 = jnp.where(first, pltpu.roll(t01, WIDE - 1, 0)[0:128], t01[0:128]).T
        t2 = pltpu.roll(t2, 1, 0)[0:128].T
        gi_o[r] = (t01[0:64] + t01[64:128] + t2).astype(BF16)

    @pl.loop(0, ROWS // 2, unroll=2)
    def _(r):
        input_row(r)

    p2_start(1)

    @pl.loop(ROWS // 2, ROWS, unroll=2)
    def _(r):
        input_row(r)

    z_start(0)
    z_start(1)
    p4_start(0)
    p4_start(1)
    p5_start(0)

    @pl.when(is_pole)
    def _():
        turned.wait_send()

    @pl.when(jnp.logical_not(is_pole))
    def _():
        above.wait_send()

    for copy in always:
        copy.wait_send()

    @pl.when(jnp.logical_not(is_last))
    def _():
        for copy in down:
            copy.wait_send()

    drain(0)
    p5_finish(0)
    p5_start(1)
    drain(1)
    p5_finish(1)
    p5_copy(0).wait_send()
    p5_copy(1).wait_send()


def write_out(gi_v, gw_v, gi_o, gw1_o, gw2_o, sem):
    copies = [
        pltpu.make_async_copy(gw_v.at[pl.ds(0, 768)], gw2_o.at[pl.ds(384, 768)], sem.at[0]),
        pltpu.make_async_copy(gw_v.at[pl.ds(1024, 384)], gw2_o.at[pl.ds(0, 384)], sem.at[1]),
        pltpu.make_async_copy(gw_v.at[pl.ds(1408, 576)], gw1_o, sem.at[2]),
        pltpu.make_async_copy(gi_v, gi_o, sem.at[3]),
    ]
    for copy in copies:
        copy.start()
    for copy in copies:
        copy.wait()


def section(nlat, nlon, inputs, pre_first, grad_out, w_first, w_second):
    nq, nz = nlat * 2, nlon // 4
    chunk = HALF // nq
    hbm = pl.BlockSpec(memory_space=pltpu.HBM)
    vmem = pltpu.VMEM
    dma = pltpu.SemaphoreType.DMA
    gi, gw = pl.pallas_call(
        functools.partial(kernel, nlat, nlon),
        out_shape=(vmem((ROWS, C0, COLS), BF16), vmem((2048, 128), F32)),
        in_specs=[hbm] * 5,
        out_specs=(pl.BlockSpec(memory_space=vmem), pl.BlockSpec(memory_space=vmem)),
        scratch_shapes=[
            vmem((ROWS, COLS, C1), BF16),
            vmem((ROWS, C0, COLS), BF16),
            vmem((ROWS // 2, COLS // 2, C1), BF16),
            vmem((9, C0, C1), BF16),
            vmem((9, C1, C1), BF16),
            vmem((2, 384, 384), BF16),
            vmem((2, 384, 192), BF16),
            vmem((2, 48, 128), BF16),
            vmem((2, 256, 128), BF16),
            vmem((6, 48, 128), BF16),
            vmem((2, 256, 128), BF16),
            vmem((2, 32, 128), F32),
            vmem((2, 32, 128), F32),
            vmem((2, 24, 128), F32),
            vmem((2, 32, 128), F32),
            vmem((18, WIDE, 128), F32),
            vmem((19 * 128, 384), BF16),
            vmem((10, PWIDE, 128), BF16),
            vmem((128, 20 * 128), BF16),
            vmem((128, 128), BF16),
            vmem((384, 128), BF16),
            vmem((192, 18 * 128), BF16),
            vmem((18, WIDE, 128), BF16),
            vmem((18, WIDE, 128), F32),
            vmem((384, 384), F32),
            vmem((2, 2 * HALF, 128), F32),
            vmem((2, HALF, 128), BF16),
            vmem((2, HALF, 128), BF16),
            vmem((2, HALF, 128), BF16),
            vmem((2, nq, chunk, 128), BF16),
            vmem((2, nz, chunk, 128), BF16),
            vmem((2, 2, HALF, 128), BF16),
            dma((5,)),
            dma((8,)), dma((8,)),
            dma((2,)), dma((2,)),
            dma((2,)), dma((2,)),
            dma((2,)), dma((2,)),
            dma((2,)), dma((2,)),
            dma((2,)), dma((2,)),
        ],
        compiler_params=pltpu.CompilerParams(
            collective_id=0, has_side_effects=True, vmem_limit_bytes=40 * 1024 * 1024
        ),
        cost_estimate=pl.CostEstimate(flops=1_800_000_000, bytes_accessed=3_000_000, transcendentals=600_000),
    )(
        *(
            pltpu.with_memory_space_constraint(x, pltpu.HBM)
            for x in (
                pre_first,
                jnp.transpose(inputs, (0, 2, 1)),
                grad_out,
                w_first.reshape(9, C0, C1),
                w_second.reshape(9, C1, C1),
            )
        )
    )
    gi, grad_w_first, grad_w_second = pl.pallas_call(
        write_out,
        out_shape=(
            jax.ShapeDtypeStruct((ROWS, C0, COLS), BF16),
            jax.ShapeDtypeStruct((9 * C0, C1), F32),
            jax.ShapeDtypeStruct((9 * C1, C1), F32),
        ),
        in_specs=[pl.BlockSpec(memory_space=vmem)] * 2,
        out_specs=(pl.BlockSpec(memory_space=pl.ANY),) * 3,
        scratch_shapes=[dma((4,))],
        compiler_params=pltpu.CompilerParams(vmem_limit_bytes=16 * 1024 * 1024),
    )(gi, gw)
    return (
        jnp.transpose(gi, (0, 2, 1)),
        grad_w_first.reshape(3, 3, C0, C1),
        grad_w_second.reshape(3, 3, C1, C1),
    )


def solution(mesh):
    nlat, nlon = mesh.shape["lat"], mesh.shape["lon"]
    in_specs = (P("lat", "lon", None), P("lat", "lon", None), P("lat", "lon", None), P(), P())
    out_specs = (P("lat", "lon", None), P(), P())
    return jax.shard_map(
        functools.partial(section, nlat, nlon), mesh=mesh, in_specs=in_specs, out_specs=out_specs, check_vma=False
    )
```

```python
import functools

import jax
import jax.numpy as jnp
from jax import lax
from jax.experimental import pallas as pl
from jax.experimental.pallas import tpu as pltpu
from jax.sharding import PartitionSpec as P

INV_ROOT = 0.7071067811865476
DENSITY = 0.3989422804014327
BF16 = jnp.bfloat16
F32 = jnp.float32
MESH = pl.DeviceIdType.MESH

ROWS, COLS, C0, C1 = 16, 128, 64, 128
WIDE = COLS + 32
PWIDE = COLS // 2 + 16
HALF = 512


def far_first(n):
    return sorted(range(1, n), key=lambda k: (-min(k, n - k), k))


def gelu_parts(value):
    cdf = 0.5 * (1.0 + lax.erf(value * INV_ROOT))
    act = value * cdf
    slope = cdf + value * jnp.exp(-0.5 * value * value) * DENSITY
    return act, slope


def dot(a, b):
    return lax.dot_general(a, b, (((1,), (0,)), ((), ())), preferred_element_type=F32)


def kernel(
    nlat, nlon,
    pre_h, in_h, go_h, w1_h, w2_h,
    gi_o, gw_o,
    pre_v, in_v, go_v, w1_v, w2_v, wa, wb,
    e_s, row_s, e_r, row_r, hc, hs, hg, hi,
    slope_f, act3, pext, gpt, gpt_top, gpt_side, in3, in_edge, g_edge, g_v, ga_f, both,
    acc, p1s, p1r, p2s, p2r, zb, res,
    load_sem, halo_send, halo_recv, p1_send, p1_recv, p2_send, p2_recv,
    z_send, z_recv, p4_send, p4_recv, p5_send, p5_recv,
):
    lat, lon = lax.axis_index("lat"), lax.axis_index("lon")
    nq, nz = nlat * 2, nlon // 4
    chunk = HALF // nq
    z, yhi, core = lon // 4, (lon % 4) // 2, lon % 2
    q = lat * 2 + yhi
    is_pole = lat == 0
    is_last = lat == nlat - 1
    half = nlon // 2

    def chip(p, k):
        return (p // 2, z * 4 + (p % 2) * 2 + k)

    def at(dlat, dlon):
        return (dlat, lax.rem(dlon + 2 * nlon, nlon))

    loads = [
        pltpu.make_async_copy(src, dst, load_sem.at[i])
        for i, (src, dst) in enumerate(
            ((pre_h, pre_v), (in_h, in_v), (go_h, go_v), (w2_h, w2_v), (w1_h, w1_v))
        )
    ]
    for load in loads:
        load.start()

    barrier = pltpu.get_barrier_semaphore()

    def greet(device):
        pl.semaphore_signal(barrier, inc=1, device_id=device, device_id_type=MESH)

    top_lat = jnp.where(is_pole, 0, lat - 1)
    top_lon = jnp.where(is_pole, lon + half, lon)
    for d in (-1, 0, 1):
        greet(at(top_lat, top_lon + d))
    for k in far_first(nz):
        greet((lat, lax.rem(lon + 4 * k, nlon)))
    for k in far_first(nq):
        greet(chip(lax.rem(q + k, nq), core))
    for d in (-1, 1):
        greet(at(lat, lon + d))

    @pl.when(jnp.logical_not(is_last))
    def _():
        for d in (-1, 0, 1):
            greet(at(lat + 1, lon + d))

    greet(chip(q, 1 - core))

    loads[0].wait()
    loads[1].wait()
    loads[2].wait()
    lane = lax.broadcasted_iota(jnp.int32, (C0, 128), 1)
    sub = lax.broadcasted_iota(jnp.int32, (16, 128), 0)
    zero16 = jnp.zeros((16, 128), F32)
    for side, (col, first) in enumerate(((0, 0), (15, 112))):
        edge = zero16
        for r in range(ROWS):
            tile = pre_v[r, first : first + 16, :].astype(F32)
            edge = jnp.where(sub == r, jnp.broadcast_to(tile[col : col + 1], (16, 128)), edge)
        e_s[side, 0:16, :] = edge.astype(BF16)
        edge = zero16
        for r in range(ROWS // 2):
            tile = go_v[r, first // 112 * 48 : first // 112 * 48 + 16, :].astype(F32)
            edge = jnp.where(sub == r, jnp.broadcast_to(tile[col : col + 1], (16, 128)), edge)
        e_s[side, 16:32, :] = edge.astype(BF16)
        edge = jnp.zeros((C0, 128), F32)
        for r in range(ROWS):
            shift = r if side == 0 else r + 1
            edge = jnp.where(lane == r, pltpu.roll(in_v[r].astype(F32), shift, 1), edge)
        e_s[side, 32:48, 0:64] = edge.T[0:16].astype(BF16)
        e_s[side, 32:48, 64:128] = jnp.zeros((16, 64), BF16)
    for end, r in enumerate((0, ROWS - 1)):
        row_s[end, 0:128, :] = pre_v[r]
        row_s[end, 128:192, :] = go_v[r // 2]
        row_s[end, 192:256, :] = in_v[r]

    pl.semaphore_wait(barrier, jnp.where(is_last, 0, 3) + 2 + 3 + 1 + (nq - 1) + (nz - 1))

    up = jnp.where(is_pole, 0, 2)

    def edge_copy(number, side, slot, device):
        return pltpu.make_async_remote_copy(
            src_ref=e_s.at[side], dst_ref=e_r.at[slot], send_sem=halo_send.at[number],
            recv_sem=halo_recv.at[slot], device_id=device, device_id_type=MESH,
        )

    def row_copy(number, end, slot, device, size=256):
        return pltpu.make_async_remote_copy(
            src_ref=row_s.at[end, pl.ds(0, size)], dst_ref=row_r.at[slot, pl.ds(0, size)], send_sem=halo_send.at[number],
            recv_sem=halo_recv.at[6 + slot], device_id=device, device_id_type=MESH,
        )

    turned = row_copy(0, 0, 0, at(0, lon + half), 192)
    above = row_copy(0, 0, 1, at(lat - 1, lon))
    always = [
        edge_copy(3, 1, up, at(top_lat, top_lon + 1)),
        edge_copy(4, 0, up + 3, at(top_lat, top_lon - 1)),
        edge_copy(1, 1, 1, at(lat, lon + 1)),
        edge_copy(2, 0, 4, at(lat, lon - 1)),
    ]
    down = [
        row_copy(5, 1, 0, at(lat + 1, lon)),
        edge_copy(6, 1, 0, at(lat + 1, lon + 1)),
        edge_copy(7, 0, 3, at(lat + 1, lon - 1)),
    ]
    for copy in always[:2]:
        copy.start()

    @pl.when(is_pole)
    def _():
        turned.start()

    @pl.when(jnp.logical_not(is_pole))
    def _():
        above.start()

    for copy in always[2:]:
        copy.start()

    @pl.when(jnp.logical_not(is_last))
    def _():
        for copy in down:
            copy.start()

    @pl.when(is_last)
    def _():
        e_r[2] = jnp.zeros((48, 128), BF16)
        e_r[5] = jnp.zeros((48, 128), BF16)
        row_r[1] = jnp.zeros((256, 128), BF16)

    loads[3].wait()
    loads[4].wait()
    for a in range(3):
        for b in range(3):
            t = w2_v[3 * a + b].astype(F32).T.astype(BF16)
            wa[0, 128 * a : 128 * a + 128, 128 * b : 128 * b + 128] = t
            u = w1_v[3 * a + b].astype(F32).T.astype(BF16)
            wb[0, 128 * a : 128 * a + 128, 64 * b : 64 * b + 64] = u
    wa[1] = wa[0]
    wb[1] = wb[0]

    @pl.when(is_pole)
    def _():
        wa[1, 256:384, :] = wa[0, 0:128, :]
        wb[1, 256:384, :] = wb[0, 0:128, :]

    def p1_copy(s):
        return pltpu.make_async_remote_copy(
            src_ref=p1s.at[s], dst_ref=p1r.at[s], send_sem=p1_send.at[s], recv_sem=p1_recv.at[s],
            device_id=chip(q, 1 - core), device_id_type=MESH,
        )

    def p1_start(s):
        p1s[s] = acc[s, pl.ds(pl.multiple_of((1 - core) * HALF, HALF), HALF), :].astype(BF16)
        p1_copy(s).start()

    def chunk_rows(p):
        return pl.ds(pl.multiple_of(p * chunk, 32), chunk)

    def p2_copy(s, p):
        return pltpu.make_async_remote_copy(
            src_ref=p2s.at[s, chunk_rows(p)], dst_ref=p2r.at[s, q], send_sem=p2_send.at[s],
            recv_sem=p2_recv.at[s], device_id=chip(p, core), device_id_type=MESH,
        )

    def p2_start(s):
        p1_copy(s).wait()
        own = pl.ds(pl.multiple_of(core * HALF, HALF), HALF)
        total = acc[s, own, :] + p1r[s].astype(F32)
        acc[s, own, :] = total
        p2s[s] = total.astype(BF16)
        for k in far_first(nq):
            p2_copy(s, lax.rem(q + k, nq)).start()

    def z_copy(s, k):
        return pltpu.make_async_remote_copy(
            src_ref=zb.at[s, z], dst_ref=zb.at[s, z], send_sem=z_send.at[s], recv_sem=z_recv.at[s],
            device_id=(lat, lax.rem(lon + 4 * k, nlon)), device_id_type=MESH,
        )

    def all_of(ref, sem):
        pltpu.make_async_copy(ref, ref, sem).wait()

    def z_start(s):
        total = acc[s, pl.ds(pl.multiple_of(core * HALF + q * chunk, 32), chunk), :]
        all_of(p2r.at[s, pl.ds(0, nq - 1)], p2_recv.at[s])
        for k in range(1, nq):
            total = total + p2r[s, lax.rem(q + nq - k, nq)].astype(F32)
        zb[s, z] = total.astype(BF16)
        for k in far_first(nz):
            z_copy(s, k).start()

    def p4_copy(s, p):
        mine = res.at[s, core, chunk_rows(q)]
        return pltpu.make_async_remote_copy(
            src_ref=mine, dst_ref=mine, send_sem=p4_send.at[s], recv_sem=p4_recv.at[s],
            device_id=chip(p, core), device_id_type=MESH,
        )

    def p4_start(s):
        all_of(zb.at[s, pl.ds(0, nz - 1)], z_recv.at[s])
        total = zb[s, 0].astype(F32)
        for k in range(1, nz):
            total = total + zb[s, k].astype(F32)
        res[s, core, chunk_rows(q), :] = total.astype(BF16)
        for k in far_first(nq):
            p4_copy(s, lax.rem(q + k, nq)).start()

    def p5_copy(s):
        rows = res.at[s, core]
        return pltpu.make_async_remote_copy(
            src_ref=rows, dst_ref=rows, send_sem=p5_send.at[s], recv_sem=p5_recv.at[s],
            device_id=chip(q, 1 - core), device_id_type=MESH,
        )

    def deliver(s, k):
        rows = pl.ds(pl.multiple_of(s * 2 * HALF + k * HALF, HALF), HALF)
        gw_o[rows, :] = res[s, k].astype(F32)

    def p5_start(s):
        all_of(res.at[s, core, pl.ds(0, HALF - chunk)], p4_recv.at[s])
        p5_copy(s).start()
        deliver(s, core)

    def p5_finish(s):
        p5_copy(s).wait_recv()
        deliver(s, 1 - core)

    def drain(s):
        all_of(p2s.at[s, pl.ds(0, HALF - chunk)], p2_send.at[s])
        all_of(zb.at[s, pl.ds(0, nz - 1)], z_send.at[s])
        all_of(res.at[s, core, pl.ds(0, HALF - chunk)], p4_send.at[s])

    column = lax.broadcasted_iota(jnp.int32, (128, 128), 0)

    def act_row(t, x, left, right):
        rows = pl.ds(pl.multiple_of(t * 128, 128), 128)
        act3[rows, 0:128] = jnp.where(column == 0, left, pltpu.roll(x, 1, 0)).astype(BF16)
        act3[rows, 128:256] = x.astype(BF16)
        act3[rows, 256:384] = jnp.where(column == 127, right, pltpu.roll(x, 127, 0)).astype(BF16)

    @pl.loop(0, ROWS, unroll=4)
    def _(r):
        act, slope = gelu_parts(pre_v[r].astype(F32))
        act_row(r + 1, act, 0.0, 0.0)
        slope_f[r + 1, 0:128, :] = slope

    copies = lax.broadcasted_iota(jnp.int32, (64, 128), 1) // 2
    copies = jnp.where(copies == lax.broadcasted_iota(jnp.int32, (64, 128), 0), 0.25, 0.0).astype(BF16)
    gpt[:, 0:256] = jnp.zeros((128, 256), BF16)
    gpt[:, 18 * 128 : 20 * 128] = jnp.zeros((128, 256), BF16)
    for i in range(ROWS // 2):
        t = lax.dot_general(
            go_v[i], copies, (((0,), (0,)), ((), ())), preferred_element_type=F32
        ).astype(BF16)
        gpt[:, (2 * i + 2) * 128 : (2 * i + 3) * 128] = t
        gpt[:, (2 * i + 3) * 128 : (2 * i + 4) * 128] = t

    corner = jnp.concatenate([e_s[0, 16:32, :], e_s[1, 16:32, :]], 0)
    place = lax.broadcasted_iota(jnp.int32, (32, 128), 1)
    source = lax.broadcasted_iota(jnp.int32, (32, 128), 0)
    for a in range(3):
        row = place % 32 - 7 - a
        chosen = jnp.logical_and(
            jnp.logical_and(row >= 0, row < ROWS), place // 32 * 16 + (row + 16) // 2 - 8 == source
        )
        chosen = jnp.where(chosen, 0.25, 0.0).astype(BF16)
        gpt_side[128 * a : 128 * a + 128, :] = lax.dot_general(
            corner, chosen, (((0,), (0,)), ((), ())), preferred_element_type=F32
        ).astype(BF16)

    lhs = jnp.concatenate([gpt[:, (3 - a) * 128 : (3 - a) * 128 + 2048] for a in range(3)], 0)
    both[...] = dot(lhs, act3[128 : 17 * 128, :])

    def grad_rows(i, taps):
        here, after = pext[i], pext[i + 1]
        lhs = jnp.concatenate(
            [jnp.concatenate([after, here, here], 1), jnp.concatenate([after, after, here], 1)], 0
        )
        terms = dot(lhs, taps)
        for s in range(2):
            part = terms[PWIDE * s : PWIDE * (s + 1)]
            t0, t1, t2 = part[:, 0:128], part[:, 128:256], part[:, 256:384]
            ga_f[2 * i + s, pl.ds(0, PWIDE, stride=2), :] = t0 + t1 + pltpu.roll(t2, 1, 0)
            ga_f[2 * i + s, pl.ds(1, PWIDE, stride=2), :] = pltpu.roll(t0, PWIDE - 1, 0) + t1 + t2
            g_v[2 * i + s] = (ga_f[2 * i + s] * slope_f[2 * i + s]).astype(BF16)

    for i in range(1, 9):
        pext[i, 0:64, :] = (0.25 * go_v[i - 1].astype(F32)).astype(BF16)
        pext[i, 64:80, :] = jnp.zeros((16, 128), BF16)

    @pl.loop(1, 8, unroll=7)
    def _(i):
        grad_rows(i, wa[0])

    def in_row(t, x, left, right):
        cells = slice(128 * t, 128 * t + 128)
        in3[0:64, cells] = jnp.where(lane == 0, left, pltpu.roll(x, 1, 1)).astype(BF16)
        in3[64:128, cells] = x.astype(BF16)
        in3[128:192, cells] = jnp.where(lane == 127, right, pltpu.roll(x, 127, 1)).astype(BF16)

    for t in range(1, 17):
        in_row(t, in_v[t - 1].astype(F32), 0.0, 0.0)

    inner = jnp.where(jnp.logical_and(column > 0, column < 127), 1.0, 0.0)
    lhs = jnp.concatenate([in3[:, (a + 1) * 128 : (a + 15) * 128] for a in range(3)], 0)
    rhs = [(g_v[t, 0:128, :].astype(F32) * inner).astype(BF16) for t in range(2, 16)]
    acc[1, 384:960, :] = dot(lhs, jnp.concatenate(rhs, 0))
    acc[1, 960:1024, :] = jnp.zeros((64, 128), F32)

    g_edge[...] = jnp.zeros((128, 128), F32)
    for b, (low, high) in enumerate(((None, 126), (0, 127), (1, None))):
        edge = jnp.zeros((C0, 128), F32)
        for r in range(ROWS):
            x = in_v[r].astype(F32)
            if low is not None:
                edge = jnp.where(lane == 8 + r, pltpu.roll(x, 8 + r - low, 1), edge)
            if high is not None:
                edge = jnp.where(lane == 40 + r, pltpu.roll(x, (40 + r - high) % 128, 1), edge)
        in_edge[b] = edge

    def arrived(slot):
        dst = e_r.at[slot] if slot < 6 else row_r.at[slot - 6]
        pltpu.make_async_copy(dst, dst, halo_recv.at[slot]).wait()

    for slot in (1, 4):
        arrived(slot)

    @pl.when(jnp.logical_not(is_last))
    def _():
        for slot in (2, 5, 7):
            arrived(slot)

    keep = jnp.where(is_last, 0.0, 1.0).astype(F32)
    zero8 = jnp.zeros((8, 128), F32)
    for side in range(2):
        mid = e_r[3 * side + 1].astype(F32)
        low = e_r[3 * side + 2].astype(F32)
        hc[side, 8:24, :] = mid[0:16]
        hc[side, 24:32, :] = jnp.broadcast_to(low[0:1], (8, 128))
        act, slope = gelu_parts(hc[side, 8:32, :])
        hc[side, 8:32, :] = act
        hs[side, 8:32, :] = slope
        hg[side, 8:16, :] = 0.25 * mid[16:24]
        hg[side, 16:24, :] = 0.25 * jnp.broadcast_to(low[16:17], (8, 128))
        hi[side, 0:8, :] = zero8
        hi[side, 8:24, :] = mid[32:48]
        hi[side, 24:32, :] = jnp.broadcast_to(low[32:33], (8, 128))
    act, slope = gelu_parts(row_r[1, 0:128, :].astype(F32))
    act_row(17, act, 0.0, 0.0)
    slope_f[17, 0:128, :] = slope * keep

    def sides(t):
        scale = keep if t == 17 else 1.0
        for side, place in enumerate((152, 128)):
            slope_f[t, place : place + 8, :] = scale * jnp.broadcast_to(hs[side, t + 7 : t + 8, :], (8, 128))

    def pooled(i):
        left = jnp.broadcast_to(hg[0, i + 7 : i + 8, :], (16, 128))
        right = jnp.broadcast_to(hg[1, i + 7 : i + 8, :], (16, 128))
        tile = jnp.where(sub == 0, right, jnp.where(sub == 15, left, 0.0))
        pext[i, 64:80, :] = tile.astype(BF16)

    below = jnp.logical_and(
        lax.broadcasted_iota(jnp.int32, (32, 128), 0) >= 8, lax.broadcasted_iota(jnp.int32, (32, 128), 0) < 25
    )
    act3[2304:2432, :] = jnp.zeros((128, 384), BF16)
    act3[2304:2336, 0:128] = jnp.where(below, hc[0], 0.0).astype(BF16)
    act3[2336:2368, 256:384] = jnp.where(below, hc[1], 0.0).astype(BF16)
    lhs = jnp.concatenate(
        [jnp.concatenate([gpt[:, (19 - a) * 128 : (20 - a) * 128] for a in range(3)], 0), gpt_side[...]], 1
    )
    terms = both[...] + dot(lhs, act3[2176:2432, :])
    for a in range(1, 3):
        for b in range(3):
            block = terms[128 * a : 128 * a + 128, 128 * b : 128 * b + 128]
            acc[0, (3 * a + b - 3) * 128 : (3 * a + b - 2) * 128, :] = block.T
    both[0:128, :] = terms[0:128]
    acc[0, 768:1024, :] = jnp.zeros((256, 128), F32)
    p1_start(0)

    for t in range(1, 18):
        sides(t)
    pext[9, 0:64, :] = (0.25 * row_r[1, 128:192, :].astype(F32)).astype(BF16)
    for i in range(1, 10):
        pooled(i)
    tiles = [pext[i, 64:80, :] for i in range(1, 9)]
    lhs = jnp.concatenate(
        [
            jnp.concatenate([tiles[(t + 2) // 2 - 1], tiles[(t + 1) // 2 - 1], tiles[t // 2 - 1]], 1)
            for t in range(2, 16)
        ],
        0,
    )
    terms = dot(lhs, wa[0])
    for t in range(2, 16):
        part = terms[16 * (t - 2) : 16 * (t - 1)]
        t0, t1, t2 = part[:, 0:128], part[:, 128:256], part[:, 256:384]
        for first, at_row, more in ((0, 0, t2[15:16]), (112, 15, t0[0:1]), (128, 0, (t0 + t1)[0:1]), (144, 15, (t1 + t2)[15:16])):
            more = jnp.where(sub == at_row, jnp.broadcast_to(more, (16, 128)), 0.0)
            cells = slice(first, first + 16)
            grad = (ga_f[t, cells, :] + more) * slope_f[t, cells, :]
            g_v[t, cells, :] = grad.astype(BF16)
            if first == 0:
                g_edge[t + 7 : t + 8, :] = grad[0:1]
            if first == 112:
                g_edge[t + 39 : t + 40, :] = grad[15:16]
    grad_rows(8, wa[0])

    edges = [jnp.concatenate([hi[side], jnp.zeros((96, 128), F32)], 0).T[0:64] for side in range(2)]
    for t in (1, 2, 15, 16, 17):
        x = (in_v[t - 1] if t < 17 else row_r[1, 192:256, :]).astype(F32)
        in_row(t, x, pltpu.roll(edges[0], 121 - t, 1), pltpu.roll(edges[1], 120 - t, 1))
    beside = [
        jnp.where(lane < 32, edges[0], in_edge[0]),
        in_edge[1],
        jnp.where(lane < 32, in_edge[2], pltpu.roll(edges[1], 32, 1)),
    ]
    beside = jnp.concatenate(
        [(pltpu.roll(x, (1 - a) % 128, 1) if a != 1 else x).astype(BF16) for a in range(3) for x in beside], 0
    )

    @pl.when(is_pole)
    def _():
        dst = row_r.at[0, pl.ds(0, 192)]
        pltpu.make_async_copy(dst, dst, halo_recv.at[6]).wait()
        row_r[0, 192:256, :] = jnp.zeros((64, 128), BF16)

    @pl.when(jnp.logical_not(is_pole))
    def _():
        arrived(6)

    arrived(0)
    arrived(3)
    for side in range(2):
        top = e_r[3 * side].astype(F32)

        def pick(first, last):
            return jnp.broadcast_to(jnp.where(is_pole, top[first : first + 1], top[last : last + 1]), (8, 128))

        act, slope = gelu_parts(pick(0, 15))
        hc[side, 0:8, :] = act
        hs[side, 0:8, :] = slope
        hg[side, 0:8, :] = 0.25 * pick(16, 23)
        hi[side, 0:8, :] = jnp.where(is_pole, 0.0, pick(32, 47))
    act, slope = gelu_parts(row_r[0, 0:128, :].astype(F32))
    slope_f[0, 0:128, :] = slope
    sides(0)
    pext[0, 0:64, :] = (0.25 * row_r[0, 128:192, :].astype(F32)).astype(BF16)
    pooled(0)
    grad_rows(0, wa[1])

    act_row(0, act, jnp.broadcast_to(hc[0, 7:8, :], (128, 128)), jnp.broadcast_to(hc[1, 7:8, :], (128, 128)))
    top_go = lax.dot_general(
        row_r[0, 128:192, :], copies, (((0,), (0,)), ((), ())), preferred_element_type=F32
    ).astype(BF16)
    gpt_top[...] = jnp.where(is_pole, top_go.astype(F32), gpt[:, 256:384].astype(F32)).astype(BF16)

    @pl.when(is_pole)
    def _():
        act_row(
            0,
            act3[128:256, 128:256].astype(F32),
            jnp.broadcast_to(hc[0, 8:9, :], (128, 128)),
            jnp.broadcast_to(hc[1, 8:9, :], (128, 128)),
        )

    first_row = both[0:128, :] + dot(gpt_top[...], act3[0:128, :])
    for b in range(3):
        acc[1, b * 128 : (b + 1) * 128, :] = first_row[:, 128 * b : 128 * b + 128].T

    x = row_r[0, 192:256, :].astype(F32)
    edges = [jnp.concatenate([hi[side], jnp.zeros((96, 128), F32)], 0).T[0:64] for side in range(2)]
    in_row(0, x, pltpu.roll(edges[0], 121, 1), pltpu.roll(edges[1], 120, 1))
    here = jnp.concatenate([in3[:, 0:128], in3[:, 128:256], in3[:, 256:384]], 0)
    fold = jnp.where(is_pole, in3[:, 128:256].astype(F32), 0.0).astype(BF16)
    there = jnp.concatenate([fold, jnp.zeros((384, 128), BF16)], 0)
    last = jnp.concatenate([in3[:, 15 * 128 : 16 * 128], in3[:, 16 * 128 : 17 * 128], in3[:, 17 * 128 : 18 * 128]], 0)
    rhs = [g_v[1, 0:128, :], g_v[0, 0:128, :], g_v[16, 0:128, :], g_edge[...].astype(BF16)]
    acc[1, 384:960, :] += dot(jnp.concatenate([here, there, last, beside], 1), jnp.concatenate(rhs, 0))

    p1_start(1)
    p2_start(0)

    def input_row(r):
        lhs = jnp.concatenate([g_v[r + 2], g_v[r + 1], g_v[r]], 1)
        terms = dot(lhs, wb[jnp.where(r == 0, 1, 0)])
        t01, t2 = terms[:, 0:128], terms[:, 128:192]
        first = lax.broadcasted_iota(jnp.int32, (128, 128), 1) < 64
        t01 = jnp.where(first, pltpu.roll(t01, WIDE - 1, 0)[0:128], t01[0:128]).T
        t2 = pltpu.roll(t2, 1, 0)[0:128].T
        gi_o[r] = (t01[0:64] + t01[64:128] + t2).astype(BF16)

    @pl.loop(0, ROWS // 2, unroll=4)
    def _(r):
        input_row(r)

    p2_start(1)

    @pl.loop(ROWS // 2, ROWS, unroll=4)
    def _(r):
        input_row(r)

    z_start(0)
    z_start(1)
    p4_start(0)
    p4_start(1)
    p5_start(0)

    @pl.when(is_pole)
    def _():
        turned.wait_send()

    @pl.when(jnp.logical_not(is_pole))
    def _():
        above.wait_send()

    for copy in always:
        copy.wait_send()

    @pl.when(jnp.logical_not(is_last))
    def _():
        for copy in down:
            copy.wait_send()

    drain(0)
    p5_finish(0)
    p5_start(1)
    drain(1)
    p5_finish(1)
    p5_copy(0).wait_send()
    p5_copy(1).wait_send()


def write_out(gi_v, gw_v, gi_o, gw1_o, gw2_o, sem):
    copies = [
        pltpu.make_async_copy(gw_v.at[pl.ds(0, 768)], gw2_o.at[pl.ds(384, 768)], sem.at[0]),
        pltpu.make_async_copy(gw_v.at[pl.ds(1024, 384)], gw2_o.at[pl.ds(0, 384)], sem.at[1]),
        pltpu.make_async_copy(gw_v.at[pl.ds(1408, 576)], gw1_o, sem.at[2]),
        pltpu.make_async_copy(gi_v, gi_o, sem.at[3]),
    ]
    for copy in copies:
        copy.start()
    for copy in copies:
        copy.wait()


def section(nlat, nlon, inputs, pre_first, grad_out, w_first, w_second):
    nq, nz = nlat * 2, nlon // 4
    chunk = HALF // nq
    hbm = pl.BlockSpec(memory_space=pltpu.HBM)
    vmem = pltpu.VMEM
    dma = pltpu.SemaphoreType.DMA
    gi, gw = pl.pallas_call(
        functools.partial(kernel, nlat, nlon),
        out_shape=(vmem((ROWS, C0, COLS), BF16), vmem((2048, 128), F32)),
        in_specs=[hbm] * 5,
        out_specs=(pl.BlockSpec(memory_space=vmem), pl.BlockSpec(memory_space=vmem)),
        scratch_shapes=[
            vmem((ROWS, COLS, C1), BF16),
            vmem((ROWS, C0, COLS), BF16),
            vmem((ROWS // 2, COLS // 2, C1), BF16),
            vmem((9, C0, C1), BF16),
            vmem((9, C1, C1), BF16),
            vmem((2, 384, 384), BF16),
            vmem((2, 384, 192), BF16),
            vmem((2, 48, 128), BF16),
            vmem((2, 256, 128), BF16),
            vmem((6, 48, 128), BF16),
            vmem((2, 256, 128), BF16),
            vmem((2, 32, 128), F32),
            vmem((2, 32, 128), F32),
            vmem((2, 24, 128), F32),
            vmem((2, 32, 128), F32),
            vmem((18, WIDE, 128), F32),
            vmem((19 * 128, 384), BF16),
            vmem((10, PWIDE, 128), BF16),
            vmem((128, 20 * 128), BF16),
            vmem((128, 128), BF16),
            vmem((384, 128), BF16),
            vmem((192, 18 * 128), BF16),
            vmem((3, C0, 128), F32),
            vmem((128, 128), F32),
            vmem((18, WIDE, 128), BF16),
            vmem((18, WIDE, 128), F32),
            vmem((384, 384), F32),
            vmem((2, 2 * HALF, 128), F32),
            vmem((2, HALF, 128), BF16),
            vmem((2, HALF, 128), BF16),
            vmem((2, HALF, 128), BF16),
            vmem((2, nq, chunk, 128), BF16),
            vmem((2, nz, chunk, 128), BF16),
            vmem((2, 2, HALF, 128), BF16),
            dma((5,)),
            dma((8,)), dma((8,)),
            dma((2,)), dma((2,)),
            dma((2,)), dma((2,)),
            dma((2,)), dma((2,)),
            dma((2,)), dma((2,)),
            dma((2,)), dma((2,)),
        ],
        compiler_params=pltpu.CompilerParams(
            collective_id=0, has_side_effects=True, vmem_limit_bytes=40 * 1024 * 1024
        ),
        cost_estimate=pl.CostEstimate(flops=1_800_000_000, bytes_accessed=3_000_000, transcendentals=600_000),
    )(
        *(
            pltpu.with_memory_space_constraint(x, pltpu.HBM)
            for x in (
                pre_first,
                jnp.transpose(inputs, (0, 2, 1)),
                grad_out,
                w_first.reshape(9, C0, C1),
                w_second.reshape(9, C1, C1),
            )
        )
    )
    gi, grad_w_first, grad_w_second = pl.pallas_call(
        write_out,
        out_shape=(
            jax.ShapeDtypeStruct((ROWS, C0, COLS), BF16),
            jax.ShapeDtypeStruct((9 * C0, C1), F32),
            jax.ShapeDtypeStruct((9 * C1, C1), F32),
        ),
        in_specs=[pl.BlockSpec(memory_space=vmem)] * 2,
        out_specs=(pl.BlockSpec(memory_space=pl.ANY),) * 3,
        scratch_shapes=[dma((4,))],
        compiler_params=pltpu.CompilerParams(vmem_limit_bytes=16 * 1024 * 1024),
    )(gi, gw)
    return (
        jnp.transpose(gi, (0, 2, 1)),
        grad_w_first.reshape(3, 3, C0, C1),
        grad_w_second.reshape(3, 3, C1, C1),
    )


def solution(mesh):
    nlat, nlon = mesh.shape["lat"], mesh.shape["lon"]
    in_specs = (P("lat", "lon", None), P("lat", "lon", None), P("lat", "lon", None), P(), P())
    out_specs = (P("lat", "lon", None), P(), P())
    return jax.shard_map(
        functools.partial(section, nlat, nlon), mesh=mesh, in_specs=in_specs, out_specs=out_specs, check_vma=False
    )
```

```python
import functools

import jax
import jax.numpy as jnp
from jax import lax
from jax.experimental import pallas as pl
from jax.experimental.pallas import tpu as pltpu
from jax.sharding import PartitionSpec as P

INV_ROOT = 0.7071067811865476
DENSITY = 0.3989422804014327
BF16 = jnp.bfloat16
F32 = jnp.float32
MESH = pl.DeviceIdType.MESH

ROWS, COLS, C0, C1 = 16, 128, 64, 128
WIDE = COLS + 32
PWIDE = COLS // 2 + 16
HALF = 512


def far_first(n):
    return sorted(range(1, n), key=lambda k: (-min(k, n - k), k))


def gelu_parts(value):
    cdf = 0.5 * (1.0 + lax.erf(value * INV_ROOT))
    act = value * cdf
    slope = cdf + value * jnp.exp(-0.5 * value * value) * DENSITY
    return act, slope


def dot(a, b):
    return lax.dot_general(a, b, (((1,), (0,)), ((), ())), preferred_element_type=F32)


def kernel(
    nlat, nlon,
    pre_h, in_h, go_h, w1_h, w2_h,
    gi_o, gw_o,
    pre_v, in_v, go_v, w1_v, w2_v, wa, wb,
    e_s, row_s, e_r, row_r, hc, hs, hg, hi,
    slope_f, act3, pext, gpt, gpt_top, gpt_side, in3, in_edge, g_edge, wide, g_v, ga_f, both,
    acc, p1s, p1r, p2s, p2r, zb, res,
    load_sem, halo_send, halo_recv, p1_send, p1_recv, p2_send, p2_recv,
    z_send, z_recv, p4_send, p4_recv, p5_send, p5_recv,
):
    lat, lon = lax.axis_index("lat"), lax.axis_index("lon")
    nq, nz = nlat * 2, nlon // 4
    chunk = HALF // nq
    z, yhi, core = lon // 4, (lon % 4) // 2, lon % 2
    q = lat * 2 + yhi
    is_pole = lat == 0
    is_last = lat == nlat - 1
    half = nlon // 2

    def chip(p, k):
        return (p // 2, z * 4 + (p % 2) * 2 + k)

    def at(dlat, dlon):
        return (dlat, lax.rem(dlon + 2 * nlon, nlon))

    loads = [
        pltpu.make_async_copy(src, dst, load_sem.at[i])
        for i, (src, dst) in enumerate(
            ((pre_h, pre_v), (in_h, in_v), (go_h, go_v), (w2_h, w2_v), (w1_h, w1_v))
        )
    ]
    for load in loads:
        load.start()

    barrier = pltpu.get_barrier_semaphore()

    def greet(device):
        pl.semaphore_signal(barrier, inc=1, device_id=device, device_id_type=MESH)

    top_lat = jnp.where(is_pole, 0, lat - 1)
    top_lon = jnp.where(is_pole, lon + half, lon)
    for d in (-1, 0, 1):
        greet(at(top_lat, top_lon + d))
    for k in far_first(nz)[:1]:
        greet((lat, lax.rem(lon + 4 * k, nlon)))
    for k in far_first(nq)[:3]:
        greet(chip(lax.rem(q + k, nq), core))
    for d in (-1, 1):
        greet(at(lat, lon + d))

    @pl.when(jnp.logical_not(is_last))
    def _():
        for d in (-1, 1, 0):
            greet(at(lat + 1, lon + d))

    for k in far_first(nz)[1:]:
        greet((lat, lax.rem(lon + 4 * k, nlon)))
    for k in far_first(nq)[3:]:
        greet(chip(lax.rem(q + k, nq), core))
    greet(chip(q, 1 - core))

    loads[0].wait()
    loads[1].wait()
    loads[2].wait()
    lane = lax.broadcasted_iota(jnp.int32, (C0, 128), 1)
    sub = lax.broadcasted_iota(jnp.int32, (16, 128), 0)
    zero16 = jnp.zeros((16, 128), F32)
    for side, (col, first) in enumerate(((0, 0), (15, 112))):
        edge = zero16
        for r in range(ROWS):
            tile = pre_v[r, first : first + 16, :].astype(F32)
            edge = jnp.where(sub == r, jnp.broadcast_to(tile[col : col + 1], (16, 128)), edge)
        e_s[side, 0:16, :] = edge.astype(BF16)
        edge = zero16
        for r in range(ROWS // 2):
            tile = go_v[r, first // 112 * 48 : first // 112 * 48 + 16, :].astype(F32)
            edge = jnp.where(sub == r, jnp.broadcast_to(tile[col : col + 1], (16, 128)), edge)
        e_s[side, 16:32, :] = edge.astype(BF16)
        edge = jnp.zeros((C0, 128), F32)
        for r in range(ROWS):
            shift = r if side == 0 else r + 1
            edge = jnp.where(lane == r, pltpu.roll(in_v[r].astype(F32), shift, 1), edge)
        e_s[side, 32:48, 0:64] = edge.T[0:16].astype(BF16)
        e_s[side, 32:48, 64:128] = jnp.zeros((16, 64), BF16)
    for end, r in enumerate((0, ROWS - 1)):
        row_s[end, 0:128, :] = pre_v[r]
        row_s[end, 128:192, :] = go_v[r // 2]
        row_s[end, 192:256, :] = in_v[r]

    pl.semaphore_wait(barrier, jnp.where(is_last, 0, 3) + 2 + 3 + 1 + (nq - 1) + (nz - 1))

    up = jnp.where(is_pole, 0, 2)

    def edge_copy(number, side, slot, device):
        return pltpu.make_async_remote_copy(
            src_ref=e_s.at[side], dst_ref=e_r.at[slot], send_sem=halo_send.at[number],
            recv_sem=halo_recv.at[slot], device_id=device, device_id_type=MESH,
        )

    def row_copy(number, end, slot, device, size=256):
        return pltpu.make_async_remote_copy(
            src_ref=row_s.at[end, pl.ds(0, size)], dst_ref=row_r.at[slot, pl.ds(0, size)], send_sem=halo_send.at[number],
            recv_sem=halo_recv.at[6 + slot], device_id=device, device_id_type=MESH,
        )

    turned = row_copy(0, 0, 0, at(0, lon + half), 192)
    above = row_copy(0, 0, 1, at(lat - 1, lon))
    always = [
        edge_copy(3, 1, up, at(top_lat, top_lon + 1)),
        edge_copy(4, 0, up + 3, at(top_lat, top_lon - 1)),
        edge_copy(1, 1, 1, at(lat, lon + 1)),
        edge_copy(2, 0, 4, at(lat, lon - 1)),
    ]
    down = [
        row_copy(5, 1, 0, at(lat + 1, lon)),
        edge_copy(6, 1, 0, at(lat + 1, lon + 1)),
        edge_copy(7, 0, 3, at(lat + 1, lon - 1)),
    ]
    for copy in always[:2]:
        copy.start()

    @pl.when(is_pole)
    def _():
        turned.start()

    @pl.when(jnp.logical_not(is_pole))
    def _():
        above.start()

    for copy in always[2:]:
        copy.start()

    @pl.when(jnp.logical_not(is_last))
    def _():
        for copy in down:
            copy.start()

    @pl.when(is_last)
    def _():
        e_r[2] = jnp.zeros((48, 128), BF16)
        e_r[5] = jnp.zeros((48, 128), BF16)
        row_r[1] = jnp.zeros((256, 128), BF16)

    loads[3].wait()
    loads[4].wait()
    for a in range(3):
        for b in range(3):
            t = w2_v[3 * a + b].astype(F32).T.astype(BF16)
            wa[0, 128 * a : 128 * a + 128, 128 * b : 128 * b + 128] = t
            u = w1_v[3 * a + b].astype(F32).T.astype(BF16)
            wb[0, 128 * a : 128 * a + 128, 64 * b : 64 * b + 64] = u
    wa[1] = wa[0]
    wb[1] = wb[0]

    @pl.when(is_pole)
    def _():
        wa[1, 256:384, :] = wa[0, 0:128, :]
        wb[1, 256:384, :] = wb[0, 0:128, :]

    def p1_copy(s):
        return pltpu.make_async_remote_copy(
            src_ref=p1s.at[s], dst_ref=p1r.at[s], send_sem=p1_send.at[s], recv_sem=p1_recv.at[s],
            device_id=chip(q, 1 - core), device_id_type=MESH,
        )

    def p1_start(s):
        p1s[s] = acc[s, pl.ds(pl.multiple_of((1 - core) * HALF, HALF), HALF), :].astype(BF16)
        p1_copy(s).start()

    def chunk_rows(p):
        return pl.ds(pl.multiple_of(p * chunk, 32), chunk)

    def p2_copy(s, p):
        return pltpu.make_async_remote_copy(
            src_ref=p2s.at[s, chunk_rows(p)], dst_ref=p2r.at[s, q], send_sem=p2_send.at[s],
            recv_sem=p2_recv.at[s], device_id=chip(p, core), device_id_type=MESH,
        )

    def p2_start(s):
        p1_copy(s).wait()
        own = pl.ds(pl.multiple_of(core * HALF, HALF), HALF)
        total = acc[s, own, :] + p1r[s].astype(F32)
        acc[s, own, :] = total
        p2s[s] = total.astype(BF16)
        for k in far_first(nq):
            p2_copy(s, lax.rem(q + k, nq)).start()

    def z_copy(s, k):
        return pltpu.make_async_remote_copy(
            src_ref=zb.at[s, z], dst_ref=zb.at[s, z], send_sem=z_send.at[s], recv_sem=z_recv.at[s],
            device_id=(lat, lax.rem(lon + 4 * k, nlon)), device_id_type=MESH,
        )

    def all_of(ref, sem):
        pltpu.make_async_copy(ref, ref, sem).wait()

    def z_start(s):
        total = acc[s, pl.ds(pl.multiple_of(core * HALF + q * chunk, 32), chunk), :]
        all_of(p2r.at[s, pl.ds(0, nq - 1)], p2_recv.at[s])
        for k in range(1, nq):
            total = total + p2r[s, lax.rem(q + nq - k, nq)].astype(F32)
        zb[s, z] = total.astype(BF16)
        for k in far_first(nz):
            z_copy(s, k).start()

    def p4_copy(s, p):
        mine = res.at[s, core, chunk_rows(q)]
        return pltpu.make_async_remote_copy(
            src_ref=mine, dst_ref=mine, send_sem=p4_send.at[s], recv_sem=p4_recv.at[s],
            device_id=chip(p, core), device_id_type=MESH,
        )

    def p4_start(s):
        all_of(zb.at[s, pl.ds(0, nz - 1)], z_recv.at[s])
        total = zb[s, 0].astype(F32)
        for k in range(1, nz):
            total = total + zb[s, k].astype(F32)
        res[s, core, chunk_rows(q), :] = total.astype(BF16)
        for k in far_first(nq):
            p4_copy(s, lax.rem(q + k, nq)).start()

    def p5_copy(s):
        rows = res.at[s, core]
        return pltpu.make_async_remote_copy(
            src_ref=rows, dst_ref=rows, send_sem=p5_send.at[s], recv_sem=p5_recv.at[s],
            device_id=chip(q, 1 - core), device_id_type=MESH,
        )

    def deliver(s, k):
        rows = pl.ds(pl.multiple_of(s * 2 * HALF + k * HALF, HALF), HALF)
        gw_o[rows, :] = res[s, k].astype(F32)

    def p5_start(s):
        all_of(res.at[s, core, pl.ds(0, HALF - chunk)], p4_recv.at[s])
        p5_copy(s).start()
        deliver(s, core)

    def p5_finish(s):
        p5_copy(s).wait_recv()
        deliver(s, 1 - core)

    def drain(s):
        all_of(p2s.at[s, pl.ds(0, HALF - chunk)], p2_send.at[s])
        all_of(zb.at[s, pl.ds(0, nz - 1)], z_send.at[s])
        all_of(res.at[s, core, pl.ds(0, HALF - chunk)], p4_send.at[s])

    column = lax.broadcasted_iota(jnp.int32, (128, 128), 0)

    def act_row(t, x, left, right):
        rows = pl.ds(pl.multiple_of(t * 128, 128), 128)
        act3[rows, 0:128] = jnp.where(column == 0, left, pltpu.roll(x, 1, 0)).astype(BF16)
        act3[rows, 128:256] = x.astype(BF16)
        act3[rows, 256:384] = jnp.where(column == 127, right, pltpu.roll(x, 127, 0)).astype(BF16)

    @pl.loop(0, ROWS, unroll=4)
    def _(r):
        act, slope = gelu_parts(pre_v[r].astype(F32))
        act_row(r + 1, act, 0.0, 0.0)
        slope_f[r + 1, 0:128, :] = slope

    copies = lax.broadcasted_iota(jnp.int32, (64, 128), 1) // 2
    copies = jnp.where(copies == lax.broadcasted_iota(jnp.int32, (64, 128), 0), 0.25, 0.0).astype(BF16)
    gpt[:, 0:256] = jnp.zeros((128, 256), BF16)
    gpt[:, 18 * 128 : 20 * 128] = jnp.zeros((128, 256), BF16)
    for i in range(ROWS // 2):
        t = lax.dot_general(
            go_v[i], copies, (((0,), (0,)), ((), ())), preferred_element_type=F32
        ).astype(BF16)
        gpt[:, (2 * i + 2) * 128 : (2 * i + 3) * 128] = t
        gpt[:, (2 * i + 3) * 128 : (2 * i + 4) * 128] = t

    corner = jnp.concatenate([e_s[0, 16:32, :], e_s[1, 16:32, :]], 0)
    place = lax.broadcasted_iota(jnp.int32, (32, 128), 1)
    source = lax.broadcasted_iota(jnp.int32, (32, 128), 0)
    for a in range(3):
        row = place % 32 - 7 - a
        chosen = jnp.logical_and(
            jnp.logical_and(row >= 0, row < ROWS), place // 32 * 16 + (row + 16) // 2 - 8 == source
        )
        chosen = jnp.where(chosen, 0.25, 0.0).astype(BF16)
        gpt_side[128 * a : 128 * a + 128, :] = lax.dot_general(
            corner, chosen, (((0,), (0,)), ((), ())), preferred_element_type=F32
        ).astype(BF16)

    lhs = jnp.concatenate([gpt[:, (3 - a) * 128 : (3 - a) * 128 + 2048] for a in range(3)], 0)
    both[...] = dot(lhs, act3[128 : 17 * 128, :])

    def grad_rows(i, taps):
        here, after = pext[i], pext[i + 1]
        lhs = jnp.concatenate(
            [jnp.concatenate([after, here, here], 1), jnp.concatenate([after, after, here], 1)], 0
        )
        terms = dot(lhs, taps)
        for s in range(2):
            part = terms[PWIDE * s : PWIDE * (s + 1)]
            t0, t1, t2 = part[:, 0:128], part[:, 128:256], part[:, 256:384]
            ga_f[2 * i + s, pl.ds(0, PWIDE, stride=2), :] = t0 + t1 + pltpu.roll(t2, 1, 0)
            ga_f[2 * i + s, pl.ds(1, PWIDE, stride=2), :] = pltpu.roll(t0, PWIDE - 1, 0) + t1 + t2
            g_v[2 * i + s] = (ga_f[2 * i + s] * slope_f[2 * i + s]).astype(BF16)

    for i in range(1, 9):
        pext[i, 0:64, :] = (0.25 * go_v[i - 1].astype(F32)).astype(BF16)
        pext[i, 64:80, :] = jnp.zeros((16, 128), BF16)

    @pl.loop(1, 8, unroll=7)
    def _(i):
        grad_rows(i, wa[0])

    def in_row(t, x, left, right):
        cells = slice(128 * t, 128 * t + 128)
        in3[0:64, cells] = jnp.where(lane == 0, left, pltpu.roll(x, 1, 1)).astype(BF16)
        in3[64:128, cells] = x.astype(BF16)
        in3[128:192, cells] = jnp.where(lane == 127, right, pltpu.roll(x, 127, 1)).astype(BF16)

    for t in range(1, 17):
        in_row(t, in_v[t - 1].astype(F32), 0.0, 0.0)

    inner = jnp.where(jnp.logical_and(column > 0, column < 127), 1.0, 0.0)
    lhs = jnp.concatenate([in3[:, (a + 1) * 128 : (a + 15) * 128] for a in range(3)], 0)
    rhs = [(g_v[t, 0:128, :].astype(F32) * inner).astype(BF16) for t in range(2, 16)]
    acc[1, 384:960, :] = dot(lhs, jnp.concatenate(rhs, 0))
    acc[1, 960:1024, :] = jnp.zeros((64, 128), F32)

    g_edge[...] = jnp.zeros((128, 128), F32)
    for b, (low, high) in enumerate(((None, 126), (0, 127), (1, None))):
        edge = jnp.zeros((C0, 128), F32)
        for r in range(ROWS):
            x = in_v[r].astype(F32)
            if low is not None:
                edge = jnp.where(lane == 8 + r, pltpu.roll(x, 8 + r - low, 1), edge)
            if high is not None:
                edge = jnp.where(lane == 40 + r, pltpu.roll(x, (40 + r - high) % 128, 1), edge)
        in_edge[b] = edge

    def arrived(slot):
        dst = e_r.at[slot] if slot < 6 else row_r.at[slot - 6]
        pltpu.make_async_copy(dst, dst, halo_recv.at[slot]).wait()

    for slot in (1, 4):
        arrived(slot)

    @pl.when(jnp.logical_not(is_last))
    def _():
        for slot in (2, 5, 7):
            arrived(slot)

    keep = jnp.where(is_last, 0.0, 1.0).astype(F32)
    zero8 = jnp.zeros((8, 128), F32)
    for side in range(2):
        mid = e_r[3 * side + 1].astype(F32)
        low = e_r[3 * side + 2].astype(F32)
        hc[side, 8:24, :] = mid[0:16]
        hc[side, 24:32, :] = jnp.broadcast_to(low[0:1], (8, 128))
        act, slope = gelu_parts(hc[side, 8:32, :])
        hc[side, 8:32, :] = act
        hs[side, 8:32, :] = slope
        hg[side, 8:16, :] = 0.25 * mid[16:24]
        hg[side, 16:24, :] = 0.25 * jnp.broadcast_to(low[16:17], (8, 128))
        hi[side, 0:8, :] = zero8
        hi[side, 8:24, :] = mid[32:48]
        hi[side, 24:32, :] = jnp.broadcast_to(low[32:33], (8, 128))
    act, slope = gelu_parts(row_r[1, 0:128, :].astype(F32))
    act_row(17, act, 0.0, 0.0)
    slope_f[17, 0:128, :] = slope * keep

    def sides(t):
        scale = keep if t == 17 else 1.0
        for side, place in enumerate((152, 128)):
            slope_f[t, place : place + 8, :] = scale * jnp.broadcast_to(hs[side, t + 7 : t + 8, :], (8, 128))

    def pooled(i):
        left = jnp.broadcast_to(hg[0, i + 7 : i + 8, :], (16, 128))
        right = jnp.broadcast_to(hg[1, i + 7 : i + 8, :], (16, 128))
        tile = jnp.where(sub == 0, right, jnp.where(sub == 15, left, 0.0))
        pext[i, 64:80, :] = tile.astype(BF16)

    below = jnp.logical_and(
        lax.broadcasted_iota(jnp.int32, (32, 128), 0) >= 8, lax.broadcasted_iota(jnp.int32, (32, 128), 0) < 25
    )
    act3[2304:2432, :] = jnp.zeros((128, 384), BF16)
    act3[2304:2336, 0:128] = jnp.where(below, hc[0], 0.0).astype(BF16)
    act3[2336:2368, 256:384] = jnp.where(below, hc[1], 0.0).astype(BF16)
    lhs = jnp.concatenate(
        [jnp.concatenate([gpt[:, (19 - a) * 128 : (20 - a) * 128] for a in range(3)], 0), gpt_side[...]], 1
    )
    terms = both[...] + dot(lhs, act3[2176:2432, :])
    for a in range(1, 3):
        for b in range(3):
            block = terms[128 * a : 128 * a + 128, 128 * b : 128 * b + 128]
            acc[0, (3 * a + b - 3) * 128 : (3 * a + b - 2) * 128, :] = block.T
    both[0:128, :] = terms[0:128]
    acc[0, 768:1024, :] = jnp.zeros((256, 128), F32)
    p1_start(0)

    for t in range(1, 18):
        sides(t)
    pext[9, 0:64, :] = (0.25 * row_r[1, 128:192, :].astype(F32)).astype(BF16)
    for i in range(1, 10):
        pooled(i)
    tiles = [pext[i, 64:80, :] for i in range(1, 9)]
    lhs = jnp.concatenate(
        [
            jnp.concatenate([tiles[(t + 2) // 2 - 1], tiles[(t + 1) // 2 - 1], tiles[t // 2 - 1]], 1)
            for t in range(2, 16)
        ],
        0,
    )
    terms = dot(lhs, wa[0])
    for t in range(2, 16):
        part = terms[16 * (t - 2) : 16 * (t - 1)]
        t0, t1, t2 = part[:, 0:128], part[:, 128:256], part[:, 256:384]
        low = (ga_f[t, 0:1, :] + t2[15:16]) * slope_f[t, 0:1, :]
        high = (ga_f[t, 127:128, :] + t0[0:1]) * slope_f[t, 127:128, :]
        g_edge[t + 7 : t + 8, :] = low
        g_edge[t + 39 : t + 40, :] = high
        wide[t, 0:1, :] = t2[15:16]
        wide[t, 1:2, :] = t0[0:1]
        wide[t, 2:3, :] = (t0 + t1)[0:1]
        wide[t, 3:4, :] = (t1 + t2)[15:16]
    grad_rows(8, wa[0])

    @pl.when(is_pole)
    def _():
        dst = row_r.at[0, pl.ds(0, 192)]
        pltpu.make_async_copy(dst, dst, halo_recv.at[6]).wait()
        row_r[0, 192:256, :] = jnp.zeros((64, 128), BF16)

    @pl.when(jnp.logical_not(is_pole))
    def _():
        arrived(6)

    arrived(0)
    arrived(3)
    for side in range(2):
        top = e_r[3 * side].astype(F32)

        def pick(first, last):
            return jnp.broadcast_to(jnp.where(is_pole, top[first : first + 1], top[last : last + 1]), (8, 128))

        act, slope = gelu_parts(pick(0, 15))
        hc[side, 0:8, :] = act
        hs[side, 0:8, :] = slope
        hg[side, 0:8, :] = 0.25 * pick(16, 23)
        hi[side, 0:8, :] = jnp.where(is_pole, 0.0, pick(32, 47))
    act, slope = gelu_parts(row_r[0, 0:128, :].astype(F32))
    slope_f[0, 0:128, :] = slope
    sides(0)
    pext[0, 0:64, :] = (0.25 * row_r[0, 128:192, :].astype(F32)).astype(BF16)
    pooled(0)
    grad_rows(0, wa[1])

    cells, left, right = (
        jnp.where(is_pole, own, above)
        for own, above in (
            (act3[128:256, 128:256].astype(F32), act),
            (hc[0, 8:9, :], hc[0, 7:8, :]),
            (hc[1, 8:9, :], hc[1, 7:8, :]),
        )
    )
    act_row(0, cells, jnp.broadcast_to(left, (128, 128)), jnp.broadcast_to(right, (128, 128)))
    top_go = lax.dot_general(
        row_r[0, 128:192, :], copies, (((0,), (0,)), ((), ())), preferred_element_type=F32
    ).astype(BF16)
    gpt_top[...] = jnp.where(is_pole, top_go.astype(F32), gpt[:, 256:384].astype(F32)).astype(BF16)

    first_row = both[0:128, :] + dot(gpt_top[...], act3[0:128, :])
    for b in range(3):
        acc[1, b * 128 : (b + 1) * 128, :] = first_row[:, 128 * b : 128 * b + 128].T

    edges = [jnp.concatenate([hi[side], jnp.zeros((96, 128), F32)], 0).T[0:64] for side in range(2)]
    for t in (0, 1, 2, 15, 16, 17):
        x = (in_v[t - 1] if 0 < t < 17 else row_r[t // 17, 192:256, :]).astype(F32)
        in_row(t, x, pltpu.roll(edges[0], 121 - t, 1), pltpu.roll(edges[1], 120 - t, 1))
    beside = [
        jnp.where(lane < 32, edges[0], in_edge[0]),
        in_edge[1],
        jnp.where(lane < 32, in_edge[2], pltpu.roll(edges[1], 32, 1)),
    ]
    beside = jnp.concatenate(
        [(pltpu.roll(x, (1 - a) % 128, 1) if a != 1 else x).astype(BF16) for a in range(3) for x in beside], 0
    )
    here = jnp.concatenate([in3[:, 0:128], in3[:, 128:256], in3[:, 256:384]], 0)
    fold = jnp.where(is_pole, in3[:, 128:256].astype(F32), 0.0).astype(BF16)
    there = jnp.concatenate([fold, jnp.zeros((384, 128), BF16)], 0)
    last = jnp.concatenate([in3[:, 15 * 128 : 16 * 128], in3[:, 16 * 128 : 17 * 128], in3[:, 17 * 128 : 18 * 128]], 0)
    rhs = [g_v[1, 0:128, :], g_v[0, 0:128, :], g_v[16, 0:128, :], g_edge[...].astype(BF16)]
    acc[1, 384:960, :] += dot(jnp.concatenate([here, there, last, beside], 1), jnp.concatenate(rhs, 0))

    p1_start(1)
    p2_start(0)

    for t in range(2, 16):
        for i, (first, at_row) in enumerate(((0, 0), (112, 15), (128, 0), (144, 15))):
            more = jnp.where(sub == at_row, jnp.broadcast_to(wide[t, i : i + 1, :], (16, 128)), 0.0)
            cells = slice(first, first + 16)
            g_v[t, cells, :] = ((ga_f[t, cells, :] + more) * slope_f[t, cells, :]).astype(BF16)

    def input_row(r):
        lhs = jnp.concatenate([g_v[r + 2], g_v[r + 1], g_v[r]], 1)
        terms = dot(lhs, wb[jnp.where(r == 0, 1, 0)])
        t01, t2 = terms[:, 0:128], terms[:, 128:192]
        first = lax.broadcasted_iota(jnp.int32, (128, 128), 1) < 64
        t01 = jnp.where(first, pltpu.roll(t01, WIDE - 1, 0)[0:128], t01[0:128]).T
        t2 = pltpu.roll(t2, 1, 0)[0:128].T
        gi_o[r] = (t01[0:64] + t01[64:128] + t2).astype(BF16)

    p2_start(1)

    @pl.loop(0, ROWS // 2, unroll=4)
    def _(r):
        input_row(r)

    z_start(0)
    z_start(1)

    @pl.loop(ROWS // 2, ROWS, unroll=4)
    def _(r):
        input_row(r)

    p4_start(0)
    p4_start(1)
    p5_start(0)

    @pl.when(is_pole)
    def _():
        turned.wait_send()

    @pl.when(jnp.logical_not(is_pole))
    def _():
        above.wait_send()

    for copy in always:
        copy.wait_send()

    @pl.when(jnp.logical_not(is_last))
    def _():
        for copy in down:
            copy.wait_send()

    drain(0)
    p5_finish(0)
    p5_start(1)
    drain(1)
    p5_finish(1)
    p5_copy(0).wait_send()
    p5_copy(1).wait_send()


def write_out(gi_v, gw_v, gi_o, gw1_o, gw2_o, sem):
    copies = [
        pltpu.make_async_copy(gw_v.at[pl.ds(0, 768)], gw2_o.at[pl.ds(384, 768)], sem.at[0]),
        pltpu.make_async_copy(gw_v.at[pl.ds(1024, 384)], gw2_o.at[pl.ds(0, 384)], sem.at[1]),
        pltpu.make_async_copy(gw_v.at[pl.ds(1408, 576)], gw1_o, sem.at[2]),
        pltpu.make_async_copy(gi_v, gi_o, sem.at[3]),
    ]
    for copy in copies:
        copy.start()
    for copy in copies:
        copy.wait()


def section(nlat, nlon, inputs, pre_first, grad_out, w_first, w_second):
    nq, nz = nlat * 2, nlon // 4
    chunk = HALF // nq
    hbm = pl.BlockSpec(memory_space=pltpu.HBM)
    vmem = pltpu.VMEM
    dma = pltpu.SemaphoreType.DMA
    gi, gw = pl.pallas_call(
        functools.partial(kernel, nlat, nlon),
        out_shape=(vmem((ROWS, C0, COLS), BF16), vmem((2048, 128), F32)),
        in_specs=[hbm] * 5,
        out_specs=(pl.BlockSpec(memory_space=vmem), pl.BlockSpec(memory_space=vmem)),
        scratch_shapes=[
            vmem((ROWS, COLS, C1), BF16),
            vmem((ROWS, C0, COLS), BF16),
            vmem((ROWS // 2, COLS // 2, C1), BF16),
            vmem((9, C0, C1), BF16),
            vmem((9, C1, C1), BF16),
            vmem((2, 384, 384), BF16),
            vmem((2, 384, 192), BF16),
            vmem((2, 48, 128), BF16),
            vmem((2, 256, 128), BF16),
            vmem((6, 48, 128), BF16),
            vmem((2, 256, 128), BF16),
            vmem((2, 32, 128), F32),
            vmem((2, 32, 128), F32),
            vmem((2, 24, 128), F32),
            vmem((2, 32, 128), F32),
            vmem((18, WIDE, 128), F32),
            vmem((19 * 128, 384), BF16),
            vmem((10, PWIDE, 128), BF16),
            vmem((128, 20 * 128), BF16),
            vmem((128, 128), BF16),
            vmem((384, 128), BF16),
            vmem((192, 18 * 128), BF16),
            vmem((3, C0, 128), F32),
            vmem((128, 128), F32),
            vmem((18, 8, 128), F32),
            vmem((18, WIDE, 128), BF16),
            vmem((18, WIDE, 128), F32),
            vmem((384, 384), F32),
            vmem((2, 2 * HALF, 128), F32),
            vmem((2, HALF, 128), BF16),
            vmem((2, HALF, 128), BF16),
            vmem((2, HALF, 128), BF16),
            vmem((2, nq, chunk, 128), BF16),
            vmem((2, nz, chunk, 128), BF16),
            vmem((2, 2, HALF, 128), BF16),
            dma((5,)),
            dma((8,)), dma((8,)),
            dma((2,)), dma((2,)),
            dma((2,)), dma((2,)),
            dma((2,)), dma((2,)),
            dma((2,)), dma((2,)),
            dma((2,)), dma((2,)),
        ],
        compiler_params=pltpu.CompilerParams(
            collective_id=0, has_side_effects=True, vmem_limit_bytes=40 * 1024 * 1024
        ),
        cost_estimate=pl.CostEstimate(flops=1_800_000_000, bytes_accessed=3_000_000, transcendentals=600_000),
    )(
        *(
            pltpu.with_memory_space_constraint(x, pltpu.HBM)
            for x in (
                pre_first,
                jnp.transpose(inputs, (0, 2, 1)),
                grad_out,
                w_first.reshape(9, C0, C1),
                w_second.reshape(9, C1, C1),
            )
        )
    )
    gi, grad_w_first, grad_w_second = pl.pallas_call(
        write_out,
        out_shape=(
            jax.ShapeDtypeStruct((ROWS, C0, COLS), BF16),
            jax.ShapeDtypeStruct((9 * C0, C1), F32),
            jax.ShapeDtypeStruct((9 * C1, C1), F32),
        ),
        in_specs=[pl.BlockSpec(memory_space=vmem)] * 2,
        out_specs=(pl.BlockSpec(memory_space=pl.ANY),) * 3,
        scratch_shapes=[dma((4,))],
        compiler_params=pltpu.CompilerParams(vmem_limit_bytes=16 * 1024 * 1024),
    )(gi, gw)
    return (
        jnp.transpose(gi, (0, 2, 1)),
        grad_w_first.reshape(3, 3, C0, C1),
        grad_w_second.reshape(3, 3, C1, C1),
    )


def solution(mesh):
    nlat, nlon = mesh.shape["lat"], mesh.shape["lon"]
    in_specs = (P("lat", "lon", None), P("lat", "lon", None), P("lat", "lon", None), P(), P())
    out_specs = (P("lat", "lon", None), P(), P())
    return jax.shard_map(
        functools.partial(section, nlat, nlon), mesh=mesh, in_specs=in_specs, out_specs=out_specs, check_vma=False
    )
```

```python
import functools

import jax
import jax.numpy as jnp
from jax import lax
from jax.experimental import pallas as pl
from jax.experimental.pallas import tpu as pltpu
from jax.sharding import PartitionSpec as P

INV_ROOT = 0.7071067811865476
DENSITY = 0.3989422804014327
BF16 = jnp.bfloat16
F32 = jnp.float32
MESH = pl.DeviceIdType.MESH

ROWS, COLS, C0, C1 = 16, 128, 64, 128
WIDE = COLS + 32
PWIDE = COLS // 2 + 16
HALF = 512


def far_first(n):
    return sorted(range(1, n), key=lambda k: (-min(k, n - k), k))


def gelu_parts(value):
    cdf = 0.5 * (1.0 + lax.erf(value * INV_ROOT))
    act = value * cdf
    slope = cdf + value * jnp.exp(-0.5 * value * value) * DENSITY
    return act, slope


def dot(a, b):
    return lax.dot_general(a, b, (((1,), (0,)), ((), ())), preferred_element_type=F32)


def kernel(
    nlat, nlon,
    pre_h, in_h, go_h, w1_h, w2_h,
    gi_o, gw_o,
    pre_v, in_v, go_v, w1_v, w2_v, wa, wb,
    e_s, row_s, e_r, row_r, hc, hs, hg, hi,
    slope_f, act3, pext, gpt, gpt_top, gpt_side, in3, in_edge, g_edge, wide, g_v, ga_f, both,
    acc, p1s, p1r, p2s, p2r, zb, res,
    load_sem, halo_send, halo_recv, p1_send, p1_recv, p2_send, p2_recv,
    z_send, z_recv, p4_send, p4_recv, p5_send, p5_recv,
):
    lat, lon = lax.axis_index("lat"), lax.axis_index("lon")
    nq, nz = nlat * 2, nlon // 4
    chunk = HALF // nq
    z, yhi, core = lon // 4, (lon % 4) // 2, lon % 2
    q = lat * 2 + yhi
    is_pole = lat == 0
    is_last = lat == nlat - 1
    half = nlon // 2

    def chip(p, k):
        return (p // 2, z * 4 + (p % 2) * 2 + k)

    def at(dlat, dlon):
        return (dlat, lax.rem(dlon + 2 * nlon, nlon))

    loads = [
        pltpu.make_async_copy(src, dst, load_sem.at[i])
        for i, (src, dst) in enumerate(
            ((pre_h, pre_v), (in_h, in_v), (go_h, go_v), (w2_h, w2_v), (w1_h, w1_v))
        )
    ]
    for load in loads:
        load.start()

    barrier = pltpu.get_barrier_semaphore()

    def greet(device):
        pl.semaphore_signal(barrier, inc=1, device_id=device, device_id_type=MESH)

    top_lat = jnp.where(is_pole, 0, lat - 1)
    top_lon = jnp.where(is_pole, lon + half, lon)
    for d in (-1, 0, 1):
        greet(at(top_lat, top_lon + d))
    for k in far_first(nz)[:1]:
        greet((lat, lax.rem(lon + 4 * k, nlon)))
    for k in far_first(nq)[:3]:
        greet(chip(lax.rem(q + k, nq), core))
    for d in (-1, 1):
        greet(at(lat, lon + d))

    @pl.when(jnp.logical_not(is_last))
    def _():
        for d in (-1, 1, 0):
            greet(at(lat + 1, lon + d))

    for k in far_first(nz)[1:]:
        greet((lat, lax.rem(lon + 4 * k, nlon)))
    for k in far_first(nq)[3:]:
        greet(chip(lax.rem(q + k, nq), core))
    greet(chip(q, 1 - core))

    loads[0].wait()
    loads[1].wait()
    loads[2].wait()
    lane = lax.broadcasted_iota(jnp.int32, (C0, 128), 1)
    sub = lax.broadcasted_iota(jnp.int32, (16, 128), 0)
    zero16 = jnp.zeros((16, 128), F32)
    for side, (col, first) in enumerate(((0, 0), (15, 112))):
        edge = zero16
        for r in range(ROWS):
            tile = pre_v[r, first : first + 16, :].astype(F32)
            edge = jnp.where(sub == r, jnp.broadcast_to(tile[col : col + 1], (16, 128)), edge)
        e_s[side, 0:16, :] = edge.astype(BF16)
        edge = zero16
        for r in range(ROWS // 2):
            tile = go_v[r, first // 112 * 48 : first // 112 * 48 + 16, :].astype(F32)
            edge = jnp.where(sub == r, jnp.broadcast_to(tile[col : col + 1], (16, 128)), edge)
        e_s[side, 16:32, :] = edge.astype(BF16)
        edge = jnp.zeros((C0, 128), F32)
        for r in range(ROWS):
            shift = r if side == 0 else r + 1
            edge = jnp.where(lane == r, pltpu.roll(in_v[r].astype(F32), shift, 1), edge)
        e_s[side, 32:48, 0:64] = edge.T[0:16].astype(BF16)
        e_s[side, 32:48, 64:128] = jnp.zeros((16, 64), BF16)
    for end, r in enumerate((0, ROWS - 1)):
        row_s[end, 0:128, :] = pre_v[r]
        row_s[end, 128:192, :] = go_v[r // 2]
        row_s[end, 192:256, :] = in_v[r]

    pl.semaphore_wait(barrier, jnp.where(is_last, 0, 3) + 2 + 3 + 1 + (nq - 1) + (nz - 1))

    up = jnp.where(is_pole, 0, 2)

    def edge_copy(number, side, slot, device):
        return pltpu.make_async_remote_copy(
            src_ref=e_s.at[side], dst_ref=e_r.at[slot], send_sem=halo_send.at[number],
            recv_sem=halo_recv.at[slot], device_id=device, device_id_type=MESH,
        )

    def row_copy(number, end, slot, device, size=256):
        return pltpu.make_async_remote_copy(
            src_ref=row_s.at[end, pl.ds(0, size)], dst_ref=row_r.at[slot, pl.ds(0, size)], send_sem=halo_send.at[number],
            recv_sem=halo_recv.at[6 + slot], device_id=device, device_id_type=MESH,
        )

    turned = row_copy(0, 0, 0, at(0, lon + half), 192)
    above = row_copy(0, 0, 1, at(lat - 1, lon))
    always = [
        edge_copy(3, 1, up, at(top_lat, top_lon + 1)),
        edge_copy(4, 0, up + 3, at(top_lat, top_lon - 1)),
        edge_copy(1, 1, 1, at(lat, lon + 1)),
        edge_copy(2, 0, 4, at(lat, lon - 1)),
    ]
    down = [
        row_copy(5, 1, 0, at(lat + 1, lon)),
        edge_copy(6, 1, 0, at(lat + 1, lon + 1)),
        edge_copy(7, 0, 3, at(lat + 1, lon - 1)),
    ]
    for copy in always[:2]:
        copy.start()

    @pl.when(is_pole)
    def _():
        turned.start()

    @pl.when(jnp.logical_not(is_pole))
    def _():
        above.start()

    for copy in always[2:]:
        copy.start()

    @pl.when(jnp.logical_not(is_last))
    def _():
        for copy in down:
            copy.start()

    @pl.when(is_last)
    def _():
        e_r[2] = jnp.zeros((48, 128), BF16)
        e_r[5] = jnp.zeros((48, 128), BF16)
        row_r[1] = jnp.zeros((256, 128), BF16)

    loads[3].wait()
    loads[4].wait()
    for a in range(3):
        for b in range(3):
            t = w2_v[3 * a + b].astype(F32).T.astype(BF16)
            wa[0, 128 * a : 128 * a + 128, 128 * b : 128 * b + 128] = t
            u = w1_v[3 * a + b].astype(F32).T.astype(BF16)
            wb[0, 128 * a : 128 * a + 128, 64 * b : 64 * b + 64] = u
    wa[1] = wa[0]
    wb[1] = wb[0]

    @pl.when(is_pole)
    def _():
        wa[1, 256:384, :] = wa[0, 0:128, :]
        wb[1, 256:384, :] = wb[0, 0:128, :]

    def p1_copy(s):
        return pltpu.make_async_remote_copy(
            src_ref=p1s.at[s], dst_ref=p1r.at[s], send_sem=p1_send.at[s], recv_sem=p1_recv.at[s],
            device_id=chip(q, 1 - core), device_id_type=MESH,
        )

    def p1_start(s):
        p1s[s] = acc[s, pl.ds(pl.multiple_of((1 - core) * HALF, HALF), HALF), :].astype(BF16)
        p1_copy(s).start()

    def chunk_rows(p):
        return pl.ds(pl.multiple_of(p * chunk, 32), chunk)

    def p2_copy(s, p):
        return pltpu.make_async_remote_copy(
            src_ref=p2s.at[s, chunk_rows(p)], dst_ref=p2r.at[s, q], send_sem=p2_send.at[s],
            recv_sem=p2_recv.at[s], device_id=chip(p, core), device_id_type=MESH,
        )

    def p2_start(s):
        p1_copy(s).wait()
        own = pl.ds(pl.multiple_of(core * HALF, HALF), HALF)
        total = acc[s, own, :] + p1r[s].astype(F32)
        acc[s, own, :] = total
        p2s[s] = total.astype(BF16)
        for k in far_first(nq):
            p2_copy(s, lax.rem(q + k, nq)).start()

    def z_copy(s, k):
        return pltpu.make_async_remote_copy(
            src_ref=zb.at[s, z], dst_ref=zb.at[s, z], send_sem=z_send.at[s], recv_sem=z_recv.at[s],
            device_id=(lat, lax.rem(lon + 4 * k, nlon)), device_id_type=MESH,
        )

    def all_of(ref, sem):
        pltpu.make_async_copy(ref, ref, sem).wait()

    def z_start(s):
        total = acc[s, pl.ds(pl.multiple_of(core * HALF + q * chunk, 32), chunk), :]
        all_of(p2r.at[s, pl.ds(0, nq - 1)], p2_recv.at[s])
        for k in range(1, nq):
            total = total + p2r[s, lax.rem(q + nq - k, nq)].astype(F32)
        zb[s, z] = total.astype(BF16)
        for k in far_first(nz):
            z_copy(s, k).start()

    def p4_copy(s, p):
        mine = res.at[s, core, chunk_rows(q)]
        return pltpu.make_async_remote_copy(
            src_ref=mine, dst_ref=mine, send_sem=p4_send.at[s], recv_sem=p4_recv.at[s],
            device_id=chip(p, core), device_id_type=MESH,
        )

    def p4_start(s):
        all_of(zb.at[s, pl.ds(0, nz - 1)], z_recv.at[s])
        total = zb[s, 0].astype(F32)
        for k in range(1, nz):
            total = total + zb[s, k].astype(F32)
        res[s, core, chunk_rows(q), :] = total.astype(BF16)
        for k in far_first(nq):
            p4_copy(s, lax.rem(q + k, nq)).start()

    def p5_copy(s):
        rows = res.at[s, core]
        return pltpu.make_async_remote_copy(
            src_ref=rows, dst_ref=rows, send_sem=p5_send.at[s], recv_sem=p5_recv.at[s],
            device_id=chip(q, 1 - core), device_id_type=MESH,
        )

    def deliver(s, k):
        rows = pl.ds(pl.multiple_of(s * 2 * HALF + k * HALF, HALF), HALF)
        gw_o[rows, :] = res[s, k].astype(F32)

    def p5_start(s):
        all_of(res.at[s, core, pl.ds(0, HALF - chunk)], p4_recv.at[s])
        p5_copy(s).start()
        deliver(s, core)

    def p5_finish(s):
        p5_copy(s).wait_recv()
        deliver(s, 1 - core)

    def drain(s):
        all_of(p2s.at[s, pl.ds(0, HALF - chunk)], p2_send.at[s])
        all_of(zb.at[s, pl.ds(0, nz - 1)], z_send.at[s])
        all_of(res.at[s, core, pl.ds(0, HALF - chunk)], p4_send.at[s])

    column = lax.broadcasted_iota(jnp.int32, (128, 128), 0)

    def act_row(t, x, left, right):
        rows = pl.ds(pl.multiple_of(t * 128, 128), 128)
        act3[rows, 0:128] = jnp.where(column == 0, left, pltpu.roll(x, 1, 0)).astype(BF16)
        act3[rows, 128:256] = x.astype(BF16)
        act3[rows, 256:384] = jnp.where(column == 127, right, pltpu.roll(x, 127, 0)).astype(BF16)

    @pl.loop(0, ROWS, unroll=4)
    def _(r):
        act, slope = gelu_parts(pre_v[r].astype(F32))
        act_row(r + 1, act, 0.0, 0.0)
        slope_f[r + 1, 0:128, :] = slope

    copies = lax.broadcasted_iota(jnp.int32, (64, 128), 1) // 2
    copies = jnp.where(copies == lax.broadcasted_iota(jnp.int32, (64, 128), 0), 0.25, 0.0).astype(BF16)
    gpt[:, 0:256] = jnp.zeros((128, 256), BF16)
    gpt[:, 18 * 128 : 20 * 128] = jnp.zeros((128, 256), BF16)
    for i in range(ROWS // 2):
        t = lax.dot_general(
            go_v[i], copies, (((0,), (0,)), ((), ())), preferred_element_type=F32
        ).astype(BF16)
        gpt[:, (2 * i + 2) * 128 : (2 * i + 3) * 128] = t
        gpt[:, (2 * i + 3) * 128 : (2 * i + 4) * 128] = t

    corner = jnp.concatenate([e_s[0, 16:32, :], e_s[1, 16:32, :]], 0)
    place = lax.broadcasted_iota(jnp.int32, (32, 128), 1)
    source = lax.broadcasted_iota(jnp.int32, (32, 128), 0)
    for a in range(3):
        row = place % 32 - 7 - a
        chosen = jnp.logical_and(
            jnp.logical_and(row >= 0, row < ROWS), place // 32 * 16 + (row + 16) // 2 - 8 == source
        )
        chosen = jnp.where(chosen, 0.25, 0.0).astype(BF16)
        gpt_side[128 * a : 128 * a + 128, :] = lax.dot_general(
            corner, chosen, (((0,), (0,)), ((), ())), preferred_element_type=F32
        ).astype(BF16)

    lhs = jnp.concatenate([gpt[:, (3 - a) * 128 : (3 - a) * 128 + 2048] for a in range(3)], 0)
    both[...] = dot(lhs, act3[128 : 17 * 128, :])

    def grad_rows(i, taps):
        here, after = pext[i], pext[i + 1]
        lhs = jnp.concatenate(
            [jnp.concatenate([after, here, here], 1), jnp.concatenate([after, after, here], 1)], 0
        )
        terms = dot(lhs, taps)
        for s in range(2):
            part = terms[PWIDE * s : PWIDE * (s + 1)]
            t0, t1, t2 = part[:, 0:128], part[:, 128:256], part[:, 256:384]
            ga_f[2 * i + s, pl.ds(0, PWIDE, stride=2), :] = t0 + t1 + pltpu.roll(t2, 1, 0)
            ga_f[2 * i + s, pl.ds(1, PWIDE, stride=2), :] = pltpu.roll(t0, PWIDE - 1, 0) + t1 + t2
            g_v[2 * i + s] = (ga_f[2 * i + s] * slope_f[2 * i + s]).astype(BF16)

    for i in range(1, 9):
        pext[i, 0:64, :] = (0.25 * go_v[i - 1].astype(F32)).astype(BF16)
        pext[i, 64:80, :] = jnp.zeros((16, 128), BF16)

    @pl.loop(1, 8, unroll=7)
    def _(i):
        grad_rows(i, wa[0])

    def in_row(t, x, left, right):
        cells = slice(128 * t, 128 * t + 128)
        in3[0:64, cells] = jnp.where(lane == 0, left, pltpu.roll(x, 1, 1)).astype(BF16)
        in3[64:128, cells] = x.astype(BF16)
        in3[128:192, cells] = jnp.where(lane == 127, right, pltpu.roll(x, 127, 1)).astype(BF16)

    for t in range(1, 17):
        in_row(t, in_v[t - 1].astype(F32), 0.0, 0.0)

    inner = jnp.where(jnp.logical_and(column > 0, column < 127), 1.0, 0.0)
    lhs = jnp.concatenate([in3[:, (a + 1) * 128 : (a + 15) * 128] for a in range(3)], 0)
    rhs = [(g_v[t, 0:128, :].astype(F32) * inner).astype(BF16) for t in range(2, 16)]
    acc[1, 384:960, :] = dot(lhs, jnp.concatenate(rhs, 0))
    acc[1, 960:1024, :] = jnp.zeros((64, 128), F32)

    g_edge[...] = jnp.zeros((128, 128), F32)
    for b, (low, high) in enumerate(((None, 126), (0, 127), (1, None))):
        edge = jnp.zeros((C0, 128), F32)
        for r in range(ROWS):
            x = in_v[r].astype(F32)
            if low is not None:
                edge = jnp.where(lane == 8 + r, pltpu.roll(x, 8 + r - low, 1), edge)
            if high is not None:
                edge = jnp.where(lane == 40 + r, pltpu.roll(x, (40 + r - high) % 128, 1), edge)
        in_edge[b] = edge

    def arrived(slot):
        dst = e_r.at[slot] if slot < 6 else row_r.at[slot - 6]
        pltpu.make_async_copy(dst, dst, halo_recv.at[slot]).wait()

    for slot in (1, 4):
        arrived(slot)

    @pl.when(jnp.logical_not(is_last))
    def _():
        for slot in (2, 5, 7):
            arrived(slot)

    keep = jnp.where(is_last, 0.0, 1.0).astype(F32)
    zero8 = jnp.zeros((8, 128), F32)
    for side in range(2):
        mid = e_r[3 * side + 1].astype(F32)
        low = e_r[3 * side + 2].astype(F32)
        hc[side, 8:24, :] = mid[0:16]
        hc[side, 24:32, :] = jnp.broadcast_to(low[0:1], (8, 128))
        act, slope = gelu_parts(hc[side, 8:32, :])
        hc[side, 8:32, :] = act
        hs[side, 8:32, :] = slope
        hg[side, 8:16, :] = 0.25 * mid[16:24]
        hg[side, 16:24, :] = 0.25 * jnp.broadcast_to(low[16:17], (8, 128))
        hi[side, 0:8, :] = zero8
        hi[side, 8:24, :] = mid[32:48]
        hi[side, 24:32, :] = jnp.broadcast_to(low[32:33], (8, 128))
    act, slope = gelu_parts(row_r[1, 0:128, :].astype(F32))
    act_row(17, act, 0.0, 0.0)
    slope_f[17, 0:128, :] = slope * keep

    def sides(t):
        scale = keep if t == 17 else 1.0
        for side, place in enumerate((152, 128)):
            slope_f[t, place : place + 8, :] = scale * jnp.broadcast_to(hs[side, t + 7 : t + 8, :], (8, 128))

    def pooled(i):
        left = jnp.broadcast_to(hg[0, i + 7 : i + 8, :], (16, 128))
        right = jnp.broadcast_to(hg[1, i + 7 : i + 8, :], (16, 128))
        tile = jnp.where(sub == 0, right, jnp.where(sub == 15, left, 0.0))
        pext[i, 64:80, :] = tile.astype(BF16)

    below = jnp.logical_and(
        lax.broadcasted_iota(jnp.int32, (32, 128), 0) >= 8, lax.broadcasted_iota(jnp.int32, (32, 128), 0) < 25
    )
    act3[2304:2432, :] = jnp.zeros((128, 384), BF16)
    act3[2304:2336, 0:128] = jnp.where(below, hc[0], 0.0).astype(BF16)
    act3[2336:2368, 256:384] = jnp.where(below, hc[1], 0.0).astype(BF16)
    lhs = jnp.concatenate(
        [jnp.concatenate([gpt[:, (19 - a) * 128 : (20 - a) * 128] for a in range(3)], 0), gpt_side[...]], 1
    )
    terms = both[...] + dot(lhs, act3[2176:2432, :])
    for a in range(1, 3):
        for b in range(3):
            block = terms[128 * a : 128 * a + 128, 128 * b : 128 * b + 128]
            acc[0, (3 * a + b - 3) * 128 : (3 * a + b - 2) * 128, :] = block.T
    both[0:128, :] = terms[0:128]
    acc[0, 768:1024, :] = jnp.zeros((256, 128), F32)
    p1_start(0)

    for t in range(1, 18):
        sides(t)
    pext[9, 0:64, :] = (0.25 * row_r[1, 128:192, :].astype(F32)).astype(BF16)
    for i in range(1, 10):
        pooled(i)
    tiles = [pext[i, 64:80, :] for i in range(1, 9)]
    lhs = jnp.concatenate(
        [
            jnp.concatenate([tiles[(t + 2) // 2 - 1], tiles[(t + 1) // 2 - 1], tiles[t // 2 - 1]], 1)
            for t in range(2, 16)
        ],
        0,
    )
    terms = dot(lhs, wa[0])
    for t in range(2, 16):
        part = terms[16 * (t - 2) : 16 * (t - 1)]
        t0, t1, t2 = part[:, 0:128], part[:, 128:256], part[:, 256:384]
        low = (ga_f[t, 0:1, :] + t2[15:16]) * slope_f[t, 0:1, :]
        high = (ga_f[t, 127:128, :] + t0[0:1]) * slope_f[t, 127:128, :]
        g_edge[t + 7 : t + 8, :] = low
        g_edge[t + 39 : t + 40, :] = high
        wide[t, 0:1, :] = t2[15:16]
        wide[t, 1:2, :] = t0[0:1]
        wide[t, 2:3, :] = (t0 + t1)[0:1]
        wide[t, 3:4, :] = (t1 + t2)[15:16]
    grad_rows(8, wa[0])

    @pl.when(is_pole)
    def _():
        dst = row_r.at[0, pl.ds(0, 192)]
        pltpu.make_async_copy(dst, dst, halo_recv.at[6]).wait()
        row_r[0, 192:256, :] = jnp.zeros((64, 128), BF16)

    @pl.when(jnp.logical_not(is_pole))
    def _():
        arrived(6)

    arrived(0)
    arrived(3)
    for side in range(2):
        top = e_r[3 * side].astype(F32)

        def pick(first, last):
            return jnp.broadcast_to(jnp.where(is_pole, top[first : first + 1], top[last : last + 1]), (8, 128))

        act, slope = gelu_parts(pick(0, 15))
        hc[side, 0:8, :] = act
        hs[side, 0:8, :] = slope
        hg[side, 0:8, :] = 0.25 * pick(16, 23)
        hi[side, 0:8, :] = jnp.where(is_pole, 0.0, pick(32, 47))
    act, slope = gelu_parts(row_r[0, 0:128, :].astype(F32))
    slope_f[0, 0:128, :] = slope
    sides(0)
    pext[0, 0:64, :] = (0.25 * row_r[0, 128:192, :].astype(F32)).astype(BF16)
    pooled(0)
    grad_rows(0, wa[1])

    cells, left, right = (
        jnp.where(is_pole, own, above)
        for own, above in (
            (act3[128:256, 128:256].astype(F32), act),
            (hc[0, 8:9, :], hc[0, 7:8, :]),
            (hc[1, 8:9, :], hc[1, 7:8, :]),
        )
    )
    act_row(0, cells, jnp.broadcast_to(left, (128, 128)), jnp.broadcast_to(right, (128, 128)))
    top_go = lax.dot_general(
        row_r[0, 128:192, :], copies, (((0,), (0,)), ((), ())), preferred_element_type=F32
    ).astype(BF16)
    gpt_top[...] = jnp.where(is_pole, top_go.astype(F32), gpt[:, 256:384].astype(F32)).astype(BF16)

    first_row = both[0:128, :] + dot(gpt_top[...], act3[0:128, :])
    for b in range(3):
        acc[1, b * 128 : (b + 1) * 128, :] = first_row[:, 128 * b : 128 * b + 128].T

    edges = [jnp.concatenate([hi[side], jnp.zeros((96, 128), F32)], 0).T[0:64] for side in range(2)]
    for t in (0, 1, 2, 15, 16, 17):
        x = (in_v[t - 1] if 0 < t < 17 else row_r[t // 17, 192:256, :]).astype(F32)
        in_row(t, x, pltpu.roll(edges[0], 121 - t, 1), pltpu.roll(edges[1], 120 - t, 1))
    beside = [
        jnp.where(lane < 32, edges[0], in_edge[0]),
        in_edge[1],
        jnp.where(lane < 32, in_edge[2], pltpu.roll(edges[1], 32, 1)),
    ]
    beside = jnp.concatenate(
        [(pltpu.roll(x, (1 - a) % 128, 1) if a != 1 else x).astype(BF16) for a in range(3) for x in beside], 0
    )
    here = jnp.concatenate([in3[:, 0:128], in3[:, 128:256], in3[:, 256:384]], 0)
    fold = jnp.where(is_pole, in3[:, 128:256].astype(F32), 0.0).astype(BF16)
    there = jnp.concatenate([fold, jnp.zeros((384, 128), BF16)], 0)
    last = jnp.concatenate([in3[:, 15 * 128 : 16 * 128], in3[:, 16 * 128 : 17 * 128], in3[:, 17 * 128 : 18 * 128]], 0)
    rhs = [g_v[1, 0:128, :], g_v[0, 0:128, :], g_v[16, 0:128, :], g_edge[...].astype(BF16)]
    acc[1, 384:960, :] += dot(jnp.concatenate([here, there, last, beside], 1), jnp.concatenate(rhs, 0))

    p1_start(1)
    p2_start(0)

    for t in range(2, 16):
        for i, (first, at_row) in enumerate(((0, 0), (112, 15), (128, 0), (144, 15))):
            more = jnp.where(sub == at_row, jnp.broadcast_to(wide[t, i : i + 1, :], (16, 128)), 0.0)
            cells = slice(first, first + 16)
            g_v[t, cells, :] = ((ga_f[t, cells, :] + more) * slope_f[t, cells, :]).astype(BF16)

    def input_row(r):
        lhs = jnp.concatenate([g_v[r + 2], g_v[r + 1], g_v[r]], 1)
        terms = dot(lhs, wb[jnp.where(r == 0, 1, 0)])
        t01, t2 = terms[:, 0:128], terms[:, 128:192]
        first = lax.broadcasted_iota(jnp.int32, (128, 128), 1) < 64
        t01 = jnp.where(first, pltpu.roll(t01, WIDE - 1, 0)[0:128], t01[0:128]).T
        t2 = pltpu.roll(t2, 1, 0)[0:128].T
        gi_o[r] = (t01[0:64] + t01[64:128] + t2).astype(BF16)

    p2_start(1)

    @pl.loop(0, ROWS // 2, unroll=4)
    def _(r):
        input_row(r)

    z_start(0)
    z_start(1)

    @pl.loop(ROWS // 2, ROWS, unroll=4)
    def _(r):
        input_row(r)

    p4_start(0)
    p4_start(1)
    p5_start(0)

    @pl.when(is_pole)
    def _():
        turned.wait_send()

    @pl.when(jnp.logical_not(is_pole))
    def _():
        above.wait_send()

    for copy in always:
        copy.wait_send()

    @pl.when(jnp.logical_not(is_last))
    def _():
        for copy in down:
            copy.wait_send()

    drain(0)
    p5_finish(0)
    p5_start(1)
    drain(1)
    p5_finish(1)
    p5_copy(0).wait_send()
    p5_copy(1).wait_send()


def write_out(gi_v, gw_v, gi_o, gw1_o, gw2_o, sem):
    copies = [
        pltpu.make_async_copy(gw_v.at[pl.ds(0, 768)], gw2_o.at[pl.ds(384, 768)], sem.at[0]),
        pltpu.make_async_copy(gw_v.at[pl.ds(1024, 384)], gw2_o.at[pl.ds(0, 384)], sem.at[1]),
        pltpu.make_async_copy(gw_v.at[pl.ds(1408, 576)], gw1_o, sem.at[2]),
        pltpu.make_async_copy(gi_v, gi_o, sem.at[3]),
    ]
    for copy in copies:
        copy.start()
    for copy in copies:
        copy.wait()


def section(nlat, nlon, inputs, pre_first, grad_out, w_first, w_second):
    nq, nz = nlat * 2, nlon // 4
    chunk = HALF // nq
    hbm = pl.BlockSpec(memory_space=pltpu.HBM)
    vmem = pltpu.VMEM
    dma = pltpu.SemaphoreType.DMA
    gi, gw = pl.pallas_call(
        functools.partial(kernel, nlat, nlon),
        out_shape=(vmem((ROWS, C0, COLS), BF16), vmem((2048, 128), F32)),
        in_specs=[hbm] * 5,
        out_specs=(pl.BlockSpec(memory_space=vmem), pl.BlockSpec(memory_space=vmem)),
        scratch_shapes=[
            vmem((ROWS, COLS, C1), BF16),
            vmem((ROWS, C0, COLS), BF16),
            vmem((ROWS // 2, COLS // 2, C1), BF16),
            vmem((9, C0, C1), BF16),
            vmem((9, C1, C1), BF16),
            vmem((2, 384, 384), BF16),
            vmem((2, 384, 192), BF16),
            vmem((2, 48, 128), BF16),
            vmem((2, 256, 128), BF16),
            vmem((6, 48, 128), BF16),
            vmem((2, 256, 128), BF16),
            vmem((2, 32, 128), F32),
            vmem((2, 32, 128), F32),
            vmem((2, 24, 128), F32),
            vmem((2, 32, 128), F32),
            vmem((18, WIDE, 128), F32),
            vmem((19 * 128, 384), BF16),
            vmem((10, PWIDE, 128), BF16),
            vmem((128, 20 * 128), BF16),
            vmem((128, 128), BF16),
            vmem((384, 128), BF16),
            vmem((192, 18 * 128), BF16),
            vmem((3, C0, 128), F32),
            vmem((128, 128), F32),
            vmem((18, 8, 128), F32),
            vmem((18, WIDE, 128), BF16),
            vmem((19, WIDE, 128), F32),
            vmem((384, 384), F32),
            vmem((2, 2 * HALF, 128), F32),
            vmem((2, HALF, 128), BF16),
            vmem((2, HALF, 128), BF16),
            vmem((2, HALF, 128), BF16),
            vmem((2, nq, chunk, 128), BF16),
            vmem((2, nz, chunk, 128), BF16),
            vmem((2, 2, HALF, 128), BF16),
            dma((5,)),
            dma((8,)), dma((8,)),
            dma((2,)), dma((2,)),
            dma((2,)), dma((2,)),
            dma((2,)), dma((2,)),
            dma((2,)), dma((2,)),
            dma((2,)), dma((2,)),
        ],
        compiler_params=pltpu.CompilerParams(
            collective_id=0, has_side_effects=True, vmem_limit_bytes=40 * 1024 * 1024
        ),
        cost_estimate=pl.CostEstimate(flops=1_800_000_000, bytes_accessed=3_000_000, transcendentals=600_000),
    )(
        *(
            pltpu.with_memory_space_constraint(x, pltpu.HBM)
            for x in (
                pre_first,
                jnp.transpose(inputs, (0, 2, 1)),
                grad_out,
                w_first.reshape(9, C0, C1),
                w_second.reshape(9, C1, C1),
            )
        )
    )
    gi, grad_w_first, grad_w_second = pl.pallas_call(
        write_out,
        out_shape=(
            jax.ShapeDtypeStruct((ROWS, C0, COLS), BF16),
            jax.ShapeDtypeStruct((9 * C0, C1), F32),
            jax.ShapeDtypeStruct((9 * C1, C1), F32),
        ),
        in_specs=[pl.BlockSpec(memory_space=vmem)] * 2,
        out_specs=(pl.BlockSpec(memory_space=pl.ANY),) * 3,
        scratch_shapes=[dma((4,))],
        compiler_params=pltpu.CompilerParams(vmem_limit_bytes=16 * 1024 * 1024),
    )(gi, gw)
    return (
        jnp.transpose(gi, (0, 2, 1)),
        grad_w_first.reshape(3, 3, C0, C1),
        grad_w_second.reshape(3, 3, C1, C1),
    )


def solution(mesh):
    nlat, nlon = mesh.shape["lat"], mesh.shape["lon"]
    in_specs = (P("lat", "lon", None), P("lat", "lon", None), P("lat", "lon", None), P(), P())
    out_specs = (P("lat", "lon", None), P(), P())
    return jax.shard_map(
        functools.partial(section, nlat, nlon), mesh=mesh, in_specs=in_specs, out_specs=out_specs, check_vma=False
    )
```
